32 devices in a mesh: wide: 4 (over z), batch: 8 (over y, x, core).
Axes of the slice: x: 2, y: 2, z: 4, core: 2. Of those that a mesh axis runs over, the one named last changes fastest.
Arguments:
- series: bfloat16 [64, 1056, 64], P('batch', 'wide'), may hold values from -60 to 60
- lengths: int32 [64], P('batch'), may hold values from 792 to 1056, as said below
- freqs: int32 [5], replicated, may hold values from 2 to 528, as said below
- cotangent: bfloat16 [64, 1056, 64], P('batch', 'wide'), may hold values from -6 to 6
- kernels: float32 [2342912], P(('wide', 'batch')), may hold values from -0.25 to 0.25
- kernel_m: float32 [2342912], P(('wide', 'batch')), may hold values from -0.0004272461 to 0.0004272461
- kernel_v: float32 [2342912], P(('wide', 'batch')), may hold values from 2.1338632e-10 to 3.4141812e-09
- small: float32 [256], replicated, may hold values from -2 to 2
- small_m: float32 [256], replicated, may hold values from -0.0012207031 to 0.0012207031
- small_v: float32 [256], replicated, may hold values from 8.535453e-10 to 1.2803179e-08
Outputs:
- output: bfloat16 [64, 1056, 64], P('batch', 'wide')
- grad_series: bfloat16 [64, 1056, 64], P('batch', 'wide')
- grad_norm: float32 [], replicated
- new_kernels: float32 [2342912], P(('wide', 'batch'))
- new_kernel_m: float32 [2342912], P(('wide', 'batch'))
- new_kernel_v: float32 [2342912], P(('wide', 'batch'))
- new_small: float32 [256], replicated
- new_small_m: float32 [256], replicated
- new_small_v: float32 [256], replicated
The draws below stay inside these ranges and needn't reach their ends.
Inputs may be any that keep to these rules, and one draw needn't show every extreme that they name: `freqs`: 5 different divisors of 1056, among them 2 and 528. `lengths`: among the 8 series of each batch index one has length 1056 and one has length 792.
All inputs are finite; a program needn't handle non-finite values.
Results may differ from the reference program's by a relative error of at most 0.0037.
Values may be sent and summed in bfloat16 or wider, within the bound.
A program may use at most 320 MiB of HBM per device.

```python
import math
import jax
import jax.numpy as jnp
import numpy as np
from jax import lax

C = 64
FF = 64
K = 5
NKER = 6
L = 1056
S_DEV = 8
STEP = 10
SPAN = 11
HALF = 5
TAPS = 286
SERIES = 64
S_LOC = 2
KSIZE = 2342912
SMALL = 256
PARAMS = 2343168


def pick_freqs(key):
    options = np.array([value for value in range(3, L // 2) if L % value == 0], np.int32)
    ranking = jax.random.permutation(key, options.shape[0])
    chosen = jnp.asarray(options)[ranking[:K - 2]]
    fixed_pair = jnp.array([2, L // 2], jnp.int32)
    picked = jnp.concatenate([fixed_pair, chosen])
    shuffle = jax.random.permutation(jax.random.fold_in(key, 5), K)
    return picked[shuffle]


def draw_freqs(key, part):
    frequencies = pick_freqs(key)
    return frequencies


def draw_series(key, part):
    frequencies = pick_freqs(key)
    key = jax.random.fold_in(key, 11)
    keys = jax.random.split(key, 4)
    positions = jnp.arange(L, dtype=jnp.int32)
    strength = jnp.exp(jax.random.uniform(keys[0], (SERIES, K), minval=math.log(0.3), maxval=math.log(3.0)))
    channel = jnp.exp(jax.random.uniform(keys[1], (SERIES, K, C), minval=math.log(0.5), maxval=math.log(2.0)))
    phase = jax.random.uniform(keys[2], (SERIES, K, C), minval=-math.pi, maxval=math.pi)
    signal = jnp.zeros((SERIES, L, C), jnp.float32)
    for which in range(K):
        turns = (positions * frequencies[which] % L).astype(jnp.float32) * (2.0 * math.pi / L)
        amplitude = strength[:, which, None, None] * channel[:, which, None, :]
        signal = signal + amplitude * jnp.cos(turns[None, :, None] + phase[:, which, None, :])
    noise = 0.5 * jnp.clip(jax.random.normal(keys[3], (SERIES, L, C)), -4.0, 4.0)
    envelope = 0.6 + 1.2 * positions.astype(jnp.float32) / L
    return (envelope[None, :, None] * (signal + noise)).astype(jnp.bfloat16)


def draw_lengths(key, part):
    key = jax.random.fold_in(key, 13)
    keys = jax.random.split(key, 3)
    groups = SERIES // S_DEV
    shortest = 3 * L // 4
    drawn = jax.random.randint(keys[0], (groups, S_DEV), shortest, L + 1)
    full_slot = jax.random.randint(keys[1], (groups, 1), 0, S_DEV)
    short_slot = (full_slot + 1 + jax.random.randint(keys[2], (groups, 1), 0, S_DEV - 1)) % S_DEV
    slots = jnp.arange(S_DEV, dtype=jnp.int32)[None, :]
    drawn = jnp.where(slots == full_slot, L, jnp.where(slots == short_slot, shortest, drawn))
    return drawn.reshape(SERIES).astype(jnp.int32)


def draw_small(key, part):
    key = jax.random.fold_in(key, 17)
    keys = jax.random.split(key, 3)
    biases = 0.3 * jnp.clip(jax.random.normal(keys[0], (FF + C,)), -4.0, 4.0)
    gains = 1.0 + jax.random.uniform(keys[1], (C,), minval=-0.5, maxval=0.5)
    shifts = 0.3 * jnp.clip(jax.random.normal(keys[2], (C,)), -4.0, 4.0)
    return jnp.concatenate([biases, gains, shifts])


def shard_levels(key, dims, cuts, least, largest):
    level = 1.0
    for axis_at, shards_of in cuts:
        heights = jax.random.uniform(jax.random.fold_in(jax.random.fold_in(key, 6), axis_at), (shards_of,), jnp.float32, least / len(cuts), largest / len(cuts))
        level = level * jnp.repeat(jnp.exp(heights), dims[axis_at] // shards_of).reshape((-1,) + (1,) * (len(dims) - 1 - axis_at))
    return level


def bell_draw(key, shape, width, limit, cuts=(), kind=jnp.bfloat16):
    entries = jax.random.normal(key, shape, jnp.float32) * width
    if len(cuts) > 0:
        entries = shard_levels(key, shape, cuts, -0.22, 0.18) * entries
    return jnp.clip(entries, min=-limit, max=limit).astype(kind)


def setup_inputs(seed: int = 0) -> dict:
    key_of = jax.random.split(jax.random.key(seed), 11)
    return {
        "series": draw_series(jax.random.fold_in(key_of[10], 71), 0),
        "lengths": draw_lengths(jax.random.fold_in(key_of[10], 71), 0),
        "freqs": draw_freqs(jax.random.fold_in(key_of[10], 71), 0),
        "cotangent": bell_draw(key_of[3], (SERIES, L, C), 1.0, 6.0, ((0, 8), (1, 4))),
        "kernels": bell_draw(key_of[4], (KSIZE,), (TAPS * C // 36) ** -0.5, 0.25, ((0, 32),), jnp.float32),
        "kernel_m": bell_draw(key_of[5], (KSIZE,), (0.11 / PARAMS ** 0.5), 0.0004272461, ((0, 32),), jnp.float32),
        "kernel_v": jnp.clip(jnp.exp(math.log(3.4141811600107985e-09) - 2.7725887 * jax.random.uniform(key_of[6], (KSIZE,), jnp.float32) ** shard_levels(key_of[6], (KSIZE,), ((0, 32),), -0.2, 0.2)), 2.133863225006749e-10, 3.4141811600107985e-09),
        "small": draw_small(jax.random.fold_in(key_of[10], 71), 0),
        "small_m": bell_draw(key_of[8], (SMALL,), (0.3 / PARAMS ** 0.5), 0.0012207031, (), jnp.float32),
        "small_v": jnp.clip(jnp.exp(jax.random.uniform(key_of[9], (SMALL,), jnp.float32, math.log(8.535452900026996e-10), math.log(1.2803178961462436e-08))), 8.535452900026996e-10, 1.2803178961462436e-08),
    }


@jax.custom_vjp
def low(v):
    return lax.optimization_barrier(v.astype(jnp.bfloat16)).astype(jnp.float32)

@jax.custom_vjp
def low_back(v):
    return v

def low_keep(v):
    return (low(v), None)

def low_pass(kept, grad):
    return (grad,)

def back_keep(v):
    return (v, None)

def back_low(kept, grad):
    return (low(grad),)
low.defvjp(low_keep, low_pass)
low_back.defvjp(back_keep, back_low)
precise = lax.Precision.HIGHEST
beta_one = 0.9
beta_two = 0.999
learn_rate = 0.1
weight_decay = 0.01
adam_eps = 1e-08
clip_norm = 1.0
norm_eps = 1e-05

def tap_table():
    table = np.zeros((SPAN * SPAN, TAPS), np.float32)
    column = 0
    for kernel in range(NKER):
        for row_off in range(-kernel, kernel + 1):
            for col_off in range(-kernel, kernel + 1):
                table[(row_off + HALF) * SPAN + col_off + HALF, column] = 1.0 / NKER
                column += 1
    return table

def column_shifts(values, period):
    length = values.shape[1]
    padded = jnp.pad(values, ((0, 0), (HALF, HALF), (0, 0)))
    within = jnp.arange(length, dtype=jnp.int32) % period
    pieces = []
    for col_off in range(-HALF, HALF + 1):
        inside = (within + col_off >= 0) & (within + col_off < period)
        shifted = padded[:, HALF + col_off:HALF + col_off + length, :]
        pieces.append(jnp.where(inside[None, :, None], shifted, jnp.zeros_like(shifted)))
    return jnp.concatenate(pieces, axis=2)

def rows_sum(spread, period):
    length = spread.shape[1]
    positions = jnp.arange(length, dtype=jnp.int32)
    summed = jnp.zeros((spread.shape[0], length, spread.shape[3]), jnp.float32)
    for row_off in range(-HALF, HALF + 1):
        source = positions + row_off * period
        inside = (source >= 0) & (source < length)
        rolled = jnp.roll(spread[:, :, row_off + HALF, :], -row_off * period, axis=1)
        summed = summed + jnp.where(inside[None, :, None], rolled, jnp.zeros_like(rolled))
    return summed

def conv_apply(values, matrix, period, chan_out):
    shifted = column_shifts(values, period)
    spread = jnp.einsum('slk,km->slm', shifted, matrix, precision=precise)
    spread = spread.reshape(shifted.shape[0], shifted.shape[1], SPAN, chan_out)
    return rows_sum(spread, period)

def forward_matrix(merged, chan_in, chan_out):
    grid = merged.reshape(SPAN, SPAN, chan_in, chan_out)
    return grid.transpose(1, 2, 0, 3).reshape(SPAN * chan_in, SPAN * chan_out)

def adam_update(param, grad, first, second):
    first_new = beta_one * first + (1.0 - beta_one) * grad
    second_new = beta_two * second + (1.0 - beta_two) * grad * grad
    first_hat = first_new / (1.0 - beta_one ** STEP)
    second_hat = second_new / (1.0 - beta_two ** STEP)
    param_new = param - learn_rate * (first_hat / (jnp.sqrt(second_hat) + adam_eps) + weight_decay * param)
    return (param_new, first_new, second_new)

def reference(series, lengths, freqs, cotangent, kernels, kernel_m, kernel_v, small, small_m, small_v):
    table = jnp.asarray(tap_table())
    positions = jnp.arange(L, dtype=jnp.int32)
    valid = (positions[None, :] < lengths[:, None]).astype(jnp.float32)
    turns = positions[:, None] * freqs[None, :] % L
    angle = turns.astype(jnp.float32) * (2.0 * math.pi / L)
    cos_table = jnp.cos(angle)
    sin_table = jnp.sin(angle)
    periods = L // freqs
    groups = SERIES // S_LOC
    split_at = TAPS * C * FF

    def forward(inputs, weights_flat, small_flat):
        taps_one = weights_flat[:split_at].reshape(TAPS, C, FF)
        taps_two = weights_flat[split_at:].reshape(TAPS, FF, C)
        matrix_one = low(forward_matrix(jnp.einsum('xt,tio->xio', table, taps_one, precision=precise), C, FF))
        matrix_two = low(forward_matrix(jnp.einsum('xt,tio->xio', table, taps_two, precision=precise), FF, C))
        bias_one = small_flat[:FF]
        bias_two = small_flat[FF:FF + C]
        gain = small_flat[FF + C:FF + 2 * C]
        ln_shift = small_flat[FF + 2 * C:]

        def group_fn(packed):
            values, valid_rows = packed
            masked = low_back(values * valid_rows[:, :, None])
            real_part = jnp.einsum('slc,lk->skc', masked, cos_table, precision=precise) * (2.0 / L)
            imag_part = jnp.einsum('slc,lk->skc', masked, sin_table, precision=precise) * (2.0 / L)
            magnitude = jnp.sqrt(real_part * real_part + imag_part * imag_part + 1.0)
            branch_weights = jax.nn.softmax(lax.optimization_barrier(jnp.mean(magnitude, axis=2)), axis=1)
            merged = masked
            for which in range(K):
                period = periods[which]
                hidden_pre = low_back(conv_apply(masked, matrix_one, period, FF) + bias_one)
                activated = low(jax.nn.gelu(hidden_pre, approximate=False))
                branch = low_back(conv_apply(activated, matrix_two, period, C) + bias_two)
                merged = merged + branch_weights[:, which, None, None] * branch
            centered = merged - lax.optimization_barrier(jnp.mean(merged, axis=2, keepdims=True))
            normed = centered * lax.rsqrt(lax.optimization_barrier(jnp.mean(centered * centered, axis=2, keepdims=True)) + norm_eps)
            return (normed * gain + ln_shift) * valid_rows[:, :, None]
        grouped = (inputs.reshape(groups, S_LOC, L, C), valid.reshape(groups, S_LOC, L))
        outputs = lax.map(jax.checkpoint(group_fn), grouped)
        return outputs.reshape(SERIES, L, C)
    inputs = series.astype(jnp.float32)
    outputs, pullback = jax.vjp(forward, inputs, kernels, small)
    grad_inputs, grad_kernels, grad_small = pullback(cotangent.astype(jnp.float32))
    grad_norm = jnp.sqrt(jnp.sum(grad_kernels * grad_kernels) + jnp.sum(grad_small * grad_small))
    factor = jnp.minimum(1.0, clip_norm / (grad_norm + 1e-06))
    new_kernels, new_kernel_m, new_kernel_v = adam_update(kernels, grad_kernels * factor, kernel_m, kernel_v)
    new_small, new_small_m, new_small_v = adam_update(small, grad_small * factor, small_m, small_v)
    return (outputs.astype(jnp.bfloat16), grad_inputs.astype(jnp.bfloat16), grad_norm, new_kernels, new_kernel_m, new_kernel_v, new_small, new_small_m, new_small_v)
```

```python
import functools
import math

import jax
import jax.numpy as jnp
import numpy as np
from jax import lax
from jax.experimental import pallas as pl
from jax.experimental.pallas import tpu as pltpu
from jax.sharding import PartitionSpec as P

C = 64
K = 5
NKER = 6
STEP = 10
SPAN = 11
HALF = 5
TAPS = 286
CELLS = SPAN * SPAN
TAP = C * C

beta_one = 0.9
beta_two = 0.999
learn_rate = 0.1
weight_decay = 0.01
adam_eps = 1e-08
clip_norm = 1.0
norm_eps = 1e-05
inv_root_two = 1.0 / math.sqrt(2.0)
inv_root_tau = 1.0 / math.sqrt(2.0 * math.pi)

bf16 = jnp.bfloat16
f32 = jnp.float32
precise = lax.Precision.HIGHEST

OFFS = (-1, 0, 1, 2, -3, -2, 3, 4, -5, -4, 5, 6)
BASES = (-1, 1, -3, 3, -5, 5)
W = 12 * C
CH = 96


def tap_cells():
    cells = []
    for block in range(2):
        for kernel in range(NKER):
            for row_off in range(-kernel, kernel + 1):
                for col_off in range(-kernel, kernel + 1):
                    cells.append(block * CELLS + (row_off + HALF) * SPAN + col_off + HALF)
    return np.array(cells)


@functools.lru_cache(None)
def plan(count):
    cells = tap_cells()
    share = cells.size * TAP // count
    span = max((share * (d + 1) - 1) // TAP - share * d // TAP + 1 for d in range(count))
    needs = []
    clash = [set() for _ in range(2 * CELLS)]
    for d in range(count):
        first = share * d // TAP
        last = (share * (d + 1) - 1) // TAP
        need = set(cells[first : last + 1].tolist())
        needs.append((first, last, need))
        for cell in need:
            clash[cell].update(need)
    room = -(-2 * CELLS // count)
    order = sorted(range(2 * CELLS), key=lambda cell: -len(clash[cell]))
    for seed in range(1000):
        rng = np.random.RandomState(seed)
        owner = np.full(2 * CELLS, -1)
        filled = np.zeros(count, int)
        for cell in order:
            used = {owner[other] for other in clash[cell]}
            free = [d for d in range(count) if d not in used and filled[d] < room]
            if not free:
                break
            least = min(filled[d] for d in free)
            free = [d for d in free if filled[d] == least]
            owner[cell] = free[rng.randint(len(free))]
            filled[owner[cell]] += 1
        else:
            break
    place = np.zeros(2 * CELLS, int)
    filled[:] = 0
    for cell in range(2 * CELLS):
        place[cell] = filled[owner[cell]]
        filled[owner[cell]] += 1
    spread = np.zeros((count, count, span), np.float32)
    pick = np.zeros((count, room, count), np.float32)
    for d, (first, last, need) in enumerate(needs):
        for tap in range(first, last + 1):
            spread[d, owner[cells[tap]], tap - first] = 1.0
        for cell in need:
            pick[owner[cell], place[cell], d] = 1.0
    weight = np.zeros((count, room), np.float32)
    for cell in range(2 * CELLS):
        row, col = divmod(cell % CELLS, SPAN)
        weight[owner[cell], place[cell]] = NKER - max(abs(row - HALF), abs(col - HALF))
    row_of = owner * room + place
    return span, room, spread, pick, weight, row_of


def block_kernel(
    length,
    freq_ref,
    len_ref,
    x_ref,
    cot_ref,
    trig_ref,
    w1_ref,
    w2_ref,
    small_ref,
    out_ref,
    gser_ref,
    gm1_ref,
    gm2_ref,
    gsm_ref,
    xf_ref,
    af_ref,
    pk_ref,
    xs_ref,
    s_ref,
    gf_ref,
    gp_ref,
    gr_ref,
    act_ref,
    slope_ref,
    br_ref,
    mg_ref,
    gin_ref,
    wi_ref,
    w1s_ref,
    w2s_ref,
    w1r_ref,
    w2r_ref,
    wv_ref,
    gw_ref,
    gb_ref,
):
    L = length
    NCH = L // CH
    GP = 544

    def lanes(rows):
        return lax.broadcasted_iota(jnp.int32, (rows, 128), 1) < C

    def swap(v):
        return pltpu.roll(v, C, 1)

    def rows(i, n=CH):
        return pl.ds(pl.multiple_of(i * n, 16), n)

    def half_sum(v):
        low = lanes(v.shape[0])
        a = jnp.sum(jnp.where(low, v, 0.0), axis=1, keepdims=True)
        b = jnp.sum(jnp.where(low, 0.0, v), axis=1, keepdims=True)
        return jnp.where(low, a, b)

    def fold(v):
        return jnp.sum(v.reshape(v.shape[0] // 8, 8, 128), axis=0)

    def period(j):
        return L // freq_ref[j]

    s_zero = jnp.zeros((CH, 128), f32)
    for b in range(11):

        @pl.loop(0, NCH)
        def _(i):
            s_ref[b, rows(i), :] = s_zero
            s_ref[b, pl.ds(pl.multiple_of(2 * L + i * CH, 16), CH), :] = s_zero

    for s in range(2):
        for start, stop in ((0, L), (L + 1632, gf_ref.shape[1])):

            @pl.loop(0, (stop - start) // 16)
            def _(i):
                gf_ref[s, pl.ds(pl.multiple_of(start + i * 16, 8), 16), :] = jnp.zeros((16, 128), f32)

    for start, stop in ((0, GP), (GP + L, gp_ref.shape[0])):

        @pl.loop(0, (stop - start) // 16)
        def _(i):
            gp_ref[pl.ds(pl.multiple_of(start + i * 16, 8), 16), :] = jnp.zeros((16, 128), f32)

    pk_ref[0:16, :] = jnp.zeros((16, 128), f32)
    pk_ref[L + 16 : L + 48, :] = jnp.zeros((32, 128), f32)

    for src, cols, rws in ((w1_ref, w1s_ref, w1r_ref), (w2_ref, w2s_ref, w2r_ref)):
        for q in range(6):
            cols[:, 128 * q : 128 * q + 128] = swap(
                src[:, 128 * q : 128 * q + 128].astype(f32)
            ).astype(bf16)
            rws[128 * q : 128 * q + 64, :] = src[128 * q + 64 : 128 * q + 128, :]
            rws[128 * q + 64 : 128 * q + 128, :] = src[128 * q : 128 * q + 64, :]

    gm1_ref[...] = jnp.zeros((W, W), f32)
    gm2_ref[...] = jnp.zeros((W, W), f32)
    gb_ref[...] = jnp.zeros((4, 8, 128), f32)
    gw_ref[...] = jnp.zeros((K, 8, 128), f32)

    own = jnp.where(lanes(1), len_ref[0], len_ref[1])

    def valid(i, n=CH):
        return i * n + lax.broadcasted_iota(jnp.int32, (n, 128), 0) < own

    @pl.loop(0, NCH)
    def _(i):
        v = jnp.where(valid(i), x_ref[rows(i), :].astype(f32), 0.0)
        mg_ref[rows(i), :] = v
        pk_ref[pl.ds(pl.multiple_of(16 + i * CH, 16), CH), :] = v

    def fill_pairs(dst):
        def step(t0, n):
            a = pk_ref[pl.ds(16 + t0, n), :]
            b = pk_ref[pl.ds(17 + t0, n), :]
            low = lanes(n)
            dst[0, pl.ds(8 + t0, n), :] = jnp.where(low, a, swap(b))
            dst[1, pl.ds(8 + t0, n), :] = jnp.where(low, swap(a), b)

        @pl.loop(0, NCH)
        def _(i):
            step(pl.multiple_of(i * CH, 8) - 8, CH)

        step(L - 8, 16)

    fill_pairs(xf_ref)

    xm = mg_ref[...].astype(bf16)
    spec = lax.dot_general(
        trig_ref[...], xm, (((0,), (0,)), ((), ())), preferred_element_type=f32
    )
    spec = (spec[0:16] + spec[16:32] + spec[32:48]) * (2.0 / L)
    real, imag = spec[0:8], spec[8:16]
    magnitude = jnp.sqrt(real * real + imag * imag + 1.0)
    mean_mag = half_sum(magnitude) * (1.0 / C)
    live = lax.broadcasted_iota(jnp.int32, (8, 128), 0) < K
    top = jnp.max(jnp.where(live, mean_mag, -1e30), axis=0, keepdims=True)
    ex = jnp.where(live, jnp.exp(mean_mag - top), 0.0)
    weights = ex / jnp.sum(ex, axis=0, keepdims=True)
    wv_ref[...] = weights

    def fill_within(p):
        inv = 1.0 / jnp.full((CH, 128), p, jnp.int32).astype(f32)
        high = jnp.where(lanes(CH), 0, 1)

        @pl.loop(0, NCH)
        def _(i):
            t = i * CH + lax.broadcasted_iota(jnp.int32, (CH, 128), 0)
            q = ((t.astype(f32) + 0.5) * inv).astype(jnp.int32)
            wi_ref[rows(i), :] = t - q * p + high

    def build_cols(src, p, nk):
        @pl.loop(0, NCH)
        def _(i):
            wi = wi_ref[rows(i), :]
            for q in range(2 * nk):
                base = BASES[q]
                keep = wi >= -base if base < 0 else wi < p - base
                for s in range(2):
                    v = src[s, pl.ds(8 + base + i * CH, CH), :]
                    xs_ref[pl.ds(pl.multiple_of(s * L + i * CH, 16), CH), 128 * q : 128 * q + 128] = (
                        jnp.where(keep, v, 0.0).astype(bf16)
                    )

    RM = L

    def to_slots(get, tiles):
        low = lanes(RM)
        for n in range(tiles):
            d0, d1 = get(n)
            for h in range(2):
                a = d0[:, 128 * h : 128 * h + 128]
                b = d1[:, 128 * h : 128 * h + 128]
                s_ref[4 * n + 2 * h, L : 2 * L, :] = jnp.where(low, a, b)
                if 4 * n + 2 * h + 1 < 11:
                    s_ref[4 * n + 2 * h + 1, L : 2 * L, :] = jnp.where(low, b, a)

    def mm_forward(w_ref, ws_ref, nk, nr):
        def get(n):
            cut = slice(256 * n, 256 * n + 256)
            return (
                jnp.dot(xs_ref[0:L, : 256 * nk], w_ref[: 256 * nk, cut], preferred_element_type=f32),
                jnp.dot(
                    xs_ref[L : 2 * L, : 256 * nk], ws_ref[: 256 * nk, cut], preferred_element_type=f32
                ),
            )

        to_slots(get, nr)

    def mm_adjoint(w_ref, wr_ref, nk, nr):
        dims = (((1,), (1,)), ((), ()))

        def get(n):
            cut = slice(256 * n, 256 * n + 256)
            return (
                lax.dot_general(
                    gr_ref[0:L, : 256 * nr], w_ref[cut, : 256 * nr], dims, preferred_element_type=f32
                ),
                lax.dot_general(
                    gr_ref[L : 2 * L, : 256 * nr],
                    wr_ref[cut, : 256 * nr],
                    dims,
                    preferred_element_type=f32,
                ),
            )

        to_slots(get, nk)

    def mm_weights(gm_ref, nk, nr):
        for n in range(nr):
            cut = slice(256 * n, 256 * n + 256)
            gm_ref[: 256 * nk, cut] += lax.dot_general(
                xs_ref[:, : 256 * nk],
                gr_ref[:, cut],
                (((0,), (0,)), ((), ())),
                preferred_element_type=f32,
            )

    def sum_rows(i, p, nr):
        even = jnp.zeros((CH, 128), f32)
        odd = even
        for b in range(min(4 * nr, 11)):
            off = L + jnp.clip(OFFS[b] * p, -L, L)
            v = s_ref[b, pl.ds(off + i * CH, CH), :]
            if b % 2 == 0:
                even = even + v
            else:
                odd = odd + v
        return even + swap(odd)

    def sum_cols(i, p, nk):
        wi = wi_ref[rows(i), :] - jnp.where(lanes(CH), 0, 1)
        even = jnp.zeros((CH, 128), f32)
        odd = even
        for b in range(min(4 * nk, 11)):
            d = OFFS[b]
            v = s_ref[b, pl.ds(L - d + i * CH, CH), :]
            if d < 0:
                v = jnp.where(wi < p + d, v, 0.0)
            elif d > 0:
                v = jnp.where(wi >= d, v, 0.0)
            if b % 2 == 0:
                even = even + v
            else:
                odd = odd + v
        return even + swap(odd)

    def build_rows(p, nr):
        @pl.loop(0, 17)
        def _(i):
            a = gp_ref[pl.ds(pl.multiple_of(GP + i * CH, 8), CH), :]
            b = gp_ref[pl.ds(GP - p + i * CH, CH), :]
            low = lanes(CH)
            at = pl.ds(pl.multiple_of(L + i * CH, 8), CH)
            gf_ref[0, at, :] = jnp.where(low, a, swap(b))
            gf_ref[1, at, :] = jnp.where(low, swap(a), b)

        @pl.loop(0, NCH)
        def _(i):
            for q in range(2 * nr):
                off = L + jnp.clip(-BASES[q] * p, -L, L + p)
                for s in range(2):
                    v = gf_ref[s, pl.ds(off + i * CH, CH), :]
                    gr_ref[pl.ds(pl.multiple_of(s * L + i * CH, 16), CH), 128 * q : 128 * q + 128] = (
                        v.astype(bf16)
                    )

    def forward(j, nk, nr):
        p = period(j)
        fill_within(p)
        build_cols(xf_ref, p, nk)
        mm_forward(w1_ref, w1s_ref, nk, nr)
        bias_one = small_ref[0:1, :]
        bias_two = small_ref[1:2, :]

        @pl.loop(0, NCH)
        def _(i):
            h = sum_rows(i, p, nr) + bias_one
            cdf = 0.5 * (1.0 + lax.erf(h * inv_root_two))
            act = (h * cdf).astype(bf16)
            slope_ref[j, rows(i), :] = cdf + h * jnp.exp(-0.5 * h * h) * inv_root_tau
            act_ref[j, rows(i), :] = act
            pk_ref[pl.ds(pl.multiple_of(16 + i * CH, 16), CH), :] = act.astype(f32)

        fill_pairs(af_ref)
        build_cols(af_ref, p, nk)
        mm_forward(w2_ref, w2s_ref, nk, nr)
        wj = wv_ref[pl.ds(j, 1), :]

        @pl.loop(0, NCH)
        def _(i):
            v = sum_rows(i, p, nr) + bias_two
            br_ref[j, rows(i), :] = v
            mg_ref[rows(i), :] += wj * v

    forward(0, 3, 1)

    @pl.loop(1, K - 1)
    def _(j):
        forward(j, 3, 3)

    forward(K - 1, 1, 3)

    same = (
        lax.broadcasted_iota(jnp.int32, (384, 128), 0) % 128 // C
        == lax.broadcasted_iota(jnp.int32, (384, 128), 1) // C
    )
    ones = jnp.where(same, 1.0 / C, 0.0).astype(bf16)

    def half_mean(v):
        a = v.astype(bf16)
        r = v - a.astype(f32)
        b = r.astype(bf16)
        c = (r - b.astype(f32)).astype(bf16)
        return jnp.dot(jnp.concatenate([a, b, c], axis=1), ones, preferred_element_type=f32)

    gain = small_ref[2:3, :]
    shift = small_ref[3:4, :]
    NB = 352

    @pl.loop(0, L // NB)
    def _(i):
        m = mg_ref[rows(i, NB), :]
        ok = valid(i, NB)
        centered = m - half_mean(m)
        inverse = lax.rsqrt(half_mean(centered * centered) + norm_eps)
        normed = centered * inverse
        out_ref[rows(i, NB), :] = jnp.where(ok, normed * gain + shift, 0.0).astype(bf16)
        g_out = jnp.where(ok, cot_ref[rows(i, NB), :].astype(f32), 0.0)
        gb_ref[2] += fold(g_out * normed)
        gb_ref[3] += fold(g_out)
        g_norm = g_out * gain
        gm = inverse * (g_norm - half_mean(g_norm) - normed * half_mean(g_norm * normed))
        mg_ref[rows(i, NB), :] = gm
        gin_ref[rows(i, NB), :] = gm

    def backward(j, nk, nr):
        p = period(j)
        fill_within(p)
        wj = wv_ref[pl.ds(j, 1), :]

        @pl.loop(0, NCH)
        def _(i):
            gm = mg_ref[rows(i), :]
            gw_ref[j] += fold(gm * br_ref[j, rows(i), :])
            g = (wj * gm).astype(bf16).astype(f32)
            gb_ref[1] += fold(g)
            gp_ref[pl.ds(pl.multiple_of(GP + i * CH, 8), CH), :] = g
            pk_ref[pl.ds(pl.multiple_of(16 + i * CH, 16), CH), :] = act_ref[j, rows(i), :].astype(f32)

        build_rows(p, nr)
        mm_adjoint(w2_ref, w2r_ref, nk, nr)
        fill_pairs(af_ref)
        build_cols(af_ref, p, nk)
        mm_weights(gm2_ref, nk, nr)

        @pl.loop(0, NCH)
        def _(i):
            g = (sum_cols(i, p, nk) * slope_ref[j, rows(i), :]).astype(bf16).astype(f32)
            gb_ref[0] += fold(g)
            gp_ref[pl.ds(pl.multiple_of(GP + i * CH, 8), CH), :] = g

        build_rows(p, nr)
        mm_adjoint(w1_ref, w1r_ref, nk, nr)
        build_cols(xf_ref, p, nk)
        mm_weights(gm1_ref, nk, nr)

        @pl.loop(0, NCH)
        def _(i):
            gin_ref[rows(i), :] += sum_cols(i, p, nk)

    backward(0, 3, 1)

    @pl.loop(1, K - 1)
    def _(j):
        backward(j, 3, 3)

    backward(K - 1, 1, 3)

    row8 = lax.broadcasted_iota(jnp.int32, (8, 128), 0)
    g_weights = jnp.zeros((8, 128), f32)
    for j in range(K):
        total = jnp.sum(gw_ref[j], axis=0, keepdims=True)
        g_weights = jnp.where(row8 == j, total, g_weights)
    g_weights = half_sum(g_weights)
    weights = wv_ref[...]
    g_score = weights * (g_weights - jnp.sum(weights * g_weights, axis=0, keepdims=True))
    coeff = g_score / (magnitude * C) * (2.0 / L)
    coef = jnp.concatenate([coeff * real, coeff * imag], axis=0)
    c_hi = coef.astype(bf16)
    c_lo = (coef - c_hi.astype(f32)).astype(bf16)
    c_all = jnp.concatenate([c_hi, c_hi, c_hi], axis=0)

    @pl.loop(0, L // NB)
    def _(i):
        t = trig_ref[rows(i, NB), :]
        g = (
            gin_ref[rows(i, NB), :]
            + jnp.dot(t, c_all, preferred_element_type=f32)
            + jnp.dot(t[:, 0:16], c_lo, preferred_element_type=f32)
        )
        gser_ref[rows(i, NB), :] = jnp.where(valid(i, NB), g, 0.0).astype(bf16)

    for q in range(4):
        total = jnp.sum(gb_ref[q], axis=0, keepdims=True)
        gsm_ref[q : q + 1, :] = total + swap(total)


def run_block(x, cot, lens, freqs, w1, w2, small):
    L = x.shape[0]
    positions = jnp.arange(L, dtype=jnp.int32)
    turns = positions[:, None] * freqs[None, :] % L
    angle = turns.astype(f32) * (2.0 * math.pi / L)
    pad = ((0, 0), (0, 8 - K))
    trig = jnp.concatenate([jnp.pad(jnp.cos(angle), pad), jnp.pad(jnp.sin(angle), pad)], axis=1)
    hi = lax.reduce_precision(trig, 8, 7)
    rest = trig - hi
    mid = lax.reduce_precision(rest, 8, 7)
    trig = jnp.concatenate([hi, mid, rest - mid], axis=1).astype(bf16)
    packed = small.reshape(4, C)
    packed = jnp.concatenate([packed, packed], axis=1)
    vm = pl.BlockSpec(memory_space=pltpu.VMEM)
    sm = pl.BlockSpec(memory_space=pltpu.SMEM)
    sds = jax.ShapeDtypeStruct
    out, gser, gm1, gm2, gsm = pl.pallas_call(
        functools.partial(block_kernel, L),
        out_shape=(
            sds((L, 128), bf16),
            sds((L, 128), bf16),
            sds((W, W), f32),
            sds((W, W), f32),
            sds((4, 128), f32),
        ),
        in_specs=[sm, sm, vm, vm, vm, vm, vm, vm],
        out_specs=(vm,) * 5,
        scratch_shapes=[
            pltpu.VMEM((2, L + 16, 128), f32),
            pltpu.VMEM((2, L + 16, 128), f32),
            pltpu.VMEM((L + 48, 128), f32),
            pltpu.VMEM((2 * L, W), bf16),
            pltpu.VMEM((11, 3 * L, 128), f32),
            pltpu.VMEM((2, 3552, 128), f32),
            pltpu.VMEM((544 + L + 576, 128), f32),
            pltpu.VMEM((2 * L, W), bf16),
            pltpu.VMEM((K, L, 128), bf16),
            pltpu.VMEM((K, L, 128), f32),
            pltpu.VMEM((K, L, 128), f32),
            pltpu.VMEM((L, 128), f32),
            pltpu.VMEM((L, 128), f32),
            pltpu.VMEM((L, 128), jnp.int32),
            pltpu.VMEM((W, W), bf16),
            pltpu.VMEM((W, W), bf16),
            pltpu.VMEM((W, W), bf16),
            pltpu.VMEM((W, W), bf16),
            pltpu.VMEM((8, 128), f32),
            pltpu.VMEM((K, 8, 128), f32),
            pltpu.VMEM((4, 8, 128), f32),
        ],
        compiler_params=pltpu.CompilerParams(vmem_limit_bytes=60 << 20),
        name="block",
    )(freqs, lens, x, cot, trig, w1, w2, packed)
    return out, gser, gm1, gm2, gsm[:, :C].reshape(-1)


def adam_update(param, grad, first, second):
    first_new = beta_one * first + (1.0 - beta_one) * grad
    second_new = beta_two * second + (1.0 - beta_two) * grad * grad
    first_hat = first_new / (1.0 - beta_one**STEP)
    second_hat = second_new / (1.0 - beta_two**STEP)
    param_new = param - learn_rate * (
        first_hat / (jnp.sqrt(second_hat) + adam_eps) + weight_decay * param
    )
    return (param_new, first_new, second_new)


SLOT_OF = np.argsort(OFFS[:11])
CELL_OF = [off + HALF for off in OFFS[:11]]


def to_matrix(merged):
    grid = merged.reshape(SPAN, SPAN, C, C)
    grid = jnp.concatenate([grid[o : o + 1] for o in CELL_OF], axis=0)
    grid = jnp.concatenate([grid[:, o : o + 1] for o in CELL_OF], axis=1)
    mat = grid.transpose(1, 2, 0, 3).reshape(SPAN * C, SPAN * C)
    return jnp.pad(mat, ((0, C), (0, C)))


def from_matrix(mat):
    grid = mat[: SPAN * C, : SPAN * C].reshape(SPAN, C, SPAN, C).transpose(2, 0, 1, 3)
    grid = jnp.concatenate([grid[o : o + 1] for o in SLOT_OF], axis=0)
    grid = jnp.concatenate([grid[:, o : o + 1] for o in SLOT_OF], axis=1)
    return grid.reshape(CELLS, TAP)


def local(series, lengths, freqs, cotangent, kernels, kernel_m, kernel_v, small, small_m, small_v):
    wide_count = lax.axis_size("wide")
    count = wide_count * lax.axis_size("batch")
    wide_index = lax.axis_index("wide")
    me = lax.axis_index(("wide", "batch"))
    both = ("wide", "batch")
    span, room, spread, pick, weight, row_of = plan(count)
    share = kernels.shape[0]

    spread_me = lax.dynamic_index_in_dim(jnp.asarray(spread), me, 0, keepdims=False)
    pick_me = lax.dynamic_index_in_dim(jnp.asarray(pick), me, 0, keepdims=False)
    weight_me = lax.dynamic_index_in_dim(jnp.asarray(weight), me, 0, keepdims=False)
    lead = me * share % TAP
    taps = lax.dynamic_update_slice_in_dim(jnp.zeros((span * TAP,), f32), kernels, lead, 0)
    slots = jnp.einsum("ot,tw->ow", spread_me, taps.reshape(span, TAP), precision=precise)
    got = lax.all_to_all(slots, both, split_axis=0, concat_axis=0, tiled=True)
    merged = jnp.einsum("kd,dw->kw", pick_me, got, precision=precise) * (1.0 / NKER)
    merged = lax.all_gather(merged.astype(bf16), both, axis=0, tiled=True)
    merged = jnp.take(merged, jnp.asarray(row_of), axis=0)
    w1 = to_matrix(merged[:CELLS])
    w2 = to_matrix(merged[CELLS:])

    local_series = series.shape[0] // wide_count
    whole_x = lax.all_to_all(series, "wide", split_axis=0, concat_axis=1, tiled=True)
    whole_cot = lax.all_to_all(cotangent, "wide", split_axis=0, concat_axis=1, tiled=True)
    own_lengths = lax.dynamic_slice_in_dim(lengths, wide_index * local_series, local_series, 0)
    if local_series % 2:
        whole_x = jnp.pad(whole_x, ((0, 1), (0, 0), (0, 0)))
        whole_cot = jnp.pad(whole_cot, ((0, 1), (0, 0), (0, 0)))
        own_lengths = jnp.pad(own_lengths, (0, 1))
    rank = jnp.sum(freqs[:, None] > freqs[None, :], axis=1)
    at = jnp.arange(K)
    ascending = jnp.sum(jnp.where(rank[:, None] == at[None, :], freqs[:, None], 0), axis=0)

    def pack(v):
        return v.transpose(1, 0, 2).reshape(v.shape[1], 2 * C)

    def unpack(v):
        return v.reshape(v.shape[0], 2, C).transpose(1, 0, 2)

    outs, gsers = [], []
    gm1, gm2, small_grad = 0.0, 0.0, 0.0
    for pair in range(whole_x.shape[0] // 2):
        cut = slice(2 * pair, 2 * pair + 2)
        out, gser, g1, g2, gs = run_block(
            pack(whole_x[cut]), pack(whole_cot[cut]), own_lengths[cut], ascending, w1, w2, small
        )
        outs.append(unpack(out))
        gsers.append(unpack(gser))
        gm1, gm2, small_grad = gm1 + g1, gm2 + g2, small_grad + gs
    output_whole = jnp.concatenate(outs)[:local_series]
    grad_whole = jnp.concatenate(gsers)[:local_series]
    output_shards = lax.all_to_all(output_whole, "wide", split_axis=1, concat_axis=0, tiled=True)
    grad_shards = lax.all_to_all(grad_whole, "wide", split_axis=1, concat_axis=0, tiled=True)

    cells = jnp.concatenate([from_matrix(gm1), from_matrix(gm2)], axis=0)
    cell_of = np.full(count * room, 2 * CELLS)
    cell_of[row_of] = np.arange(2 * CELLS)
    cells = jnp.pad(cells, ((0, 1), (0, 0)))
    cells = jnp.take(cells, jnp.asarray(cell_of), axis=0)
    summed = lax.psum_scatter(cells, both, scatter_dimension=0, tiled=True) * (1.0 / NKER)
    square = jnp.sum(jnp.sum(summed * summed, axis=1) * weight_me)
    small_sum = lax.psum(small_grad, both)
    square_sum = lax.psum(square, both) + jnp.sum(small_sum * small_sum)
    back = jnp.einsum("kd,kw->dw", pick_me, summed, precision=precise)
    got = lax.all_to_all(back, both, split_axis=0, concat_axis=0, tiled=True)
    tap_grad = jnp.einsum("ot,ow->tw", spread_me, got, precision=precise)
    share_grad = lax.dynamic_slice_in_dim(tap_grad.reshape(-1), lead, share, 0)

    grad_norm = jnp.sqrt(square_sum)
    factor = jnp.minimum(1.0, clip_norm / (grad_norm + 1e-06))
    new_kernels, new_kernel_m, new_kernel_v = adam_update(
        kernels, share_grad * factor, kernel_m, kernel_v
    )
    new_small, new_small_m, new_small_v = adam_update(small, small_sum * factor, small_m, small_v)
    return (
        output_shards,
        grad_shards,
        grad_norm,
        new_kernels,
        new_kernel_m,
        new_kernel_v,
        new_small,
        new_small_m,
        new_small_v,
    )


def solution(mesh):
    placed = (
        P("batch", "wide", None),
        P("batch"),
        P(),
        P("batch", "wide", None),
        P(("wide", "batch")),
        P(("wide", "batch")),
        P(("wide", "batch")),
        P(),
        P(),
        P(),
    )
    return jax.shard_map(
        local,
        mesh=mesh,
        in_specs=placed,
        out_specs=(
            P("batch", "wide", None),
            P("batch", "wide", None),
            P(),
            P(("wide", "batch")),
            P(("wide", "batch")),
            P(("wide", "batch")),
            P(),
            P(),
            P(),
        ),
        check_vma=False,
    )
```

```python
import functools
import math

import jax
import jax.numpy as jnp
import numpy as np
from jax import lax
from jax.experimental import pallas as pl
from jax.experimental.pallas import tpu as pltpu
from jax.sharding import PartitionSpec as P

C = 64
K = 5
NKER = 6
STEP = 10
SPAN = 11
HALF = 5
TAPS = 286
CELLS = SPAN * SPAN
TAP = C * C

beta_one = 0.9
beta_two = 0.999
learn_rate = 0.1
weight_decay = 0.01
adam_eps = 1e-08
clip_norm = 1.0
norm_eps = 1e-05
inv_root_two = 1.0 / math.sqrt(2.0)
inv_root_tau = 1.0 / math.sqrt(2.0 * math.pi)

bf16 = jnp.bfloat16
f32 = jnp.float32
precise = lax.Precision.HIGHEST

OFFS = (-1, 0, 1, 2, -3, -2, 3, 4, -5, -4, 5, 6)
BASES = (-1, 1, -3, 3, -5, 5)
W = 12 * C
CH = 96


def tap_cells():
    cells = []
    for block in range(2):
        for kernel in range(NKER):
            for row_off in range(-kernel, kernel + 1):
                for col_off in range(-kernel, kernel + 1):
                    cells.append(block * CELLS + (row_off + HALF) * SPAN + col_off + HALF)
    return np.array(cells)


@functools.lru_cache(None)
def plan(count):
    cells = tap_cells()
    half = count // 2
    share = cells.size * TAP // count
    holds = [
        range(share * d // TAP, (share * (d + 1) - 1) // TAP + 1) for d in range(count)
    ]
    span = max(len(taps) for taps in holds)
    needs = [sorted(set(cells[taps.start : taps.stop].tolist())) for taps in holds]
    room = -(-CELLS // half)
    deep = -(-max(len(need) for need in needs) // half)
    users = [[d for d in range(count) if cell in needs[d]] for cell in range(2 * CELLS)]
    order = sorted(range(2 * CELLS), key=lambda cell: -len(users[cell]))
    for seed in range(1000):
        rng = np.random.RandomState(seed)
        owner = np.full(2 * CELLS, -1)
        filled = np.zeros(count, int)
        between = np.zeros((count, count), int)
        for cell in order:
            first = cell // CELLS * half
            free = [
                o
                for o in range(first, first + half)
                if filled[o] < room and all(between[d, o] < deep for d in users[cell])
            ]
            if not free:
                break
            cost = [(sum(between[d, o] for d in users[cell]), filled[o]) for o in free]
            least = min(cost)
            free = [o for o, c in zip(free, cost) if c == least]
            o = free[rng.randint(len(free))]
            owner[cell] = o
            filled[o] += 1
            for d in users[cell]:
                between[d, o] += 1
        else:
            break
    place = np.zeros(2 * CELLS, int)
    filled[:] = 0
    for cell in range(2 * CELLS):
        place[cell] = filled[owner[cell]]
        filled[owner[cell]] += 1
    spread = np.zeros((count, half * deep, span), np.float32)
    pick = np.zeros((count, room, half * deep), np.float32)
    between[:] = 0
    for d, taps in enumerate(holds):
        for cell in needs[d]:
            o = owner[cell]
            slot = between[d, o]
            between[d, o] += 1
            pick[o, place[cell], d % half * deep + slot] = 1.0
            for tap in taps:
                if cells[tap] == cell:
                    spread[d, o % half * deep + slot, tap - taps.start] = 1.0
    weight = np.zeros((count, room), np.float32)
    for cell in range(2 * CELLS):
        row, col = divmod(cell % CELLS, SPAN)
        weight[owner[cell], place[cell]] = NKER - max(abs(row - HALF), abs(col - HALF))
    row_of = owner * room + place
    return span, room, deep, spread, pick, weight, row_of


MESH = pl.DeviceIdType.MESH


class Place:
    def __init__(self, wide, batch):
        self.nz, self.nb = wide, batch
        self.ns = math.isqrt(batch // 2)
        self.z = lax.axis_index("wide")
        self.b = lax.axis_index("batch")
        self.core = lax.rem(self.b, 2)
        self.x = lax.rem(self.b // 2, self.ns)
        self.y = self.b // (2 * self.ns)
        self.half = wide * batch // 2
        self.me = self.z * batch + self.b
        self.mine = lax.rem(self.me, self.half)

    def batch_of(self, y, x, core):
        return (y * self.ns + x) * 2 + core

    def at_z(self, d):
        return (lax.rem(self.z + d, self.nz), self.b)

    def at_y(self, d):
        return (self.z, self.batch_of(lax.rem(self.y + d, self.ns), self.x, self.core))

    def at_x(self, d):
        return (self.z, self.batch_of(self.y, lax.rem(self.x + d, self.ns), self.core))

    def sibling(self):
        return (self.z, self.batch_of(self.y, self.x, 1 - self.core))

    def at_half(self, d):
        other = self.me - self.mine + lax.rem(self.mine + d, self.half)
        return (other // self.nb, lax.rem(other, self.nb))

    def at_all(self, d):
        other = lax.rem(self.me + d, self.nz * self.nb)
        return (other // self.nb, lax.rem(other, self.nb))


def greet(peers):
    barrier = pltpu.get_barrier_semaphore()
    for peer in peers:
        pl.semaphore_signal(barrier, inc=1, device_id=peer, device_id_type=MESH)
    pl.semaphore_wait(barrier, len(peers))


def send(src, dst, sems, k, peer):
    copy = pltpu.make_async_remote_copy(
        src_ref=src,
        dst_ref=dst,
        send_sem=sems.at[0, k],
        recv_sem=sems.at[1, k],
        device_id=peer,
        device_id_type=MESH,
    )
    copy.start()
    return copy


def lane_low(rows):
    return lax.broadcasted_iota(jnp.int32, (rows, 128), 1) < C


def gather_kernel(
    wide,
    batch,
    lead_step,
    span,
    room,
    deep,
    per,
    spread_ref,
    pick_ref,
    taps_ref,
    series_ref,
    cot_ref,
    x_ref,
    c_ref,
    all_ref,
    tap_ref,
    slot_ref,
    got_ref,
    xs_ref,
    cs_ref,
    tap_sem,
    x_sem,
    c_sem,
    z_sem,
    a_sem,
    b_sem,
    core_sem,
):
    at = Place(wide, batch)
    nz, ns, half = at.nz, at.ns, at.half
    shard = series_ref.shape[1]
    pad = x_ref.shape[1] - shard
    greet(
        [at.at_half(d) for d in range(1, half)] + [at.at_z(d) for d in range(1, nz)]
    )

    held = taps_ref.shape[0]
    tap_ref[...] = jnp.zeros(tap_ref.shape, f32)
    tap_ref[pl.ds(lax.rem(at.me * lead_step, 32), held), :] = taps_ref[...]

    @pl.loop(0, half)
    def _(o):
        for s in range(deep):
            total = jnp.zeros((32, 128), f32)
            for t in range(span):
                total = total + spread_ref[o * deep + s, t] * tap_ref[32 * t : 32 * t + 32, :]
            slot_ref[o, s] = total

    waits = []
    for d in range(1, half):
        waits.append(
            send(
                slot_ref.at[lax.rem(at.mine + d, half)],
                got_ref.at[at.mine],
                tap_sem,
                d - 1,
                at.at_half(d),
            )
        )
    got_ref[at.mine] = slot_ref[at.mine]

    def pack(src, keep):
        for z in range(nz):
            first = src[per * z].astype(f32)
            second = src[per * z + 1].astype(f32) if per == 2 else jnp.zeros_like(first)
            both = jnp.concatenate([first, second], axis=1)
            both = jnp.concatenate([both, jnp.zeros((pad, 128), f32)], axis=0)
            keep[z] = both.astype(bf16)

    def exchange(keep, out, sems):
        for d in range(1, nz):
            waits.append(send(keep.at[lax.rem(at.z + d, nz)], out.at[at.z], sems, d - 1, at.at_z(d)))
        out[at.z] = keep[at.z]

    pack(series_ref, xs_ref)
    exchange(xs_ref, x_ref, x_sem)
    pack(cot_ref, cs_ref)

    for d in range(1, half):
        waits[d - 1].wait_recv()

    for k in range(room):
        total = jnp.zeros((32, 128), f32)

        def add(q, total):
            for s in range(deep):
                total = total + pick_ref[k, q * deep + s] * got_ref[q, s]
            return total

        total = lax.fori_loop(0, half, add, total)
        all_ref[at.z, at.y, at.x, at.core, 32 * k : 32 * k + 32, :] = (
            total * (1.0 / NKER)
        ).astype(bf16)

    cut = room * 32 // 2
    low, high = pl.ds(0, cut), pl.ds(cut, cut)
    block = all_ref.at[at.z, at.y, at.x, at.core]
    stage = [send(block, block, z_sem, d - 1, at.at_z(d)) for d in range(1, nz)]
    for copy in stage:
        copy.wait()
    exchange(cs_ref, c_ref, c_sem)
    stage = []
    for d in range(1, ns):
        part = all_ref.at[:, at.y, at.x, at.core, low]
        stage.append(send(part, part, a_sem, d - 1, at.at_y(d)))
        part = all_ref.at[:, at.y, at.x, at.core, high]
        stage.append(send(part, part, b_sem, d - 1, at.at_x(d)))
    for copy in stage:
        copy.wait()
    stage = []
    for d in range(1, ns):
        part = all_ref.at[:, :, at.x, at.core, low]
        stage.append(send(part, part, a_sem, ns + d - 2, at.at_x(d)))
        part = all_ref.at[:, at.y, :, at.core, high]
        stage.append(send(part, part, b_sem, ns + d - 2, at.at_y(d)))
    for copy in stage:
        copy.wait()
    part = all_ref.at[:, :, :, at.core]
    send(part, part, core_sem, 0, at.sibling()).wait()
    for copy in waits[: half - 1]:
        copy.wait_send()
    for copy in waits[half - 1 :]:
        copy.wait()


def reduce_kernel(
    wide,
    batch,
    lead_step,
    span,
    room,
    deep,
    per,
    spread_ref,
    pick_ref,
    weight_ref,
    grad_ref,
    gsm_ref,
    o_ref,
    g_ref,
    w_ref,
    m_ref,
    v_ref,
    sw_ref,
    sm_ref,
    sv_ref,
    out_ref,
    gser_ref,
    norm_ref,
    nw_ref,
    nm_ref,
    nv_ref,
    nsw_ref,
    nsm_ref,
    nsv_ref,
    oz_ref,
    gz_ref,
    send_ref,
    core_ref,
    acc_ref,
    sa_ref,
    sb_ref,
    ra_ref,
    rb_ref,
    a_ref,
    b_ref,
    sa2_ref,
    sb2_ref,
    ra2_ref,
    rb2_ref,
    sz_ref,
    rz_ref,
    sum_ref,
    back_ref,
    got_ref,
    tile_ref,
    tiles_ref,
    tap_ref,
    core_sem,
    a_sem,
    b_sem,
    z_sem,
    o_sem,
    g_sem,
    tap_sem,
    all_sem,
):
    at = Place(wide, batch)
    nz, ns, half = at.nz, at.ns, at.half
    count = nz * at.nb
    shard = out_ref.shape[1]
    greet([at.at_all(d) for d in range(1, count)])
    cut = room * 32 // 2
    link = send_ref.dtype

    for z in range(nz):
        send_ref[z] = grad_ref[z, :, :, 1 - at.core].astype(link)
    core_copy = send(send_ref, core_ref, core_sem, 0, at.sibling())

    waits = []
    for src, dst, sems in ((o_ref, oz_ref, o_sem), (g_ref, gz_ref, g_sem)):
        for d in range(1, nz):
            waits.append(send(src.at[lax.rem(at.z + d, nz)], dst.at[at.z], sems, d - 1, at.at_z(d)))
        dst[at.z] = src[at.z]

    core_copy.wait()
    for z in range(nz):
        acc_ref[z] = grad_ref[z, :, :, at.core] + core_ref[z].astype(f32)

    stage = []
    for d in range(1, ns):
        x = lax.rem(at.x + d, ns)
        y = lax.rem(at.y + d, ns)
        for z in range(nz):
            for o in range(ns):
                sa_ref[d - 1, z, o] = acc_ref[z, o, x, 0:cut, :].astype(link)
                sb_ref[d - 1, z, o] = acc_ref[z, y, o, cut : 2 * cut, :].astype(link)
        stage.append(send(sa_ref.at[d - 1], ra_ref.at[d - 1], a_sem, d - 1, at.at_x(d)))
        stage.append(send(sb_ref.at[d - 1], rb_ref.at[d - 1], b_sem, d - 1, at.at_y(d)))
    for copy in stage:
        copy.wait()
    for z in range(nz):
        for o in range(ns):
            va = acc_ref[z, o, at.x, 0:cut, :]
            vb = acc_ref[z, at.y, o, cut : 2 * cut, :]
            for d in range(1, ns):
                va = va + ra_ref[d - 1, z, o].astype(f32)
                vb = vb + rb_ref[d - 1, z, o].astype(f32)
            a_ref[z, o] = va
            b_ref[z, o] = vb
    stage = []
    for d in range(1, ns):
        x = lax.rem(at.x + d, ns)
        y = lax.rem(at.y + d, ns)
        for z in range(nz):
            sa2_ref[d - 1, z] = a_ref[z, y].astype(link)
            sb2_ref[d - 1, z] = b_ref[z, x].astype(link)
        stage.append(send(sa2_ref.at[d - 1], ra2_ref.at[d - 1], a_sem, ns + d - 2, at.at_y(d)))
        stage.append(send(sb2_ref.at[d - 1], rb2_ref.at[d - 1], b_sem, ns + d - 2, at.at_x(d)))
    for copy in stage:
        copy.wait()
    for z in range(nz):
        va = a_ref[z, at.y]
        vb = b_ref[z, at.x]
        for d in range(1, ns):
            va = va + ra2_ref[d - 1, z].astype(f32)
            vb = vb + rb2_ref[d - 1, z].astype(f32)
        sz_ref[z, 0:cut, :] = va
        sz_ref[z, cut : 2 * cut, :] = vb
    stage = [
        send(sz_ref.at[lax.rem(at.z + d, nz)], rz_ref.at[d - 1], z_sem, d - 1, at.at_z(d))
        for d in range(1, nz)
    ]
    for copy in stage:
        copy.wait()
    total = sz_ref[at.z]
    for d in range(1, nz):
        total = total + rz_ref[d - 1]
    sum_ref[...] = total * (1.0 / NKER)

    @pl.loop(0, half)
    def _(q):
        for s in range(deep):
            value = jnp.zeros((32, 128), f32)
            for k in range(room):
                value = value + pick_ref[k, q * deep + s] * sum_ref[32 * k : 32 * k + 32, :]
            back_ref[q, s] = value

    backs = [
        send(
            back_ref.at[lax.rem(at.mine + d, half)],
            got_ref.at[at.mine],
            tap_sem,
            d - 1,
            at.at_half(d),
        )
        for d in range(1, half)
    ]
    got_ref[at.mine] = back_ref[at.mine]
    square = jnp.zeros((1, 128), f32)
    for k in range(room):
        value = sum_ref[32 * k : 32 * k + 32, :]
        square = square + weight_ref[k] * jnp.sum(value * value, axis=0, keepdims=True)
    tile_ref[0:2, :] = gsm_ref[...]
    tile_ref[2:3, :] = square
    tile_ref[3:8, :] = jnp.zeros((5, 128), f32)
    tells = [
        send(tile_ref, tiles_ref.at[at.me], all_sem, d - 1, at.at_all(d)) for d in range(1, count)
    ]
    tiles_ref[at.me] = tile_ref[...]
    for copy in tells:
        copy.wait()
    tile = jnp.zeros((8, 128), f32)
    for d in range(count):
        tile = tile + tiles_ref[d]
    small = tile[0:2, :]
    lanes = jnp.sum(tile[2:3, :], axis=1, keepdims=True)
    squares = jnp.sum(jnp.sum(small * small, axis=0, keepdims=True), axis=1, keepdims=True)
    norm = jnp.sqrt(lanes + squares)
    norm_ref[...] = norm
    factor = jnp.minimum(1.0, clip_norm / (norm + 1e-06))
    nsw_ref[...], nsm_ref[...], nsv_ref[...] = adam_update(
        sw_ref[...], small * factor, sm_ref[...], sv_ref[...]
    )
    for copy in backs:
        copy.wait()

    @pl.loop(0, span)
    def _(t):
        value = jnp.zeros((32, 128), f32)
        for q in range(half):
            for s in range(deep):
                value = value + spread_ref[q * deep + s, t] * got_ref[q, s]
        tap_ref[pl.ds(pl.multiple_of(32 * t, 32), 32), :] = value

    held = w_ref.shape[0]
    grad = tap_ref[pl.ds(lax.rem(at.me * lead_step, 32), held), :]
    nw_ref[...], nm_ref[...], nv_ref[...] = adam_update(
        w_ref[...], grad * factor, m_ref[...], v_ref[...]
    )
    for copy in waits:
        copy.wait()
    for src, dst in ((oz_ref, out_ref), (gz_ref, gser_ref)):
        for z in range(nz):
            both = src[z].astype(f32)[0:shard]
            dst[per * z] = both[:, 0:C].astype(bf16)
            if per == 2:
                dst[per * z + 1] = both[:, C:].astype(bf16)


def block_kernel(
    length,
    per,
    row_of,
    freq_ref,
    len_ref,
    x_ref,
    cot_ref,
    all_ref,
    small_ref,
    out_ref,
    gser_ref,
    grad_ref,
    gsm_ref,
    gm1_ref,
    gm2_ref,
    w1_ref,
    w2_ref,
    trig_ref,
    res_ref,
    xf_ref,
    af_ref,
    pk_ref,
    xs_ref,
    s_ref,
    gf_ref,
    gp_ref,
    gr_ref,
    act_ref,
    slope_ref,
    br_ref,
    mg_ref,
    gin_ref,
    wi_ref,
    w1s_ref,
    w2s_ref,
    w1r_ref,
    w2r_ref,
    wv_ref,
    gw_ref,
    gb_ref,
):
    L = length
    NCH = L // CH
    GP = 544

    slabs = x_ref.shape[0]
    shard = L // slabs
    lanes = lane_low

    def swap(v):
        return pltpu.roll(v, C, 1)

    def rows(i, n=CH):
        return pl.ds(pl.multiple_of(i * n, 16), n)

    def half_sum(v):
        low = lanes(v.shape[0])
        a = jnp.sum(jnp.where(low, v, 0.0), axis=1, keepdims=True)
        b = jnp.sum(jnp.where(low, 0.0, v), axis=1, keepdims=True)
        return jnp.where(low, a, b)

    def fold(v):
        return jnp.sum(v.reshape(v.shape[0] // 8, 8, 128), axis=0)

    raw = [freq_ref[j] for j in range(K)]
    ranks = [sum((raw[j] > raw[k]).astype(jnp.int32) for k in range(K)) for j in range(K)]
    freqs = [
        sum(jnp.where(ranks[j] == k, raw[j], 0) for j in range(K)) for k in range(K)
    ]

    def period(j):
        f = freqs[0]
        for k in range(1, K):
            f = jnp.where(j == k, freqs[k], f)
        return L // f

    s_zero = jnp.zeros((CH, 128), f32)
    for b in range(11):

        @pl.loop(0, NCH)
        def _(i):
            s_ref[b, rows(i), :] = s_zero
            s_ref[b, pl.ds(pl.multiple_of(2 * L + i * CH, 16), CH), :] = s_zero

    for s in range(2):
        for start, stop in ((0, L), (L + 1632, gf_ref.shape[1])):

            @pl.loop(0, (stop - start) // 16)
            def _(i):
                gf_ref[s, pl.ds(pl.multiple_of(start + i * 16, 8), 16), :] = jnp.zeros((16, 128), f32)

    for start, stop in ((0, GP), (GP + L, gp_ref.shape[0])):

        @pl.loop(0, (stop - start) // 16)
        def _(i):
            gp_ref[pl.ds(pl.multiple_of(start + i * 16, 8), 16), :] = jnp.zeros((16, 128), f32)

    pk_ref[0:16, :] = jnp.zeros((16, 128), f32)
    pk_ref[L + 16 : L + 48, :] = jnp.zeros((32, 128), f32)

    r = lax.broadcasted_iota(jnp.int32, (128, 128), 0)
    c = lax.broadcasted_iota(jnp.int32, (128, 128), 1)
    order_ = jnp.where(c == r // 64 * 64 + r % 2 * 32 + r % 64 // 2, 1.0, 0.0).astype(bf16)
    low32 = lanes(32)
    w1s_ref[...] = jnp.zeros((W, W), bf16)
    w2s_ref[...] = jnp.zeros((W, W), bf16)
    cells = [[None] * 11 for _ in range(11)]
    for a in range(11):
        for b in range(11):
            cells[a][b] = (OFFS[b] + HALF) * SPAN + OFFS[a] + HALF

    def cell_rows(block, a, b):
        return slice(int(row_of[block * CELLS + cells[a][b]]) * 32,
                     int(row_of[block * CELLS + cells[a][b]]) * 32 + 32)

    for block, (raw_w, mat) in enumerate(((w1s_ref, w1_ref), (w2s_ref, w2_ref))):
        for a in range(11):
            for q in range(6):
                one = all_ref[cell_rows(block, a, 2 * q), :].astype(f32)
                two = jnp.zeros((32, 128), f32)
                if q < 5:
                    two = all_ref[cell_rows(block, a, 2 * q + 1), :].astype(f32)
                cut = slice(128 * q, 128 * q + 128)
                raw_w[64 * a : 64 * a + 32, cut] = jnp.where(low32, one, swap(two)).astype(bf16)
                raw_w[64 * a + 32 : 64 * a + 64, cut] = jnp.where(low32, swap(one), two).astype(bf16)
        for i in range(6):
            cut = slice(128 * i, 128 * i + 128)
            mat[cut, :] = jnp.dot(order_, raw_w[cut, :], preferred_element_type=f32).astype(bf16)

    for src, cols, rws in ((w1_ref, w1s_ref, w1r_ref), (w2_ref, w2s_ref, w2r_ref)):
        for q in range(6):
            cols[:, 128 * q : 128 * q + 128] = swap(
                src[:, 128 * q : 128 * q + 128].astype(f32)
            ).astype(bf16)
            rws[128 * q : 128 * q + 64, :] = src[128 * q + 64 : 128 * q + 128, :]
            rws[128 * q + 64 : 128 * q + 128, :] = src[128 * q : 128 * q + 64, :]

    gm1_ref[...] = jnp.zeros((W, W), f32)
    gm2_ref[...] = jnp.zeros((W, W), f32)
    gb_ref[...] = jnp.zeros((4, 8, 128), f32)
    gw_ref[...] = jnp.zeros((K, 8, 128), f32)

    first = lax.axis_index("wide") * per
    own = jnp.where(lanes(1), len_ref[first], len_ref[first + 1] if per == 2 else 0)

    def valid(i, n=CH):
        return i * n + lax.broadcasted_iota(jnp.int32, (n, 128), 0) < own

    for z in range(slabs):
        res_ref[shard * z : shard * z + shard, :] = x_ref[z].astype(f32)[0:shard]
        gin_ref[shard * z : shard * z + shard, :] = cot_ref[z].astype(f32)[0:shard]
    lane16 = lax.broadcasted_iota(jnp.int32, (1, 128), 1)
    turn = jnp.zeros((1, 128), jnp.int32)
    for j in range(K):
        turn = jnp.where(lane16 % 8 == j, freqs[j], turn)

    @pl.loop(0, NCH)
    def _(i):
        turns = (i * CH + lax.broadcasted_iota(jnp.int32, (CH, 128), 0)) * turn
        whole = ((turns.astype(f32) + 0.5) * (1.0 / L)).astype(jnp.int32)
        angle = (turns - whole * L).astype(f32) * (2.0 * math.pi / L)
        wave = jnp.where(lane16 < 8, jnp.cos(angle), jnp.sin(angle))
        wave = jnp.where((lane16 < 16) & (lane16 % 8 < K), wave, 0.0)
        hi = wave.astype(bf16).astype(f32)
        mid = (wave - hi).astype(bf16).astype(f32)
        lo = wave - hi - mid
        trig_ref[rows(i), :] = (
            hi + pltpu.roll(mid, 16, 1) + pltpu.roll(lo, 32, 1)
        ).astype(bf16)
        v = jnp.where(valid(i), res_ref[rows(i), :], 0.0)
        mg_ref[rows(i), :] = v
        pk_ref[pl.ds(pl.multiple_of(16 + i * CH, 16), CH), :] = v

    def fill_pairs(dst):
        def step(t0, n):
            a = pk_ref[pl.ds(16 + t0, n), :]
            b = pk_ref[pl.ds(17 + t0, n), :]
            low = lanes(n)
            dst[0, pl.ds(8 + t0, n), :] = jnp.where(low, a, swap(b))
            dst[1, pl.ds(8 + t0, n), :] = jnp.where(low, swap(a), b)

        @pl.loop(0, NCH)
        def _(i):
            step(pl.multiple_of(i * CH, 8) - 8, CH)

        step(L - 8, 16)

    fill_pairs(xf_ref)

    xm = mg_ref[...].astype(bf16)
    spec = lax.dot_general(
        trig_ref[...], xm, (((0,), (0,)), ((), ())), preferred_element_type=f32
    )
    spec = (spec[0:16] + spec[16:32] + spec[32:48]) * (2.0 / L)
    real, imag = spec[0:8], spec[8:16]
    magnitude = jnp.sqrt(real * real + imag * imag + 1.0)
    mean_mag = half_sum(magnitude) * (1.0 / C)
    live = lax.broadcasted_iota(jnp.int32, (8, 128), 0) < K
    top = jnp.max(jnp.where(live, mean_mag, -1e30), axis=0, keepdims=True)
    ex = jnp.where(live, jnp.exp(mean_mag - top), 0.0)
    weights = ex / jnp.sum(ex, axis=0, keepdims=True)
    wv_ref[...] = weights

    def twice(i, first):
        v = small_ref[i : i + 1, :]
        return jnp.where(lanes(1) == first, v, swap(v))

    def fill_within(p):
        inv = 1.0 / jnp.full((CH, 128), p, jnp.int32).astype(f32)
        high = jnp.where(lanes(CH), 0, 1)

        @pl.loop(0, NCH)
        def _(i):
            t = i * CH + lax.broadcasted_iota(jnp.int32, (CH, 128), 0)
            q = ((t.astype(f32) + 0.5) * inv).astype(jnp.int32)
            wi_ref[rows(i), :] = t - q * p + high

    def build_cols(src, p, nk):
        @pl.loop(0, NCH)
        def _(i):
            wi = wi_ref[rows(i), :]
            for q in range(2 * nk):
                base = BASES[q]
                keep = wi >= -base if base < 0 else wi < p - base
                for s in range(2):
                    v = src[s, pl.ds(8 + base + i * CH, CH), :]
                    xs_ref[pl.ds(pl.multiple_of(s * L + i * CH, 16), CH), 128 * q : 128 * q + 128] = (
                        jnp.where(keep, v, 0.0).astype(bf16)
                    )

    RM = L

    def to_slots(get, tiles):
        low = lanes(RM)
        for n in range(tiles):
            d0, d1 = get(n)
            for h in range(2):
                a = d0[:, 128 * h : 128 * h + 128]
                b = d1[:, 128 * h : 128 * h + 128]
                s_ref[4 * n + 2 * h, L : 2 * L, :] = jnp.where(low, a, b)
                if 4 * n + 2 * h + 1 < 11:
                    s_ref[4 * n + 2 * h + 1, L : 2 * L, :] = jnp.where(low, b, a)

    def mm_forward(w_ref, ws_ref, nk, nr):
        def get(n):
            cut = slice(256 * n, 256 * n + 256)
            return (
                jnp.dot(xs_ref[0:L, : 256 * nk], w_ref[: 256 * nk, cut], preferred_element_type=f32),
                jnp.dot(
                    xs_ref[L : 2 * L, : 256 * nk], ws_ref[: 256 * nk, cut], preferred_element_type=f32
                ),
            )

        to_slots(get, nr)

    def mm_adjoint(w_ref, wr_ref, nk, nr):
        dims = (((1,), (1,)), ((), ()))

        def get(n):
            cut = slice(256 * n, 256 * n + 256)
            return (
                lax.dot_general(
                    gr_ref[0:L, : 256 * nr], w_ref[cut, : 256 * nr], dims, preferred_element_type=f32
                ),
                lax.dot_general(
                    gr_ref[L : 2 * L, : 256 * nr],
                    wr_ref[cut, : 256 * nr],
                    dims,
                    preferred_element_type=f32,
                ),
            )

        to_slots(get, nk)

    def mm_weights(gm_ref, nk, nr):
        for n in range(nr):
            cut = slice(256 * n, 256 * n + 256)
            gm_ref[: 256 * nk, cut] += lax.dot_general(
                xs_ref[:, : 256 * nk],
                gr_ref[:, cut],
                (((0,), (0,)), ((), ())),
                preferred_element_type=f32,
            )

    def sum_rows(i, p, nr):
        even = jnp.zeros((CH, 128), f32)
        odd = even
        for b in range(min(4 * nr, 11)):
            off = L + jnp.clip(OFFS[b] * p, -L, L)
            v = s_ref[b, pl.ds(off + i * CH, CH), :]
            if b % 2 == 0:
                even = even + v
            else:
                odd = odd + v
        return even + swap(odd)

    def sum_cols(i, p, nk):
        wi = wi_ref[rows(i), :] - jnp.where(lanes(CH), 0, 1)
        even = jnp.zeros((CH, 128), f32)
        odd = even
        for b in range(min(4 * nk, 11)):
            d = OFFS[b]
            v = s_ref[b, pl.ds(L - d + i * CH, CH), :]
            if d < 0:
                v = jnp.where(wi < p + d, v, 0.0)
            elif d > 0:
                v = jnp.where(wi >= d, v, 0.0)
            if b % 2 == 0:
                even = even + v
            else:
                odd = odd + v
        return even + swap(odd)

    def build_rows(p, nr):
        @pl.loop(0, 17)
        def _(i):
            a = gp_ref[pl.ds(pl.multiple_of(GP + i * CH, 8), CH), :]
            b = gp_ref[pl.ds(GP - p + i * CH, CH), :]
            low = lanes(CH)
            at = pl.ds(pl.multiple_of(L + i * CH, 8), CH)
            gf_ref[0, at, :] = jnp.where(low, a, swap(b))
            gf_ref[1, at, :] = jnp.where(low, swap(a), b)

        @pl.loop(0, NCH)
        def _(i):
            for q in range(2 * nr):
                off = L + jnp.clip(-BASES[q] * p, -L, L + p)
                for s in range(2):
                    v = gf_ref[s, pl.ds(off + i * CH, CH), :]
                    gr_ref[pl.ds(pl.multiple_of(s * L + i * CH, 16), CH), 128 * q : 128 * q + 128] = (
                        v.astype(bf16)
                    )

    def forward(j, nk, nr):
        p = period(j)
        fill_within(p)
        build_cols(xf_ref, p, nk)
        mm_forward(w1_ref, w1s_ref, nk, nr)
        bias_one = twice(0, True)
        bias_two = twice(0, False)

        @pl.loop(0, NCH)
        def _(i):
            h = sum_rows(i, p, nr) + bias_one
            cdf = 0.5 * (1.0 + lax.erf(h * inv_root_two))
            act = (h * cdf).astype(bf16)
            slope_ref[j, rows(i), :] = cdf + h * jnp.exp(-0.5 * h * h) * inv_root_tau
            act_ref[j, rows(i), :] = act
            pk_ref[pl.ds(pl.multiple_of(16 + i * CH, 16), CH), :] = act.astype(f32)

        fill_pairs(af_ref)
        build_cols(af_ref, p, nk)
        mm_forward(w2_ref, w2s_ref, nk, nr)
        wj = wv_ref[pl.ds(j, 1), :]

        @pl.loop(0, NCH)
        def _(i):
            v = sum_rows(i, p, nr) + bias_two
            br_ref[j, rows(i), :] = v
            mg_ref[rows(i), :] += wj * v

    forward(0, 3, 1)

    @pl.loop(1, K - 1)
    def _(j):
        forward(j, 3, 3)

    forward(K - 1, 1, 3)

    same = (
        lax.broadcasted_iota(jnp.int32, (384, 128), 0) % 128 // C
        == lax.broadcasted_iota(jnp.int32, (384, 128), 1) // C
    )
    ones = jnp.where(same, 1.0 / C, 0.0).astype(bf16)

    def half_mean(v):
        a = v.astype(bf16)
        r = v - a.astype(f32)
        b = r.astype(bf16)
        c = (r - b.astype(f32)).astype(bf16)
        return jnp.dot(jnp.concatenate([a, b, c], axis=1), ones, preferred_element_type=f32)

    gain = twice(1, True)
    shift = twice(1, False)
    NB = 352

    @pl.loop(0, L // NB)
    def _(i):
        m = mg_ref[rows(i, NB), :]
        ok = valid(i, NB)
        centered = m - half_mean(m)
        inverse = lax.rsqrt(half_mean(centered * centered) + norm_eps)
        normed = centered * inverse
        res_ref[rows(i, NB), :] = jnp.where(ok, normed * gain + shift, 0.0)
        g_out = jnp.where(ok, gin_ref[rows(i, NB), :], 0.0)
        gb_ref[2] += fold(g_out * normed)
        gb_ref[3] += fold(g_out)
        g_norm = g_out * gain
        gm = inverse * (g_norm - half_mean(g_norm) - normed * half_mean(g_norm * normed))
        mg_ref[rows(i, NB), :] = gm
        gin_ref[rows(i, NB), :] = gm

    def to_slabs(dst):
        for z in range(slabs):
            v = res_ref[shard * z : shard * z + shard, :]
            v = jnp.concatenate([v, jnp.zeros((dst.shape[1] - shard, 128), f32)], axis=0)
            dst[z] = v.astype(bf16)

    to_slabs(out_ref)

    def backward(j, nk, nr):
        p = period(j)
        fill_within(p)
        wj = wv_ref[pl.ds(j, 1), :]

        @pl.loop(0, NCH)
        def _(i):
            gm = mg_ref[rows(i), :]
            gw_ref[j] += fold(gm * br_ref[j, rows(i), :])
            g = (wj * gm).astype(bf16).astype(f32)
            gb_ref[1] += fold(g)
            gp_ref[pl.ds(pl.multiple_of(GP + i * CH, 8), CH), :] = g
            pk_ref[pl.ds(pl.multiple_of(16 + i * CH, 16), CH), :] = act_ref[j, rows(i), :].astype(f32)

        build_rows(p, nr)
        mm_adjoint(w2_ref, w2r_ref, nk, nr)
        fill_pairs(af_ref)
        build_cols(af_ref, p, nk)
        mm_weights(gm2_ref, nk, nr)

        @pl.loop(0, NCH)
        def _(i):
            g = (sum_cols(i, p, nk) * slope_ref[j, rows(i), :]).astype(bf16).astype(f32)
            gb_ref[0] += fold(g)
            gp_ref[pl.ds(pl.multiple_of(GP + i * CH, 8), CH), :] = g

        build_rows(p, nr)
        mm_adjoint(w1_ref, w1r_ref, nk, nr)
        build_cols(xf_ref, p, nk)
        mm_weights(gm1_ref, nk, nr)

        @pl.loop(0, NCH)
        def _(i):
            gin_ref[rows(i), :] += sum_cols(i, p, nk)

    backward(0, 3, 1)

    @pl.loop(1, K - 1)
    def _(j):
        backward(j, 3, 3)

    backward(K - 1, 1, 3)

    row8 = lax.broadcasted_iota(jnp.int32, (8, 128), 0)
    g_weights = jnp.zeros((8, 128), f32)
    for j in range(K):
        total = jnp.sum(gw_ref[j], axis=0, keepdims=True)
        g_weights = jnp.where(row8 == j, total, g_weights)
    g_weights = half_sum(g_weights)
    weights = wv_ref[...]
    g_score = weights * (g_weights - jnp.sum(weights * g_weights, axis=0, keepdims=True))
    coeff = g_score / (magnitude * C) * (2.0 / L)
    coef = jnp.concatenate([coeff * real, coeff * imag], axis=0)
    c_hi = coef.astype(bf16)
    c_lo = (coef - c_hi.astype(f32)).astype(bf16)
    c_all = jnp.concatenate([c_hi, c_hi, c_hi, jnp.zeros((80, 128), bf16)], axis=0)
    c_lo = jnp.concatenate([c_lo, jnp.zeros((112, 128), bf16)], axis=0)

    @pl.loop(0, L // NB)
    def _(i):
        t = trig_ref[rows(i, NB), :]
        g = (
            gin_ref[rows(i, NB), :]
            + jnp.dot(t, c_all, preferred_element_type=f32)
            + jnp.dot(t, c_lo, preferred_element_type=f32)
        )
        res_ref[rows(i, NB), :] = jnp.where(valid(i, NB), g, 0.0)

    to_slabs(gser_ref)

    sums = []
    for q in range(4):
        total = jnp.sum(gb_ref[q], axis=0, keepdims=True)
        sums.append(total + swap(total))
    low = lanes(1)
    gsm_ref[0:1, :] = jnp.where(low, sums[0], sums[1])
    gsm_ref[1:2, :] = jnp.where(low, sums[2], sums[3])

    used = set(int(v) for v in row_of)
    for v in range(grad_ref.shape[0] // 32):
        if v not in used:
            grad_ref[32 * v : 32 * v + 32, :] = jnp.zeros((32, 128), f32)
    back = jnp.where(r == c // 64 * 64 + c % 2 * 32 + c % 64 // 2, 1.0, 0.0).astype(bf16)
    back = jnp.concatenate([back, back, back], axis=1)
    for block, mat in enumerate((gm1_ref, gm2_ref)):
        for i in range(6):
            v = mat[128 * i : 128 * i + 128, :]
            hi = v.astype(bf16)
            rest = v - hi.astype(f32)
            mid = rest.astype(bf16)
            lo = (rest - mid.astype(f32)).astype(bf16)
            v = jnp.dot(back, jnp.concatenate([hi, mid, lo], axis=0), preferred_element_type=f32)
            for a in (2 * i, 2 * i + 1):
                if a == 11:
                    continue
                top = 64 * (a % 2)
                for q in range(6):
                    even = v[top : top + 32, 128 * q : 128 * q + 128]
                    odd = v[top + 32 : top + 64, 128 * q : 128 * q + 128]
                    grad_ref[cell_rows(block, a, 2 * q), :] = jnp.where(low32, even, swap(odd))
                    if q < 5:
                        grad_ref[cell_rows(block, a, 2 * q + 1), :] = jnp.where(
                            low32, swap(even), odd
                        )


vm = pl.BlockSpec(memory_space=pltpu.VMEM)
sm = pl.BlockSpec(memory_space=pltpu.SMEM)
sds = jax.ShapeDtypeStruct


def run_block(x, cot, lens, freqs, cells, small, per, row_of, L):
    return pl.pallas_call(
        functools.partial(block_kernel, L, per, row_of),
        out_shape=(
            sds(x.shape, bf16),
            sds(x.shape, bf16),
            sds(cells.shape, f32),
            sds((2, 128), f32),
        ),
        in_specs=[sm, sm, vm, vm, vm, vm],
        out_specs=(vm,) * 4,
        scratch_shapes=[
            pltpu.VMEM((W, W), f32),
            pltpu.VMEM((W, W), f32),
            pltpu.VMEM((W, W), bf16),
            pltpu.VMEM((W, W), bf16),
            pltpu.VMEM((L, 128), bf16),
            pltpu.VMEM((L, 128), f32),
            pltpu.VMEM((2, L + 16, 128), f32),
            pltpu.VMEM((2, L + 16, 128), f32),
            pltpu.VMEM((L + 48, 128), f32),
            pltpu.VMEM((2 * L, W), bf16),
            pltpu.VMEM((11, 3 * L, 128), f32),
            pltpu.VMEM((2, 3552, 128), f32),
            pltpu.VMEM((544 + L + 576, 128), f32),
            pltpu.VMEM((2 * L, W), bf16),
            pltpu.VMEM((K, L, 128), bf16),
            pltpu.VMEM((K, L, 128), f32),
            pltpu.VMEM((K, L, 128), f32),
            pltpu.VMEM((L, 128), f32),
            pltpu.VMEM((L, 128), f32),
            pltpu.VMEM((L, 128), jnp.int32),
            pltpu.VMEM((W, W), bf16),
            pltpu.VMEM((W, W), bf16),
            pltpu.VMEM((W, W), bf16),
            pltpu.VMEM((W, W), bf16),
            pltpu.VMEM((8, 128), f32),
            pltpu.VMEM((K, 8, 128), f32),
            pltpu.VMEM((4, 8, 128), f32),
        ],
        compiler_params=pltpu.CompilerParams(vmem_limit_bytes=62 << 20),
        name="block",
    )(freqs, lens, x, cot, cells, small)


def adam_update(param, grad, first, second):
    first_new = beta_one * first + (1.0 - beta_one) * grad
    second_new = beta_two * second + (1.0 - beta_two) * grad * grad
    first_hat = first_new / (1.0 - beta_one**STEP)
    second_hat = second_new / (1.0 - beta_two**STEP)
    param_new = param - learn_rate * (
        first_hat / (jnp.sqrt(second_hat) + adam_eps) + weight_decay * param
    )
    return (param_new, first_new, second_new)


def local(series, lengths, freqs, cotangent, kernels, kernel_m, kernel_v, small, small_m, small_v):
    wide = lax.axis_size("wide")
    batch = lax.axis_size("batch")
    count = wide * batch
    half, sides = count // 2, math.isqrt(batch // 2)
    me = lax.axis_index(("wide", "batch"))
    span, room, deep, spread, pick, weight, row_of = plan(count)
    share = kernels.shape[0]
    shard = series.shape[1]
    per = series.shape[0] // wide
    slab = -(-shard // 16) * 16

    def mine(table):
        return lax.dynamic_index_in_dim(jnp.asarray(table), me, 0, keepdims=False)

    spread_me, pick_me, weight_me = mine(spread), mine(pick), mine(weight)
    aligned = share % 128 == 0
    lead = me * share % TAP

    def to_rows(v):
        if aligned:
            return v.reshape(share // 128, 128)
        wide_v = jnp.zeros((span * TAP,), f32)
        return lax.dynamic_update_slice_in_dim(wide_v, v, lead, 0).reshape(span * 32, 128)

    def from_rows(v):
        if aligned:
            return v.reshape(share)
        return lax.dynamic_slice_in_dim(v.reshape(-1), lead, share, 0)

    lead_step = share // 128 if aligned else 0
    params = pltpu.CompilerParams
    static = (wide, batch, lead_step, span, room, deep, per)
    dma = pltpu.SemaphoreType.DMA
    cell_shape = (wide, sides, sides, 2, room * 32, 128)
    slab_shape = (wide, slab, 128)
    exchange = (half, deep, 32, 128)
    taps_rows = -(-(span * 32 + 32) // 8) * 8
    taps = to_rows(kernels)
    held = taps.shape[0]

    x, cot, cells = pl.pallas_call(
        functools.partial(gather_kernel, *static),
        out_shape=(sds(slab_shape, bf16), sds(slab_shape, bf16), sds(cell_shape, bf16)),
        in_specs=[sm, sm, vm, vm, vm],
        out_specs=(vm,) * 3,
        scratch_shapes=[
            pltpu.VMEM((taps_rows, 128), f32),
            pltpu.VMEM(exchange, f32),
            pltpu.VMEM(exchange, f32),
            pltpu.VMEM(slab_shape, bf16),
            pltpu.VMEM(slab_shape, bf16),
            dma((2, half - 1)),
            dma((2, wide - 1)),
            dma((2, wide - 1)),
            dma((2, wide - 1)),
            dma((2, 2 * (sides - 1))),
            dma((2, 2 * (sides - 1))),
            dma((2, 1)),
        ],
        compiler_params=params(
            collective_id=0, has_side_effects=True, vmem_limit_bytes=48 << 20
        ),
        name="gather",
    )(spread_me, pick_me, taps, series, cotangent)

    small_rows = small.reshape(2, 128)
    out, gser, grads, gsm = run_block(
        x, cot, lengths, freqs, cells.reshape(-1, 128), small_rows, per, row_of, shard * wide
    )

    link = f32
    cut = room * 16
    results = pl.pallas_call(
        functools.partial(reduce_kernel, *static),
        out_shape=(
            sds(series.shape, bf16),
            sds(series.shape, bf16),
            sds((1, 1), f32),
            sds((held, 128), f32),
            sds((held, 128), f32),
            sds((held, 128), f32),
            sds((2, 128), f32),
            sds((2, 128), f32),
            sds((2, 128), f32),
        ),
        in_specs=[sm, sm, sm] + [vm] * 10,
        out_specs=(vm,) * 9,
        scratch_shapes=[
            pltpu.VMEM(slab_shape, bf16),
            pltpu.VMEM(slab_shape, bf16),
            pltpu.VMEM((wide, sides, sides, room * 32, 128), link),
            pltpu.VMEM((wide, sides, sides, room * 32, 128), link),
            pltpu.VMEM((wide, sides, sides, room * 32, 128), f32),
            pltpu.VMEM((sides - 1, wide, sides, cut, 128), link),
            pltpu.VMEM((sides - 1, wide, sides, cut, 128), link),
            pltpu.VMEM((sides - 1, wide, sides, cut, 128), link),
            pltpu.VMEM((sides - 1, wide, sides, cut, 128), link),
            pltpu.VMEM((wide, sides, cut, 128), f32),
            pltpu.VMEM((wide, sides, cut, 128), f32),
            pltpu.VMEM((sides - 1, wide, cut, 128), link),
            pltpu.VMEM((sides - 1, wide, cut, 128), link),
            pltpu.VMEM((sides - 1, wide, cut, 128), link),
            pltpu.VMEM((sides - 1, wide, cut, 128), link),
            pltpu.VMEM((wide, room * 32, 128), f32),
            pltpu.VMEM((wide - 1, room * 32, 128), f32),
            pltpu.VMEM((room * 32, 128), f32),
            pltpu.VMEM(exchange, f32),
            pltpu.VMEM(exchange, f32),
            pltpu.VMEM((8, 128), f32),
            pltpu.VMEM((count, 8, 128), f32),
            pltpu.VMEM((taps_rows, 128), f32),
            dma((2, 1)),
            dma((2, 2 * (sides - 1))),
            dma((2, 2 * (sides - 1))),
            dma((2, wide - 1)),
            dma((2, wide - 1)),
            dma((2, wide - 1)),
            dma((2, half - 1)),
            dma((2, count - 1)),
        ],
        compiler_params=params(
            collective_id=1, has_side_effects=True, vmem_limit_bytes=60 << 20
        ),
        name="reduce",
    )(
        spread_me,
        pick_me,
        weight_me,
        grads.reshape(cell_shape),
        gsm,
        out,
        gser,
        taps,
        to_rows(kernel_m),
        to_rows(kernel_v),
        small_rows,
        small_m.reshape(2, 128),
        small_v.reshape(2, 128),
    )
    out, gser, norm, new_w, new_m, new_v, new_sw, new_sm, new_sv = results
    return (
        out,
        gser,
        norm.reshape(()),
        from_rows(new_w),
        from_rows(new_m),
        from_rows(new_v),
        new_sw.reshape(-1),
        new_sm.reshape(-1),
        new_sv.reshape(-1),
    )


def solution(mesh):
    placed = (
        P("batch", "wide", None),
        P("batch"),
        P(),
        P("batch", "wide", None),
        P(("wide", "batch")),
        P(("wide", "batch")),
        P(("wide", "batch")),
        P(),
        P(),
        P(),
    )
    return jax.shard_map(
        local,
        mesh=mesh,
        in_specs=placed,
        out_specs=(
            P("batch", "wide", None),
            P("batch", "wide", None),
            P(),
            P(("wide", "batch")),
            P(("wide", "batch")),
            P(("wide", "batch")),
            P(),
            P(),
            P(),
        ),
        check_vma=False,
    )
```

```python
import functools
import math

import jax
import jax.numpy as jnp
import numpy as np
from jax import lax
from jax.experimental import pallas as pl
from jax.experimental.pallas import tpu as pltpu
from jax.sharding import PartitionSpec as P

C = 64
K = 5
NKER = 6
STEP = 10
SPAN = 11
HALF = 5
TAPS = 286
CELLS = SPAN * SPAN
TAP = C * C
DEEP_STEPS = 1

beta_one = 0.9
beta_two = 0.999
learn_rate = 0.1
weight_decay = 0.01
adam_eps = 1e-08
clip_norm = 1.0
norm_eps = 1e-05
inv_root_two = 1.0 / math.sqrt(2.0)
inv_root_tau = 1.0 / math.sqrt(2.0 * math.pi)

bf16 = jnp.bfloat16
f32 = jnp.float32
precise = lax.Precision.HIGHEST

OFFS = (-1, 0, 1, 2, -3, -2, 3, 4, -5, -4, 5, 6)
BASES = (-1, 1, -3, 3, -5, 5)
W = 12 * C


def tap_cells():
    cells = []
    for block in range(2):
        for kernel in range(NKER):
            for row_off in range(-kernel, kernel + 1):
                for col_off in range(-kernel, kernel + 1):
                    cells.append(block * CELLS + (row_off + HALF) * SPAN + col_off + HALF)
    return np.array(cells)


def is_deep(same_plane, step, batch):
    return same_plane or step % batch < DEEP_STEPS


@functools.lru_cache(None)
def plan(wide, batch):
    cells = tap_cells()
    count = wide * batch
    half = count // 2
    share = cells.size * TAP // count
    holds = [
        range(share * d // TAP, (share * (d + 1) - 1) // TAP + 1) for d in range(count)
    ]
    span = max(len(taps) for taps in holds)
    needs = [sorted(set(cells[taps.start : taps.stop].tolist())) for taps in holds]
    room = -(-CELLS // half)
    deep = 1 if max(len(need) for need in needs) <= 4 else 2
    users = [[d for d in range(count) if cell in needs[d]] for cell in range(2 * CELLS)]
    order = sorted(range(2 * CELLS), key=lambda cell: -len(users[cell]))
    for seed in range(1000):
        rng = np.random.RandomState(seed)
        owner = np.full(2 * CELLS, -1)
        filled = np.zeros(count, int)
        between = np.zeros((count, count), int)
        for cell in order:
            first = cell // CELLS * half
            free = [
                o
                for o in range(first, first + half)
                if filled[o] < room and all(
                    between[d, o] < (deep if is_deep(d // batch == o // batch, o - d, batch) else 1)
                    for d in users[cell]
                )
            ]
            if not free:
                break
            cost = [(sum(between[d, o] for d in users[cell]), filled[o]) for o in free]
            least = min(cost)
            free = [o for o, c in zip(free, cost) if c == least]
            o = free[rng.randint(len(free))]
            owner[cell] = o
            filled[o] += 1
            for d in users[cell]:
                between[d, o] += 1
        else:
            break
    place = np.zeros(2 * CELLS, int)
    filled[:] = 0
    for cell in range(2 * CELLS):
        place[cell] = filled[owner[cell]]
        filled[owner[cell]] += 1
    spread = np.zeros((count, half * deep, span), np.float32)
    pick = np.zeros((count, room, half * deep), np.float32)
    between[:] = 0
    for d, taps in enumerate(holds):
        for cell in needs[d]:
            o = owner[cell]
            slot = between[d, o]
            between[d, o] += 1
            pick[o, place[cell], d % half * deep + slot] = 1.0
            for tap in taps:
                if cells[tap] == cell:
                    spread[d, o % half * deep + slot, tap - taps.start] = 1.0
    weight = np.zeros((count, room), np.float32)
    for cell in range(2 * CELLS):
        row, col = divmod(cell % CELLS, SPAN)
        weight[owner[cell], place[cell]] = NKER - max(abs(row - HALF), abs(col - HALF))
    row_of = owner * room + place
    return span, room, deep, spread, pick, weight, row_of


MESH = pl.DeviceIdType.MESH


class Place:
    def __init__(self, wide, batch):
        self.nz, self.nb = wide, batch
        self.ns = math.isqrt(batch // 2)
        self.z = lax.axis_index("wide")
        self.b = lax.axis_index("batch")
        self.core = lax.rem(self.b, 2)
        self.x = lax.rem(self.b // 2, self.ns)
        self.y = self.b // (2 * self.ns)
        self.half = wide * batch // 2
        self.me = self.z * batch + self.b
        self.mine = lax.rem(self.me, self.half)

    def batch_of(self, y, x, core):
        return (y * self.ns + x) * 2 + core

    def at_z(self, d):
        return (lax.rem(self.z + d, self.nz), self.b)

    def at_y(self, d):
        return (self.z, self.batch_of(lax.rem(self.y + d, self.ns), self.x, self.core))

    def at_x(self, d):
        return (self.z, self.batch_of(self.y, lax.rem(self.x + d, self.ns), self.core))

    def sibling(self):
        return (self.z, self.batch_of(self.y, self.x, 1 - self.core))

    def in_half(self, dz, db):
        planes = self.nz // 2
        first = self.z // planes * planes
        z = lax.rem(self.z - first + dz, planes)
        b = lax.rem(self.b + db, self.nb)
        return z * self.nb + b, (first + z, b)

    def half_steps(self):
        return [
            (dz, db) for dz in range(self.nz // 2) for db in range(self.nb) if (dz, db) != (0, 0)
        ]

    def at_all(self, d):
        other = lax.rem(self.me + d, self.nz * self.nb)
        return (other // self.nb, lax.rem(other, self.nb))


def greet(peers):
    barrier = pltpu.get_barrier_semaphore()
    for peer in peers:
        pl.semaphore_signal(barrier, inc=1, device_id=peer, device_id_type=MESH)
    pl.semaphore_wait(barrier, len(peers))


def send(src, dst, sems, k, peer):
    copy = pltpu.make_async_remote_copy(
        src_ref=src,
        dst_ref=dst,
        send_sem=sems.at[0, k],
        recv_sem=sems.at[1, k],
        device_id=peer,
        device_id_type=MESH,
    )
    copy.start()
    return copy


def swap_cells(at, deep, way, src, dst, sems):
    copies = []
    for k, (dz, db) in enumerate(at.half_steps()):
        index, peer = at.in_half(dz, db)
        keep = pl.ds(0, deep if is_deep(dz == 0, way * db, at.nb) else 1)
        copies.append(send(src.at[index, keep], dst.at[at.mine, keep], sems, k, peer))
    dst[at.mine] = src[at.mine]
    return copies


def lane_low(rows):
    return lax.broadcasted_iota(jnp.int32, (rows, 128), 1) < C


def gather_kernel(
    wide,
    batch,
    lead_step,
    span,
    room,
    deep,
    per,
    table_ref,
    taps_ref,
    series_ref,
    cot_ref,
    x_ref,
    c_ref,
    all_ref,
    tap_ref,
    slot_ref,
    got_ref,
    xs_ref,
    cs_ref,
    tap_sem,
    x_sem,
    c_sem,
    z_sem,
    a_sem,
    b_sem,
    core_sem,
):
    at = Place(wide, batch)
    nz, ns, half = at.nz, at.ns, at.half
    shard = series_ref.shape[2]
    pad = x_ref.shape[1] - shard
    held = taps_ref.shape[0]
    got_ref[...] = jnp.zeros(got_ref.shape, f32)
    tap_ref[...] = jnp.zeros(tap_ref.shape, f32)
    tap_ref[pl.ds(lax.rem(at.me * lead_step, 32), held), :] = taps_ref[...]

    @pl.loop(0, half)
    def _(o):
        for s in range(deep):
            total = jnp.zeros((32, 128), f32)
            for t in range(span):
                total = total + (
                    table_ref[(o * deep + s) * span + t] * tap_ref[32 * t : 32 * t + 32, :]
                )
            slot_ref[o, s] = total

    greet(
        [at.in_half(*step)[1] for step in at.half_steps()] + [at.at_z(d) for d in range(1, nz)]
    )

    taps = swap_cells(at, deep, 1, slot_ref, got_ref, tap_sem)

    def pack(src, keep):
        for z in range(nz):
            first = src[per * z].astype(f32)
            second = src[per * z + 1].astype(f32) if per == 2 else jnp.zeros_like(first)
            both = jnp.concatenate([first, second], axis=0).T
            both = jnp.concatenate([both, jnp.zeros((pad, 128), f32)], axis=0)
            keep[z] = both.astype(bf16)

    waits = []

    def exchange(keep, out, sems):
        for d in range(1, nz):
            waits.append(send(keep.at[lax.rem(at.z + d, nz)], out.at[at.z], sems, d - 1, at.at_z(d)))
        out[at.z] = keep[at.z]

    pack(series_ref, xs_ref)
    pack(cot_ref, cs_ref)

    for copy in taps:
        copy.wait_recv()

    picks = half * deep * span
    for k in range(room):
        total = jnp.zeros((32, 128), f32)

        def add(q, total):
            for s in range(deep):
                total = total + table_ref[picks + k * half * deep + q * deep + s] * got_ref[q, s]
            return total

        total = lax.fori_loop(0, half, add, total)
        all_ref[at.z, at.y, at.x, at.core, 32 * k : 32 * k + 32, :] = (
            total * (1.0 / NKER)
        ).astype(bf16)

    cut = room * 32 // 2
    low, high = pl.ds(0, cut), pl.ds(cut, cut)
    block = all_ref.at[at.z, at.y, at.x, at.core]
    stage = [send(block, block, z_sem, d - 1, at.at_z(d)) for d in range(1, nz)]

    def to_sibling(part):
        waits.append(send(part, part, core_sem, len(waits), at.sibling()))

    for copy in stage:
        copy.wait()
    stage = []
    for d in range(1, ns):
        part = all_ref.at[:, at.y, at.x, at.core, low]
        stage.append(send(part, part, a_sem, d - 1, at.at_y(d)))
        part = all_ref.at[:, at.y, at.x, at.core, high]
        stage.append(send(part, part, b_sem, d - 1, at.at_x(d)))
    to_sibling(all_ref.at[:, at.y, at.x, at.core])
    for copy in stage:
        copy.wait()
    stage = []
    for d in range(1, ns):
        part = all_ref.at[:, :, at.x, at.core, low]
        stage.append(send(part, part, a_sem, ns + d - 2, at.at_x(d)))
        part = all_ref.at[:, at.y, :, at.core, high]
        stage.append(send(part, part, b_sem, ns + d - 2, at.at_y(d)))
    for d in range(1, ns):
        to_sibling(all_ref.at[:, lax.rem(at.y + d, ns), at.x, at.core, low])
        to_sibling(all_ref.at[:, at.y, lax.rem(at.x + d, ns), at.core, high])
    exchange(xs_ref, x_ref, x_sem)
    exchange(cs_ref, c_ref, c_sem)
    for copy in stage:
        copy.wait()
    late = []
    for d in range(1, ns):
        k = 2 * (ns - 1) + 1 + 2 * (d - 1)
        part = all_ref.at[:, :, lax.rem(at.x + d, ns), at.core, low]
        late.append(send(part, part, core_sem, k, at.sibling()))
        part = all_ref.at[:, lax.rem(at.y + d, ns), :, at.core, high]
        late.append(send(part, part, core_sem, k + 1, at.sibling()))
    for copy in waits + late:
        copy.wait()
    for copy in taps:
        copy.wait_send()


def reduce_kernel(
    wide,
    batch,
    lead_step,
    span,
    room,
    deep,
    per,
    table_ref,
    grad_ref,
    gsm_ref,
    o_ref,
    g_ref,
    oz_ref,
    gz_ref,
    share_ref,
    total_ref,
    send_ref,
    core_ref,
    acc_ref,
    sa_ref,
    sb_ref,
    ra_ref,
    rb_ref,
    a_ref,
    b_ref,
    sa2_ref,
    sb2_ref,
    ra2_ref,
    rb2_ref,
    own_ref,
    sz_ref,
    rz_ref,
    sum_ref,
    back_ref,
    got_ref,
    tile_ref,
    tiles_ref,
    tap_ref,
    core_sem,
    a_sem,
    b_sem,
    z_sem,
    o_sem,
    g_sem,
    tap_sem,
    all_sem,
):
    at = Place(wide, batch)
    nz, ns, half = at.nz, at.ns, at.half
    count = nz * at.nb
    cut = room * 32 // 2
    link = send_ref.dtype
    got_ref[...] = jnp.zeros(got_ref.shape, f32)

    for z in range(nz):
        send_ref[z] = grad_ref[z, :, :, 1 - at.core].astype(link)
    greet([at.at_all(d) for d in range(1, count)])
    core_copy = send(send_ref, core_ref, core_sem, 0, at.sibling())

    waits = []
    for src, dst, sems in ((o_ref, oz_ref, o_sem), (g_ref, gz_ref, g_sem)):
        for d in range(1, nz):
            waits.append(send(src.at[lax.rem(at.z + d, nz)], dst.at[at.z], sems, d - 1, at.at_z(d)))
        dst[at.z] = src[at.z]

    core_copy.wait()
    for z in range(nz):
        acc_ref[z] = grad_ref[z, :, :, at.core] + core_ref[z].astype(f32)

    stage = []
    for d in range(1, ns):
        x = lax.rem(at.x + d, ns)
        y = lax.rem(at.y + d, ns)
        for z in range(nz):
            for o in range(ns):
                sa_ref[d - 1, z, o] = acc_ref[z, o, x, 0:cut, :].astype(link)
                sb_ref[d - 1, z, o] = acc_ref[z, y, o, cut : 2 * cut, :].astype(link)
        stage.append(send(sa_ref.at[d - 1], ra_ref.at[d - 1], a_sem, d - 1, at.at_x(d)))
        stage.append(send(sb_ref.at[d - 1], rb_ref.at[d - 1], b_sem, d - 1, at.at_y(d)))
    for copy in stage:
        copy.wait()
    for z in range(nz):
        for o in range(ns):
            va = acc_ref[z, o, at.x, 0:cut, :]
            vb = acc_ref[z, at.y, o, cut : 2 * cut, :]
            for d in range(1, ns):
                va = va + ra_ref[d - 1, z, o].astype(f32)
                vb = vb + rb_ref[d - 1, z, o].astype(f32)
            a_ref[z, o] = va
            b_ref[z, o] = vb
    stage = []
    for d in range(1, ns):
        x = lax.rem(at.x + d, ns)
        y = lax.rem(at.y + d, ns)
        for z in range(nz):
            sa2_ref[d - 1, z] = a_ref[z, y].astype(link)
            sb2_ref[d - 1, z] = b_ref[z, x].astype(link)
        stage.append(send(sa2_ref.at[d - 1], ra2_ref.at[d - 1], a_sem, ns + d - 2, at.at_y(d)))
        stage.append(send(sb2_ref.at[d - 1], rb2_ref.at[d - 1], b_sem, ns + d - 2, at.at_x(d)))
    for copy in stage:
        copy.wait()
    for z in range(nz):
        va = a_ref[z, at.y]
        vb = b_ref[z, at.x]
        for d in range(1, ns):
            va = va + ra2_ref[d - 1, z].astype(f32)
            vb = vb + rb2_ref[d - 1, z].astype(f32)
        own_ref[z, 0:cut, :] = va
        own_ref[z, cut : 2 * cut, :] = vb
        sz_ref[z, 0:cut, :] = va.astype(link)
        sz_ref[z, cut : 2 * cut, :] = vb.astype(link)
    stage = [
        send(sz_ref.at[lax.rem(at.z + d, nz)], rz_ref.at[d - 1], z_sem, d - 1, at.at_z(d))
        for d in range(1, nz)
    ]
    for copy in stage:
        copy.wait()
    total = own_ref[at.z]
    for d in range(1, nz):
        total = total + rz_ref[d - 1].astype(f32)
    sum_ref[...] = total * (1.0 / NKER)

    picks = half * deep * span
    weights = picks + room * half * deep
    square = jnp.zeros((1, 128), f32)
    for k in range(room):
        value = sum_ref[32 * k : 32 * k + 32, :]
        square = square + table_ref[weights + k] * jnp.sum(value * value, axis=0, keepdims=True)
    tile_ref[0:2, :] = gsm_ref[...]
    tile_ref[2:3, :] = square
    tile_ref[3:8, :] = jnp.zeros((5, 128), f32)
    tells = [
        send(tile_ref, tiles_ref.at[at.me], all_sem, d - 1, at.at_all(d)) for d in range(1, count)
    ]
    tiles_ref[at.me] = tile_ref[...]

    @pl.loop(0, half)
    def _(q):
        for s in range(deep):
            value = jnp.zeros((32, 128), f32)
            for k in range(room):
                value = value + (
                    table_ref[picks + k * half * deep + q * deep + s]
                    * sum_ref[32 * k : 32 * k + 32, :]
                )
            back_ref[q, s] = value

    backs = swap_cells(at, deep, -1, back_ref, got_ref, tap_sem)
    for copy in tells:
        copy.wait()
    tile = jnp.zeros((8, 128), f32)
    for d in range(count):
        tile = tile + tiles_ref[d]
    total_ref[...] = tile
    for copy in backs:
        copy.wait()

    @pl.loop(0, span)
    def _(t):
        value = jnp.zeros((32, 128), f32)
        for q in range(half):
            for s in range(deep):
                value = value + table_ref[(q * deep + s) * span + t] * got_ref[q, s]
        tap_ref[pl.ds(pl.multiple_of(32 * t, 32), 32), :] = value

    held = share_ref.shape[0]
    share_ref[...] = tap_ref[pl.ds(lax.rem(at.me * lead_step, 32), held), :]
    for copy in waits:
        copy.wait()


def finish_kernel(
    per,
    total_ref,
    share_ref,
    o_ref,
    g_ref,
    w_ref,
    m_ref,
    v_ref,
    sw_ref,
    sm_ref,
    sv_ref,
    out_ref,
    gser_ref,
    norm_ref,
    nw_ref,
    nm_ref,
    nv_ref,
    nsw_ref,
    nsm_ref,
    nsv_ref,
):
    small = total_ref[0:2, :]
    lanes = jnp.sum(total_ref[2:3, :], axis=1, keepdims=True)
    squares = jnp.sum(jnp.sum(small * small, axis=0, keepdims=True), axis=1, keepdims=True)
    norm = jnp.sqrt(lanes + squares)
    norm_ref[...] = norm
    factor = jnp.minimum(1.0, clip_norm / (norm + 1e-06))
    nsw_ref[...], nsm_ref[...], nsv_ref[...] = adam_update(
        sw_ref[...], small * factor, sm_ref[...], sv_ref[...]
    )
    nw_ref[...], nm_ref[...], nv_ref[...] = adam_update(
        w_ref[...], share_ref[...] * factor, m_ref[...], v_ref[...]
    )
    shard = out_ref.shape[2]
    for src, dst in ((o_ref, out_ref), (g_ref, gser_ref)):
        for z in range(src.shape[0]):
            both = src[z].astype(f32).T
            dst[per * z] = both[0:C, 0:shard].astype(bf16)
            if per == 2:
                dst[per * z + 1] = both[C:, 0:shard].astype(bf16)


def block_kernel(
    L,
    per,
    row_of,
    freq_ref,
    len_ref,
    x_ref,
    cot_ref,
    all_ref,
    small_ref,
    out_ref,
    gser_ref,
    grad_ref,
    gsm_ref,
    gm1_ref,
    gm2_ref,
    w1_ref,
    w2_ref,
    w1s_ref,
    w2s_ref,
    w1r_ref,
    w2r_ref,
    trig_ref,
    res_ref,
    mg_ref,
    gin_ref,
    xf_ref,
    af_ref,
    pk_ref,
    xs_ref,
    as_ref,
    s1_ref,
    s2_ref,
    p2_ref,
    p1_ref,
    r1_ref,
    r2_ref,
    act_ref,
    slope_ref,
    br_ref,
    wv_ref,
    gw_ref,
    gb_ref,
):
    slabs = x_ref.shape[0]
    shard = L // slabs
    lanes = lane_low
    third = L // 3
    PS, PP, PK = 88, 176, 16

    def swap(v):
        return pltpu.roll(v, C, 1)

    def span_of(t, n, align=8):
        return pl.ds(pl.multiple_of(t, align), n)

    def half_sum(v):
        low = lanes(v.shape[0])
        a = jnp.sum(jnp.where(low, v, 0.0), axis=1, keepdims=True)
        b = jnp.sum(jnp.where(low, 0.0, v), axis=1, keepdims=True)
        return jnp.where(low, a, b)

    def fold(v):
        return jnp.sum(v.reshape(v.shape[0] // 8, 8, 128), axis=0)

    def split(v):
        hi = v.astype(bf16)
        rest = v - hi.astype(f32)
        mid = rest.astype(bf16)
        return hi, mid, (rest - mid.astype(f32)).astype(bf16)

    raw = [freq_ref[j] for j in range(K)]
    ranks = [sum((raw[j] > raw[k]).astype(jnp.int32) for k in range(K)) for j in range(K)]
    freqs = [sum(jnp.where(ranks[j] == k, raw[j], 0) for j in range(K)) for k in range(K)]
    order = (1, 2, 3, 0, 4)
    periods = [L // freqs[j] for j in order]
    freqs = [freqs[j] for j in order]
    tiles = [(3, 3), (3, 3), (3, 3), (3, 1), (1, 3)]

    for ref, pad in ((s1_ref, PS), (s2_ref, PS), (p1_ref, PP), (p2_ref, PP)):
        for b in range(ref.shape[0]):
            ref[b, 0:pad, :] = jnp.zeros((pad, 128), f32)
            ref[b, L + pad : L + 2 * pad, :] = jnp.zeros((pad, 128), f32)
    pk_ref[0:PK, :] = jnp.zeros((PK, 128), f32)
    pk_ref[L + PK : L + 2 * PK, :] = jnp.zeros((PK, 128), f32)
    gm1_ref[...] = jnp.zeros((W, W), f32)
    gm2_ref[...] = jnp.zeros((W, W), f32)
    gb_ref[...] = jnp.zeros((4, 8, 128), f32)
    gw_ref[...] = jnp.zeros((K, 8, 128), f32)

    r = lax.broadcasted_iota(jnp.int32, (128, 128), 0)
    c = lax.broadcasted_iota(jnp.int32, (128, 128), 1)
    ahead = jnp.where(c == r // 64 * 64 + r % 2 * 32 + r % 64 // 2, 1.0, 0.0).astype(bf16)
    low32 = lanes(32)

    def cell_rows(block, a, b):
        cell = block * CELLS + (OFFS[b] + HALF) * SPAN + OFFS[a] + HALF
        return slice(int(row_of[cell]) * 32, int(row_of[cell]) * 32 + 32)

    def lay_out(block, raw_w, mat, rws):
        raw_w[11 * C :, :] = jnp.zeros((C, W), bf16)
        for a in range(11):
            for q in range(6):
                one = all_ref[cell_rows(block, a, 2 * q), :].astype(f32)
                two = jnp.zeros((32, 128), f32)
                if q < 5:
                    two = all_ref[cell_rows(block, a, 2 * q + 1), :].astype(f32)
                cut = slice(128 * q, 128 * q + 128)
                raw_w[64 * a : 64 * a + 32, cut] = jnp.where(low32, one, swap(two)).astype(bf16)
                raw_w[64 * a + 32 : 64 * a + 64, cut] = jnp.where(low32, swap(one), two).astype(bf16)
        for i in range(6):
            cut = slice(128 * i, 128 * i + 128)
            v = jnp.dot(ahead, raw_w[cut, :], preferred_element_type=f32)
            v16 = v.astype(bf16)
            mat[cut, :] = v16
            rws[128 * i : 128 * i + 64, :] = v16[64:128]
            rws[128 * i + 64 : 128 * i + 128, :] = v16[0:64]
            for q in range(6):
                at = slice(128 * q, 128 * q + 128)
                raw_w[cut, at] = swap(v[:, at]).astype(bf16)

    own_first = lax.axis_index("wide") * per
    own = jnp.where(lanes(1), len_ref[own_first], len_ref[own_first + 1] if per == 2 else 0)

    def valid(t, n):
        return t + lax.broadcasted_iota(jnp.int32, (n, 128), 0) < own

    for z in range(slabs):
        res_ref[shard * z : shard * z + shard, :] = x_ref[z].astype(f32)[0:shard]
        gin_ref[shard * z : shard * z + shard, :] = cot_ref[z].astype(f32)[0:shard]

    for t in range(0, L, 176):
        v = jnp.where(valid(t, 176), res_ref[t : t + 176, :], 0.0)
        mg_ref[t : t + 176, :] = v
        pk_ref[PK + t : PK + t + 176, :] = v

    def pairs(i, dst):
        n = third + 16
        a = pk_ref[span_of(PK - 8 + third * i, n), :]
        b = pk_ref[pl.ds(PK - 7 + third * i, n), :]
        low = lanes(n)
        dst[0, span_of(third * i, n), :] = jnp.where(low, a, swap(b))
        dst[1, span_of(third * i, n), :] = jnp.where(low, swap(a), b)

    def within(t, n, p):
        at = t + lax.broadcasted_iota(jnp.int32, (n, 128), 0)
        inv = 1.0 / jnp.full((1, 128), p, jnp.int32).astype(f32)
        return at - ((at.astype(f32) + 0.5) * inv).astype(jnp.int32) * p

    def build_cols(i, k, src, dst):
        p, nk = periods[k], tiles[k][0]
        n = 176
        for half in range(third // n):
            t = third * i + n * half
            wi = within(t, n, p) + jnp.where(lanes(n), 0, 1)
            for q in range(2 * nk):
                base = BASES[q]
                keep = wi >= -base if base < 0 else wi < p - base
                for s in range(2):
                    v = src[s, pl.ds(8 + base + t, n), :]
                    dst[span_of(s * L + t, n, 16), 128 * q : 128 * q + 128] = jnp.where(
                        keep, v, 0.0
                    ).astype(bf16)

    def build_rows(i, k, src, dst):
        p, nr = periods[k], tiles[k][1]
        n = 176
        low = lanes(n)
        for half in range(third // n):
            t = third * i + n * half
            for q in range(2 * nr):
                one = pl.ds(PP + jnp.clip(t - OFFS[2 * q] * p, -n, L), n)
                a, b = src[0, one, :], src[1, one, :]
                if q < 5:
                    two = pl.ds(PP + jnp.clip(t - OFFS[2 * q + 1] * p, -n, L), n)
                    c, d = src[0, two, :], src[1, two, :]
                else:
                    c = d = jnp.zeros((n, 128), f32)
                cut = slice(128 * q, 128 * q + 128)
                dst[span_of(t, n, 16), cut] = jnp.where(low, a, d).astype(bf16)
                dst[span_of(L + t, n, 16), cut] = jnp.where(low, b, c).astype(bf16)

    def sum_rows(t, n, k, src):
        p, nr = periods[k], tiles[k][1]
        sums = [jnp.zeros((n, 128), f32)] * 2
        for b in range(min(4 * nr, 11)):
            off = PS + jnp.clip(OFFS[b] * p + t, -n, L)
            sums[b % 2] = sums[b % 2] + src[b, pl.ds(off, n), :]
        return sums[0] + swap(sums[1])

    def sum_cols(t, n, k, src):
        p, nk = periods[k], tiles[k][0]
        wi = within(t, n, p)
        sums = [jnp.zeros((n, 128), f32)] * 2
        for b in range(min(4 * nk, 11)):
            d = OFFS[b]
            v = src[b, pl.ds(PS - d + t, n), :]
            if d < 0:
                v = jnp.where(wi < p + d, v, 0.0)
            elif d > 0:
                v = jnp.where(wi >= d, v, 0.0)
            sums[b % 2] = sums[b % 2] + v
        return sums[0] + swap(sums[1])

    def twice(i, first):
        v = small_ref[i : i + 1, :]
        return jnp.where(lanes(1) == first, v, swap(v))

    bias_one, bias_two = twice(0, True), twice(0, False)
    gain, shift = twice(1, True), twice(1, False)
    NS = 88

    def activate(i, k):
        for j in range(third // (2 * NS)):
            acts = []
            for h in range(2):
                t = third * i + NS * (2 * j + h)
                v = sum_rows(t, NS, k, s1_ref) + bias_one
                cdf = 0.5 * (1.0 + lax.erf(v * inv_root_two))
                slope_ref[k, span_of(t, NS), :] = cdf + v * jnp.exp(-0.5 * v * v) * inv_root_tau
                acts.append(v * cdf)
            t = third * i + 2 * NS * j
            act = jnp.concatenate(acts, axis=0).astype(bf16)
            act_ref[k, span_of(t, 2 * NS, 16), :] = act
            pk_ref[span_of(PK + t, 2 * NS), :] = act.astype(f32)

    def branch(i, k):
        wk = wv_ref[k : k + 1, :]
        for j in range(third // NS):
            t = third * i + NS * j
            v = sum_rows(t, NS, k, s2_ref) + bias_two
            br_ref[k, span_of(t, NS), :] = v
            mg_ref[span_of(t, NS), :] += wk * v

    def rebuild(i, k):
        v = act_ref[k, span_of(third * i, third, 16), :].astype(f32)
        pk_ref[span_of(PK + third * i, third), :] = v

    def spread_branch(i, k):
        wk = wv_ref[k : k + 1, :]
        for j in range(third // NS):
            t = third * i + NS * j
            gm = mg_ref[span_of(t, NS), :]
            gw_ref[k] += fold(gm * br_ref[k, span_of(t, NS), :])
            g = (wk * gm).astype(bf16).astype(f32)
            gb_ref[1] += fold(g)
            p2_ref[0, span_of(PP + t, NS), :] = g
            p2_ref[1, span_of(PP + t, NS), :] = swap(g)

    def spread_hidden(i, k):
        for j in range(third // NS):
            t = third * i + NS * j
            g = sum_cols(t, NS, k, s1_ref) * slope_ref[k, span_of(t, NS), :]
            g = g.astype(bf16).astype(f32)
            gb_ref[0] += fold(g)
            p1_ref[0, span_of(PP + t, NS), :] = g
            p1_ref[1, span_of(PP + t, NS), :] = swap(g)

    def collect(i, k):
        for j in range(third // NS):
            t = third * i + NS * j
            gin_ref[span_of(t, NS), :] += sum_cols(t, NS, k, s2_ref)

    def to_slots(dst, n, t, rows, d0, d1):
        low = lanes(rows)
        for h in range(2):
            a = d0[:, 128 * h : 128 * h + 128]
            b = d1[:, 128 * h : 128 * h + 128]
            dst[4 * n + 2 * h, span_of(PS + t, rows), :] = jnp.where(low, a, b)
            dst[4 * n + 2 * h + 1, span_of(PS + t, rows), :] = jnp.where(low, b, a)

    def mm_forward(i, k, src, w, ws, dst):
        depth = slice(0, 256 * tiles[k][0])
        if tiles[k][1] == 3:
            n, t, rows = i, 0, L
        else:
            n, t, rows = 0, third * i, third
        cut = span_of(256 * n, 256, 256)
        d0 = jnp.dot(src[span_of(t, rows, 16), depth], w[depth, cut], preferred_element_type=f32)
        d1 = jnp.dot(
            src[span_of(L + t, rows, 16), depth], ws[depth, cut], preferred_element_type=f32
        )
        to_slots(dst, n, t, rows, d0, d1)

    def mm_adjoint(i, k, src, w, wr, dst):
        depth = slice(0, 256 * tiles[k][1])
        if tiles[k][0] == 3:
            n, t, rows = i, 0, L
        else:
            n, t, rows = 0, third * i, third
        cut = span_of(256 * n, 256, 256)
        dims = (((1,), (1,)), ((), ()))
        d0 = lax.dot_general(
            src[span_of(t, rows, 16), depth], w[cut, depth], dims, preferred_element_type=f32
        )
        d1 = lax.dot_general(
            src[span_of(L + t, rows, 16), depth], wr[cut, depth], dims, preferred_element_type=f32
        )
        to_slots(dst, n, t, rows, d0, d1)

    def mm_weights(i, k, left, right, gm):
        nk, nr = tiles[k]
        step = span_of(256 * i, 256, 256)
        rws, cols = (step, slice(0, 256 * nr)) if nk == 3 else (slice(0, 256), step)
        gm[rws, cols] += lax.dot_general(
            left[:, rws], right[:, cols], (((0,), (0,)), ((), ())), preferred_element_type=f32
        )

    def phase(*work):
        @pl.loop(0, 3)
        def _(i):
            for item in work:
                item[0](i, *item[1:])

    lay_out(0, w1s_ref, w1_ref, w1r_ref)
    phase((pairs, xf_ref))
    phase((build_cols, 0, xf_ref, xs_ref))

    lane = lax.broadcasted_iota(jnp.int32, (1, 128), 1)
    turn = jnp.zeros((1, 128), jnp.int32)
    for j in range(K):
        turn = jnp.where(lane % 8 == j, freqs[j], turn)

    def waves(i):
        t = i * third + lax.broadcasted_iota(jnp.int32, (third, 128), 0)
        turns = t * turn
        whole = ((turns.astype(f32) + 0.5) * (1.0 / L)).astype(jnp.int32)
        angle = (turns - whole * L).astype(f32) * (2.0 * math.pi / L)
        angle = jnp.where(lane < 8, angle, angle - 0.5 * math.pi)
        wave = jnp.where((lane < 16) & (lane % 8 < K), jnp.cos(angle), 0.0)
        hi, mid, lo = (v.astype(f32) for v in split(wave))
        trig_ref[span_of(i * third, third, 16), :] = (
            hi + pltpu.roll(mid, 16, 1) + pltpu.roll(lo, 32, 1)
        ).astype(bf16)

    phase((mm_forward, 0, xs_ref, w1_ref, w1s_ref, s1_ref), (waves,))
    lay_out(1, w2s_ref, w2_ref, w2r_ref)

    spec = lax.dot_general(
        trig_ref[...],
        mg_ref[...].astype(bf16),
        (((0,), (0,)), ((), ())),
        preferred_element_type=f32,
    )
    spec = (spec[0:16] + spec[16:32] + spec[32:48]) * (2.0 / L)
    real, imag = spec[0:8], spec[8:16]
    magnitude = jnp.sqrt(real * real + imag * imag + 1.0)
    mean_mag = half_sum(magnitude) * (1.0 / C)
    live = lax.broadcasted_iota(jnp.int32, (8, 128), 0) < K
    top = jnp.max(jnp.where(live, mean_mag, -1e30), axis=0, keepdims=True)
    ex = jnp.where(live, jnp.exp(mean_mag - top), 0.0)
    weights = ex / jnp.sum(ex, axis=0, keepdims=True)
    wv_ref[...] = weights

    phase((activate, 0), (build_cols, 1, xf_ref, xs_ref))
    for k in range(K):
        work = [(pairs, af_ref), (build_cols, k, af_ref, as_ref)]
        if k > 0:
            work.append((branch, k - 1))
        if k + 1 < K:
            work.insert(0, (mm_forward, k + 1, xs_ref, w1_ref, w1s_ref, s1_ref))
        phase(*work)
        work = [(mm_forward, k, as_ref, w2_ref, w2s_ref, s2_ref)]
        if k + 1 < K:
            work.append((activate, k + 1))
        if k + 2 < K:
            work.append((build_cols, k + 2, xf_ref, xs_ref))
        phase(*work)
    phase((branch, K - 1))

    same = (
        lax.broadcasted_iota(jnp.int32, (384, 128), 0) % 128 // C
        == lax.broadcasted_iota(jnp.int32, (384, 128), 1) // C
    )
    ones = jnp.where(same, 1.0 / C, 0.0).astype(bf16)

    def half_mean(v):
        return jnp.dot(jnp.concatenate(split(v), axis=1), ones, preferred_element_type=f32)

    def normalise(i):
        at = span_of(i * third, third)
        m = mg_ref[at, :]
        ok = valid(i * third, third)
        centered = m - half_mean(m)
        inverse = lax.rsqrt(half_mean(centered * centered) + norm_eps)
        normed = centered * inverse
        res_ref[at, :] = jnp.where(ok, normed * gain + shift, 0.0)
        g_out = jnp.where(ok, gin_ref[at, :], 0.0)
        gb_ref[2] += fold(g_out * normed)
        gb_ref[3] += fold(g_out)
        g_norm = g_out * gain
        gm = inverse * (g_norm - half_mean(g_norm) - normed * half_mean(g_norm * normed))
        mg_ref[at, :] = gm
        gin_ref[at, :] = gm

    phase((normalise,))

    def to_slabs(dst):
        for z in range(slabs):
            v = res_ref[shard * z : shard * z + shard, :]
            v = jnp.concatenate([v, jnp.zeros((dst.shape[1] - shard, 128), f32)], axis=0)
            dst[z] = v.astype(bf16)

    to_slabs(out_ref)

    phase((spread_branch, 0))
    phase((build_rows, 0, p2_ref, r2_ref))
    for k in range(K):
        phase((rebuild, k))
        work = [
            (mm_adjoint, k, r2_ref, w2_ref, w2r_ref, s1_ref),
            (pairs, af_ref),
            (build_cols, k, af_ref, as_ref),
        ]
        if k > 0:
            work.append((collect, k - 1))
        phase(*work)
        work = [(spread_hidden, k)]
        if k > 0:
            work.insert(0, (mm_weights, k - 1, xs_ref, r1_ref, gm1_ref))
        phase(*work)
        work = [
            (mm_weights, k, as_ref, r2_ref, gm2_ref),
            (build_rows, k, p1_ref, r1_ref),
            (build_cols, k, xf_ref, xs_ref),
        ]
        if k + 1 < K:
            work.append((spread_branch, k + 1))
        phase(*work)
        work = [(mm_adjoint, k, r1_ref, w1_ref, w1r_ref, s2_ref)]
        if k + 1 < K:
            work.append((build_rows, k + 1, p2_ref, r2_ref))
        phase(*work)

    row8 = lax.broadcasted_iota(jnp.int32, (8, 128), 0)
    g_weights = jnp.zeros((8, 128), f32)
    for j in range(K):
        total = jnp.sum(gw_ref[j], axis=0, keepdims=True)
        g_weights = jnp.where(row8 == j, total, g_weights)
    g_weights = half_sum(g_weights)
    weights = wv_ref[...]
    g_score = weights * (g_weights - jnp.sum(weights * g_weights, axis=0, keepdims=True))
    coeff = g_score / (magnitude * C) * (2.0 / L)
    c_hi, c_lo, _ = split(jnp.concatenate([coeff * real, coeff * imag], axis=0))
    c_all = jnp.concatenate([c_hi, c_hi, c_hi, jnp.zeros((80, 128), bf16)], axis=0)
    c_low = jnp.concatenate([c_lo, jnp.zeros((112, 128), bf16)], axis=0)

    def finish(i):
        at = span_of(i * third, third)
        t = trig_ref[span_of(i * third, third, 16), :]
        g = (
            gin_ref[at, :]
            + jnp.dot(t, c_all, preferred_element_type=f32)
            + jnp.dot(t, c_low, preferred_element_type=f32)
        )
        res_ref[at, :] = jnp.where(valid(i * third, third), g, 0.0)

    phase((mm_weights, K - 1, xs_ref, r1_ref, gm1_ref), (collect, K - 1), (finish,))
    to_slabs(gser_ref)

    sums = []
    for q in range(4):
        total = jnp.sum(gb_ref[q], axis=0, keepdims=True)
        sums.append(total + swap(total))
    gsm_ref[0:1, :] = jnp.where(lanes(1), sums[0], sums[1])
    gsm_ref[1:2, :] = jnp.where(lanes(1), sums[2], sums[3])

    used = set(int(v) for v in row_of)
    for v in range(grad_ref.shape[0] // 32):
        if v not in used:
            grad_ref[32 * v : 32 * v + 32, :] = jnp.zeros((32, 128), f32)
    back = jnp.where(r == c // 64 * 64 + c % 2 * 32 + c % 64 // 2, 1.0, 0.0).astype(bf16)
    back = jnp.concatenate([back, back, back], axis=1)
    for block, mat in enumerate((gm1_ref, gm2_ref)):
        for i in range(6):
            v = jnp.concatenate(split(mat[128 * i : 128 * i + 128, :]), axis=0)
            v = jnp.dot(back, v, preferred_element_type=f32)
            for a in (2 * i, 2 * i + 1):
                if a == 11:
                    continue
                first = 64 * (a % 2)
                for q in range(6):
                    even = v[first : first + 32, 128 * q : 128 * q + 128]
                    odd = v[first + 32 : first + 64, 128 * q : 128 * q + 128]
                    grad_ref[cell_rows(block, a, 2 * q), :] = jnp.where(low32, even, swap(odd))
                    if q < 5:
                        grad_ref[cell_rows(block, a, 2 * q + 1), :] = jnp.where(
                            low32, swap(even), odd
                        )


vm = pl.BlockSpec(memory_space=pltpu.VMEM)
sm = pl.BlockSpec(memory_space=pltpu.SMEM)
sds = jax.ShapeDtypeStruct


def run_block(x, cot, lens, freqs, cells, small, per, row_of, L):
    return pl.pallas_call(
        functools.partial(block_kernel, L, per, row_of),
        out_shape=(
            sds(x.shape, bf16),
            sds(x.shape, bf16),
            sds(cells.shape, f32),
            sds((2, 128), f32),
        ),
        in_specs=[sm, sm, vm, vm, vm, vm],
        out_specs=(vm,) * 4,
        scratch_shapes=[
            pltpu.VMEM((W, W), f32),
            pltpu.VMEM((W, W), f32),
            pltpu.VMEM((W, W), bf16),
            pltpu.VMEM((W, W), bf16),
            pltpu.VMEM((W, W), bf16),
            pltpu.VMEM((W, W), bf16),
            pltpu.VMEM((W, W), bf16),
            pltpu.VMEM((W, W), bf16),
            pltpu.VMEM((L, 128), bf16),
            pltpu.VMEM((L, 128), f32),
            pltpu.VMEM((L, 128), f32),
            pltpu.VMEM((L, 128), f32),
            pltpu.VMEM((2, L + 16, 128), f32),
            pltpu.VMEM((2, L + 16, 128), f32),
            pltpu.VMEM((L + 32, 128), f32),
            pltpu.VMEM((2 * L, W), bf16),
            pltpu.VMEM((2 * L, W), bf16),
            pltpu.VMEM((12, L + 176, 128), f32),
            pltpu.VMEM((12, L + 176, 128), f32),
            pltpu.VMEM((2, L + 352, 128), f32),
            pltpu.VMEM((2, L + 352, 128), f32),
            pltpu.VMEM((2 * L, W), bf16),
            pltpu.VMEM((2 * L, W), bf16),
            pltpu.VMEM((K, L, 128), bf16),
            pltpu.VMEM((K, L, 128), f32),
            pltpu.VMEM((K, L, 128), f32),
            pltpu.VMEM((8, 128), f32),
            pltpu.VMEM((K, 8, 128), f32),
            pltpu.VMEM((4, 8, 128), f32),
        ],
        compiler_params=pltpu.CompilerParams(vmem_limit_bytes=62 << 20),
        name="block",
    )(freqs, lens, x, cot, cells, small)


def adam_update(param, grad, first, second):
    first_new = beta_one * first + (1.0 - beta_one) * grad
    second_new = beta_two * second + (1.0 - beta_two) * grad * grad
    first_hat = first_new / (1.0 - beta_one**STEP)
    second_hat = second_new / (1.0 - beta_two**STEP)
    param_new = param - learn_rate * (
        first_hat / (jnp.sqrt(second_hat) + adam_eps) + weight_decay * param
    )
    return (param_new, first_new, second_new)


def local(series, lengths, freqs, cotangent, kernels, kernel_m, kernel_v, small, small_m, small_v):
    wide = lax.axis_size("wide")
    batch = lax.axis_size("batch")
    count = wide * batch
    half, sides = count // 2, math.isqrt(batch // 2)
    me = lax.axis_index(("wide", "batch"))
    span, room, deep, spread, pick, weight, row_of = plan(wide, batch)
    share = kernels.shape[0]
    shard = series.shape[1]
    per = series.shape[0] // wide
    slab = -(-shard // 16) * 16

    tables = np.concatenate([v.reshape(count, -1) for v in (spread, pick, weight)], axis=1)
    table = lax.dynamic_index_in_dim(jnp.asarray(tables), me, 0, keepdims=False)
    aligned = share % 128 == 0
    lead = me * share % TAP

    def to_rows(v):
        if aligned:
            return v.reshape(share // 128, 128)
        wide_v = jnp.zeros((span * TAP,), f32)
        return lax.dynamic_update_slice_in_dim(wide_v, v, lead, 0).reshape(span * 32, 128)

    def from_rows(v):
        if aligned:
            return v.reshape(share)
        return lax.dynamic_slice_in_dim(v.reshape(-1), lead, share, 0)

    lead_step = share // 128 if aligned else 0
    params = pltpu.CompilerParams
    static = (wide, batch, lead_step, span, room, deep, per)
    dma = pltpu.SemaphoreType.DMA
    cell_shape = (wide, sides, sides, 2, room * 32, 128)
    slab_shape = (wide, slab, 128)
    exchange = (half, deep, 32, 128)
    taps_rows = -(-(span * 32 + 32) // 8) * 8
    taps = to_rows(kernels)
    held = taps.shape[0]

    x, cot, cells = pl.pallas_call(
        functools.partial(gather_kernel, *static),
        out_shape=(sds(slab_shape, bf16), sds(slab_shape, bf16), sds(cell_shape, bf16)),
        in_specs=[sm, vm, vm, vm],
        out_specs=(vm,) * 3,
        scratch_shapes=[
            pltpu.VMEM((taps_rows, 128), f32),
            pltpu.VMEM(exchange, f32),
            pltpu.VMEM(exchange, f32),
            pltpu.VMEM(slab_shape, bf16),
            pltpu.VMEM(slab_shape, bf16),
            dma((2, half - 1)),
            dma((2, wide - 1)),
            dma((2, wide - 1)),
            dma((2, wide - 1)),
            dma((2, 2 * (sides - 1))),
            dma((2, 2 * (sides - 1))),
            dma((2, 4 * (sides - 1) + 1)),
        ],
        compiler_params=params(
            collective_id=0, has_side_effects=True, vmem_limit_bytes=48 << 20
        ),
        name="gather",
    )(table, taps, series.transpose(0, 2, 1), cotangent.transpose(0, 2, 1))

    small_rows = small.reshape(2, 128)
    out, gser, grads, gsm = run_block(
        x, cot, lengths, freqs, cells.reshape(-1, 128), small_rows, per, row_of, shard * wide
    )

    link = bf16
    cut = room * 16
    out, gser, grad_share, total = pl.pallas_call(
        functools.partial(reduce_kernel, *static),
        out_shape=(
            sds(slab_shape, bf16),
            sds(slab_shape, bf16),
            sds((held, 128), f32),
            sds((8, 128), f32),
        ),
        in_specs=[sm] + [vm] * 4,
        out_specs=(vm,) * 4,
        scratch_shapes=[
            pltpu.VMEM((wide, sides, sides, room * 32, 128), link),
            pltpu.VMEM((wide, sides, sides, room * 32, 128), link),
            pltpu.VMEM((wide, sides, sides, room * 32, 128), f32),
            pltpu.VMEM((sides - 1, wide, sides, cut, 128), link),
            pltpu.VMEM((sides - 1, wide, sides, cut, 128), link),
            pltpu.VMEM((sides - 1, wide, sides, cut, 128), link),
            pltpu.VMEM((sides - 1, wide, sides, cut, 128), link),
            pltpu.VMEM((wide, sides, cut, 128), f32),
            pltpu.VMEM((wide, sides, cut, 128), f32),
            pltpu.VMEM((sides - 1, wide, cut, 128), link),
            pltpu.VMEM((sides - 1, wide, cut, 128), link),
            pltpu.VMEM((sides - 1, wide, cut, 128), link),
            pltpu.VMEM((sides - 1, wide, cut, 128), link),
            pltpu.VMEM((wide, room * 32, 128), f32),
            pltpu.VMEM((wide, room * 32, 128), link),
            pltpu.VMEM((wide - 1, room * 32, 128), link),
            pltpu.VMEM((room * 32, 128), f32),
            pltpu.VMEM(exchange, f32),
            pltpu.VMEM(exchange, f32),
            pltpu.VMEM((8, 128), f32),
            pltpu.VMEM((count, 8, 128), f32),
            pltpu.VMEM((taps_rows, 128), f32),
            dma((2, 1)),
            dma((2, 2 * (sides - 1))),
            dma((2, 2 * (sides - 1))),
            dma((2, wide - 1)),
            dma((2, wide - 1)),
            dma((2, wide - 1)),
            dma((2, half - 1)),
            dma((2, count - 1)),
        ],
        compiler_params=params(
            collective_id=1, has_side_effects=True, vmem_limit_bytes=60 << 20
        ),
        name="reduce",
    )(table, grads.reshape(cell_shape), gsm, out, gser)

    turned = (series.shape[0], series.shape[2], shard)
    out, gser, norm, new_w, new_m, new_v, new_sw, new_sm, new_sv = pl.pallas_call(
        functools.partial(finish_kernel, per),
        out_shape=(
            sds(turned, bf16),
            sds(turned, bf16),
            sds((1, 1), f32),
            sds((held, 128), f32),
            sds((held, 128), f32),
            sds((held, 128), f32),
            sds((2, 128), f32),
            sds((2, 128), f32),
            sds((2, 128), f32),
        ),
        in_specs=[vm] * 10,
        out_specs=(vm,) * 9,
        compiler_params=params(vmem_limit_bytes=48 << 20),
        name="finish",
    )(
        total,
        grad_share,
        out,
        gser,
        taps,
        to_rows(kernel_m),
        to_rows(kernel_v),
        small_rows,
        small_m.reshape(2, 128),
        small_v.reshape(2, 128),
    )
    return (
        out.transpose(0, 2, 1),
        gser.transpose(0, 2, 1),
        norm.reshape(()),
        from_rows(new_w),
        from_rows(new_m),
        from_rows(new_v),
        new_sw.reshape(-1),
        new_sm.reshape(-1),
        new_sv.reshape(-1),
    )


def solution(mesh):
    placed = (
        P("batch", "wide", None),
        P("batch"),
        P(),
        P("batch", "wide", None),
        P(("wide", "batch")),
        P(("wide", "batch")),
        P(("wide", "batch")),
        P(),
        P(),
        P(),
    )
    return jax.shard_map(
        local,
        mesh=mesh,
        in_specs=placed,
        out_specs=(
            P("batch", "wide", None),
            P("batch", "wide", None),
            P(),
            P(("wide", "batch")),
            P(("wide", "batch")),
            P(("wide", "batch")),
            P(),
            P(),
            P(),
        ),
        check_vma=False,
    )
```

```python
import functools
import math

import jax
import jax.numpy as jnp
import numpy as np
from jax import lax
from jax.experimental import pallas as pl
from jax.experimental.pallas import tpu as pltpu
from jax.sharding import PartitionSpec as P

C = 64
K = 5
NKER = 6
STEP = 10
SPAN = 11
HALF = 5
TAPS = 286
CELLS = SPAN * SPAN
TAP = C * C
DEEP_STEPS = 1

beta_one = 0.9
beta_two = 0.999
learn_rate = 0.1
weight_decay = 0.01
adam_eps = 1e-08
clip_norm = 1.0
norm_eps = 1e-05
inv_root_two = 1.0 / math.sqrt(2.0)
inv_root_tau = 1.0 / math.sqrt(2.0 * math.pi)

bf16 = jnp.bfloat16
f32 = jnp.float32
precise = lax.Precision.HIGHEST

OFFS = (-1, 0, 1, 2, -3, -2, 3, 4, -5, -4, 5, 6)
BASES = (-1, 1, -3, 3, -5, 5)
W = 12 * C


def tap_cells():
    cells = []
    for block in range(2):
        for kernel in range(NKER):
            for row_off in range(-kernel, kernel + 1):
                for col_off in range(-kernel, kernel + 1):
                    cells.append(block * CELLS + (row_off + HALF) * SPAN + col_off + HALF)
    return np.array(cells)


def is_deep(same_plane, step, batch):
    return same_plane or step % batch < DEEP_STEPS


@functools.lru_cache(None)
def plan(wide, batch):
    cells = tap_cells()
    count = wide * batch
    half = count // 2
    share = cells.size * TAP // count
    holds = [
        range(share * d // TAP, (share * (d + 1) - 1) // TAP + 1) for d in range(count)
    ]
    span = max(len(taps) for taps in holds)
    needs = [sorted(set(cells[taps.start : taps.stop].tolist())) for taps in holds]
    room = -(-CELLS // half)
    deep = 1 if max(len(need) for need in needs) <= 4 else 2
    users = [[d for d in range(count) if cell in needs[d]] for cell in range(2 * CELLS)]
    order = sorted(range(2 * CELLS), key=lambda cell: -len(users[cell]))
    for seed in range(1000):
        rng = np.random.RandomState(seed)
        owner = np.full(2 * CELLS, -1)
        filled = np.zeros(count, int)
        between = np.zeros((count, count), int)
        for cell in order:
            first = cell // CELLS * half
            free = [
                o
                for o in range(first, first + half)
                if filled[o] < room and all(
                    between[d, o] < (deep if is_deep(d // batch == o // batch, o - d, batch) else 1)
                    for d in users[cell]
                )
            ]
            if not free:
                break
            cost = [(sum(between[d, o] for d in users[cell]), filled[o]) for o in free]
            least = min(cost)
            free = [o for o, c in zip(free, cost) if c == least]
            o = free[rng.randint(len(free))]
            owner[cell] = o
            filled[o] += 1
            for d in users[cell]:
                between[d, o] += 1
        else:
            break
    place = np.zeros(2 * CELLS, int)
    filled[:] = 0
    for cell in range(2 * CELLS):
        place[cell] = filled[owner[cell]]
        filled[owner[cell]] += 1
    spread = np.zeros((count, half * deep, span), np.float32)
    pick = np.zeros((count, room, half * deep), np.float32)
    between[:] = 0
    for d, taps in enumerate(holds):
        for cell in needs[d]:
            o = owner[cell]
            slot = between[d, o]
            between[d, o] += 1
            pick[o, place[cell], d % half * deep + slot] = 1.0
            for tap in taps:
                if cells[tap] == cell:
                    spread[d, o % half * deep + slot, tap - taps.start] = 1.0
    weight = np.zeros((count, room), np.float32)
    for cell in range(2 * CELLS):
        row, col = divmod(cell % CELLS, SPAN)
        weight[owner[cell], place[cell]] = NKER - max(abs(row - HALF), abs(col - HALF))
    row_of = owner * room + place
    return span, room, deep, spread, pick, weight, row_of


MESH = pl.DeviceIdType.MESH


class Place:
    def __init__(self, wide, batch):
        self.nz, self.nb = wide, batch
        self.ns = math.isqrt(batch // 2)
        self.z = lax.axis_index("wide")
        self.b = lax.axis_index("batch")
        self.core = lax.rem(self.b, 2)
        self.x = lax.rem(self.b // 2, self.ns)
        self.y = self.b // (2 * self.ns)
        self.half = wide * batch // 2
        self.me = self.z * batch + self.b
        self.mine = lax.rem(self.me, self.half)

    def batch_of(self, y, x, core):
        return (y * self.ns + x) * 2 + core

    def at_z(self, d):
        return (lax.rem(self.z + d, self.nz), self.b)

    def at_y(self, d):
        return (self.z, self.batch_of(lax.rem(self.y + d, self.ns), self.x, self.core))

    def at_x(self, d):
        return (self.z, self.batch_of(self.y, lax.rem(self.x + d, self.ns), self.core))

    def sibling(self):
        return (self.z, self.batch_of(self.y, self.x, 1 - self.core))

    def in_half(self, dz, db):
        planes = self.nz // 2
        first = self.z // planes * planes
        z = lax.rem(self.z - first + dz, planes)
        b = lax.rem(self.b + db, self.nb)
        return z * self.nb + b, (first + z, b)

    def half_steps(self):
        return [
            (dz, db) for dz in range(self.nz // 2) for db in range(self.nb) if (dz, db) != (0, 0)
        ]

    def at_all(self, d):
        other = lax.rem(self.me + d, self.nz * self.nb)
        return (other // self.nb, lax.rem(other, self.nb))


def greet(peers):
    barrier = pltpu.get_barrier_semaphore()
    for peer in peers:
        pl.semaphore_signal(barrier, inc=1, device_id=peer, device_id_type=MESH)
    pl.semaphore_wait(barrier, len(peers))


def send(src, dst, sems, k, peer):
    copy = pltpu.make_async_remote_copy(
        src_ref=src,
        dst_ref=dst,
        send_sem=sems.at[0, k],
        recv_sem=sems.at[1, k],
        device_id=peer,
        device_id_type=MESH,
    )
    copy.start()
    return copy


def swap_cells(at, deep, way, src, dst, sems):
    copies = []
    for k, (dz, db) in enumerate(at.half_steps()):
        index, peer = at.in_half(dz, db)
        keep = pl.ds(0, deep if is_deep(dz == 0, way * db, at.nb) else 1)
        copies.append(send(src.at[index, keep], dst.at[at.mine, keep], sems, k, peer))
    dst[at.mine] = src[at.mine]
    return copies


def lane_low(rows):
    return lax.broadcasted_iota(jnp.int32, (rows, 128), 1) < C


def gather_kernel(
    wide,
    batch,
    lead_step,
    span,
    room,
    deep,
    per,
    table_ref,
    taps_ref,
    series_ref,
    cot_ref,
    x_ref,
    c_ref,
    all_ref,
    tap_ref,
    slot_ref,
    got_ref,
    xs_ref,
    cs_ref,
    tap_sem,
    x_sem,
    c_sem,
    z_sem,
    a_sem,
    b_sem,
    core_sem,
):
    at = Place(wide, batch)
    nz, ns, half = at.nz, at.ns, at.half
    shard = series_ref.shape[2]
    pad = x_ref.shape[1] - shard
    held = taps_ref.shape[0]
    got_ref[...] = jnp.zeros(got_ref.shape, f32)
    tap_ref[...] = jnp.zeros(tap_ref.shape, f32)
    tap_ref[pl.ds(lax.rem(at.me * lead_step, 32), held), :] = taps_ref[...]

    @pl.loop(0, half)
    def _(o):
        for s in range(deep):
            total = jnp.zeros((32, 128), f32)
            for t in range(span):
                total = total + (
                    table_ref[(o * deep + s) * span + t] * tap_ref[32 * t : 32 * t + 32, :]
                )
            slot_ref[o, s] = total

    greet(
        [at.in_half(*step)[1] for step in at.half_steps()] + [at.at_z(d) for d in range(1, nz)]
    )

    taps = swap_cells(at, deep, 1, slot_ref, got_ref, tap_sem)

    def pack(src, keep):
        for z in range(nz):
            first = src[per * z].astype(f32)
            second = src[per * z + 1].astype(f32) if per == 2 else jnp.zeros_like(first)
            both = jnp.concatenate([first, second], axis=0).T
            both = jnp.concatenate([both, jnp.zeros((pad, 128), f32)], axis=0)
            keep[z] = both.astype(bf16)

    waits = []

    def exchange(keep, out, sems):
        for d in range(1, nz):
            waits.append(send(keep.at[lax.rem(at.z + d, nz)], out.at[at.z], sems, d - 1, at.at_z(d)))
        out[at.z] = keep[at.z]

    pack(series_ref, xs_ref)
    pack(cot_ref, cs_ref)

    for copy in taps:
        copy.wait_recv()

    picks = half * deep * span
    for k in range(room):
        total = jnp.zeros((32, 128), f32)

        def add(q, total):
            for s in range(deep):
                total = total + table_ref[picks + k * half * deep + q * deep + s] * got_ref[q, s]
            return total

        total = lax.fori_loop(0, half, add, total)
        all_ref[at.z, at.y, at.x, at.core, 32 * k : 32 * k + 32, :] = (
            total * (1.0 / NKER)
        ).astype(bf16)

    cut = room * 32 // 2
    low, high = pl.ds(0, cut), pl.ds(cut, cut)
    block = all_ref.at[at.z, at.y, at.x, at.core]
    stage = [send(block, block, z_sem, d - 1, at.at_z(d)) for d in range(1, nz)]

    def to_sibling(part):
        waits.append(send(part, part, core_sem, len(waits), at.sibling()))

    for copy in stage:
        copy.wait()
    stage = []
    for d in range(1, ns):
        part = all_ref.at[:, at.y, at.x, at.core, low]
        stage.append(send(part, part, a_sem, d - 1, at.at_y(d)))
        part = all_ref.at[:, at.y, at.x, at.core, high]
        stage.append(send(part, part, b_sem, d - 1, at.at_x(d)))
    to_sibling(all_ref.at[:, at.y, at.x, at.core])
    for copy in stage:
        copy.wait()
    stage = []
    for d in range(1, ns):
        part = all_ref.at[:, :, at.x, at.core, low]
        stage.append(send(part, part, a_sem, ns + d - 2, at.at_x(d)))
        part = all_ref.at[:, at.y, :, at.core, high]
        stage.append(send(part, part, b_sem, ns + d - 2, at.at_y(d)))
    for d in range(1, ns):
        to_sibling(all_ref.at[:, lax.rem(at.y + d, ns), at.x, at.core, low])
        to_sibling(all_ref.at[:, at.y, lax.rem(at.x + d, ns), at.core, high])
    exchange(xs_ref, x_ref, x_sem)
    exchange(cs_ref, c_ref, c_sem)
    for copy in stage:
        copy.wait()
    late = []
    for d in range(1, ns):
        k = 2 * (ns - 1) + 1 + 2 * (d - 1)
        part = all_ref.at[:, :, lax.rem(at.x + d, ns), at.core, low]
        late.append(send(part, part, core_sem, k, at.sibling()))
        part = all_ref.at[:, lax.rem(at.y + d, ns), :, at.core, high]
        late.append(send(part, part, core_sem, k + 1, at.sibling()))
    for copy in waits + late:
        copy.wait()
    for copy in taps:
        copy.wait_send()


def reduce_kernel(
    wide,
    batch,
    lead_step,
    span,
    room,
    deep,
    per,
    table_ref,
    grad_ref,
    gsm_ref,
    o_ref,
    g_ref,
    oz_ref,
    gz_ref,
    share_ref,
    total_ref,
    send_ref,
    core_ref,
    acc_ref,
    sa_ref,
    sb_ref,
    ra_ref,
    rb_ref,
    a_ref,
    b_ref,
    sa2_ref,
    sb2_ref,
    ra2_ref,
    rb2_ref,
    own_ref,
    sz_ref,
    rz_ref,
    sum_ref,
    back_ref,
    got_ref,
    tile_ref,
    tiles_ref,
    tap_ref,
    core_sem,
    a_sem,
    b_sem,
    z_sem,
    o_sem,
    g_sem,
    tap_sem,
    all_sem,
):
    at = Place(wide, batch)
    nz, ns, half = at.nz, at.ns, at.half
    count = nz * at.nb
    cut = room * 32 // 2
    link = send_ref.dtype
    got_ref[...] = jnp.zeros(got_ref.shape, f32)

    for z in range(nz):
        send_ref[z] = grad_ref[z, :, :, 1 - at.core].astype(link)
    greet([at.at_all(d) for d in range(1, count)])
    core_copy = send(send_ref, core_ref, core_sem, 0, at.sibling())

    waits = []
    for src, dst, sems in ((o_ref, oz_ref, o_sem), (g_ref, gz_ref, g_sem)):
        for d in range(1, nz):
            waits.append(send(src.at[lax.rem(at.z + d, nz)], dst.at[at.z], sems, d - 1, at.at_z(d)))
        dst[at.z] = src[at.z]

    core_copy.wait()
    for z in range(nz):
        acc_ref[z] = grad_ref[z, :, :, at.core] + core_ref[z].astype(f32)

    stage = []
    for d in range(1, ns):
        x = lax.rem(at.x + d, ns)
        y = lax.rem(at.y + d, ns)
        for z in range(nz):
            for o in range(ns):
                sa_ref[d - 1, z, o] = acc_ref[z, o, x, 0:cut, :].astype(link)
                sb_ref[d - 1, z, o] = acc_ref[z, y, o, cut : 2 * cut, :].astype(link)
        stage.append(send(sa_ref.at[d - 1], ra_ref.at[d - 1], a_sem, d - 1, at.at_x(d)))
        stage.append(send(sb_ref.at[d - 1], rb_ref.at[d - 1], b_sem, d - 1, at.at_y(d)))
    for copy in stage:
        copy.wait()
    for z in range(nz):
        for o in range(ns):
            va = acc_ref[z, o, at.x, 0:cut, :]
            vb = acc_ref[z, at.y, o, cut : 2 * cut, :]
            for d in range(1, ns):
                va = va + ra_ref[d - 1, z, o].astype(f32)
                vb = vb + rb_ref[d - 1, z, o].astype(f32)
            a_ref[z, o] = va
            b_ref[z, o] = vb
    stage = []
    for d in range(1, ns):
        x = lax.rem(at.x + d, ns)
        y = lax.rem(at.y + d, ns)
        for z in range(nz):
            sa2_ref[d - 1, z] = a_ref[z, y].astype(link)
            sb2_ref[d - 1, z] = b_ref[z, x].astype(link)
        stage.append(send(sa2_ref.at[d - 1], ra2_ref.at[d - 1], a_sem, ns + d - 2, at.at_y(d)))
        stage.append(send(sb2_ref.at[d - 1], rb2_ref.at[d - 1], b_sem, ns + d - 2, at.at_x(d)))
    for copy in stage:
        copy.wait()
    for z in range(nz):
        va = a_ref[z, at.y]
        vb = b_ref[z, at.x]
        for d in range(1, ns):
            va = va + ra2_ref[d - 1, z].astype(f32)
            vb = vb + rb2_ref[d - 1, z].astype(f32)
        own_ref[z, 0:cut, :] = va
        own_ref[z, cut : 2 * cut, :] = vb
        sz_ref[z, 0:cut, :] = va.astype(link)
        sz_ref[z, cut : 2 * cut, :] = vb.astype(link)
    stage = [
        send(sz_ref.at[lax.rem(at.z + d, nz)], rz_ref.at[d - 1], z_sem, d - 1, at.at_z(d))
        for d in range(1, nz)
    ]
    for copy in stage:
        copy.wait()
    total = own_ref[at.z]
    for d in range(1, nz):
        total = total + rz_ref[d - 1].astype(f32)
    sum_ref[...] = total * (1.0 / NKER)

    picks = half * deep * span
    weights = picks + room * half * deep
    square = jnp.zeros((1, 128), f32)
    for k in range(room):
        value = sum_ref[32 * k : 32 * k + 32, :]
        square = square + table_ref[weights + k] * jnp.sum(value * value, axis=0, keepdims=True)
    tile_ref[0:2, :] = gsm_ref[...]
    tile_ref[2:3, :] = square
    tile_ref[3:8, :] = jnp.zeros((5, 128), f32)
    tells = [
        send(tile_ref, tiles_ref.at[at.me], all_sem, d - 1, at.at_all(d)) for d in range(1, count)
    ]
    tiles_ref[at.me] = tile_ref[...]

    @pl.loop(0, half)
    def _(q):
        for s in range(deep):
            value = jnp.zeros((32, 128), f32)
            for k in range(room):
                value = value + (
                    table_ref[picks + k * half * deep + q * deep + s]
                    * sum_ref[32 * k : 32 * k + 32, :]
                )
            back_ref[q, s] = value

    backs = swap_cells(at, deep, -1, back_ref, got_ref, tap_sem)
    for copy in tells:
        copy.wait()
    tile = jnp.zeros((8, 128), f32)
    for d in range(count):
        tile = tile + tiles_ref[d]
    total_ref[...] = tile
    for copy in backs:
        copy.wait()

    @pl.loop(0, span)
    def _(t):
        value = jnp.zeros((32, 128), f32)
        for q in range(half):
            for s in range(deep):
                value = value + table_ref[(q * deep + s) * span + t] * got_ref[q, s]
        tap_ref[pl.ds(pl.multiple_of(32 * t, 32), 32), :] = value

    held = share_ref.shape[0]
    share_ref[...] = tap_ref[pl.ds(lax.rem(at.me * lead_step, 32), held), :]
    for copy in waits:
        copy.wait()


def finish_kernel(
    per,
    total_ref,
    share_ref,
    o_ref,
    g_ref,
    w_ref,
    m_ref,
    v_ref,
    sw_ref,
    sm_ref,
    sv_ref,
    out_ref,
    gser_ref,
    norm_ref,
    nw_ref,
    nm_ref,
    nv_ref,
    nsw_ref,
    nsm_ref,
    nsv_ref,
):
    small = total_ref[0:2, :]
    lanes = jnp.sum(total_ref[2:3, :], axis=1, keepdims=True)
    squares = jnp.sum(jnp.sum(small * small, axis=0, keepdims=True), axis=1, keepdims=True)
    norm = jnp.sqrt(lanes + squares)
    norm_ref[...] = norm
    factor = jnp.minimum(1.0, clip_norm / (norm + 1e-06))
    nsw_ref[...], nsm_ref[...], nsv_ref[...] = adam_update(
        sw_ref[...], small * factor, sm_ref[...], sv_ref[...]
    )
    nw_ref[...], nm_ref[...], nv_ref[...] = adam_update(
        w_ref[...], share_ref[...] * factor, m_ref[...], v_ref[...]
    )
    shard = out_ref.shape[2]
    for src, dst in ((o_ref, out_ref), (g_ref, gser_ref)):
        for z in range(src.shape[0]):
            both = src[z].astype(f32).T
            dst[per * z] = both[0:C, 0:shard].astype(bf16)
            if per == 2:
                dst[per * z + 1] = both[C:, 0:shard].astype(bf16)


def block_kernel(
    L,
    per,
    row_of,
    freq_ref,
    len_ref,
    x_ref,
    cot_ref,
    all_ref,
    small_ref,
    out_ref,
    gser_ref,
    grad_ref,
    gsm_ref,
    gm1_ref,
    gm2_ref,
    w1_ref,
    w2_ref,
    w1s_ref,
    w2s_ref,
    w1r_ref,
    w2r_ref,
    trig_ref,
    res_ref,
    mg_ref,
    gin_ref,
    xf_ref,
    af_ref,
    pk_ref,
    xs_ref,
    s1_ref,
    s2_ref,
    p2_ref,
    p1_ref,
    r_ref,
    act_ref,
    slope_ref,
    br_ref,
    wv_ref,
    gw_ref,
    gb_ref,
):
    slabs = x_ref.shape[0]
    shard = L // slabs
    lanes = lane_low
    third = L // 3
    PS, PP, PK = 88, 176, 16

    def swap(v):
        return pltpu.roll(v, C, 1)

    def span_of(t, n, align=8):
        assert t % align == 0
        return slice(t, t + n)

    def half_sum(v):
        low = lanes(v.shape[0])
        a = jnp.sum(jnp.where(low, v, 0.0), axis=1, keepdims=True)
        b = jnp.sum(jnp.where(low, 0.0, v), axis=1, keepdims=True)
        return jnp.where(low, a, b)

    def fold(v):
        return jnp.sum(v.reshape(v.shape[0] // 8, 8, 128), axis=0)

    def split(v):
        hi = v.astype(bf16)
        rest = v - hi.astype(f32)
        mid = rest.astype(bf16)
        return hi, mid, (rest - mid.astype(f32)).astype(bf16)

    raw = [freq_ref[j] for j in range(K)]
    ranks = [sum((raw[j] > raw[k]).astype(jnp.int32) for k in range(K)) for j in range(K)]
    freqs = [sum(jnp.where(ranks[j] == k, raw[j], 0) for j in range(K)) for k in range(K)]
    order = (1, 2, 3, 0, 4)
    periods = [L // freqs[j] for j in order]
    freqs = [freqs[j] for j in order]
    tiles = [(3, 3), (3, 3), (3, 3), (3, 1), (1, 3)]

    for ref, pad in ((s1_ref, PS), (s2_ref, PS), (p1_ref, PP), (p2_ref, PP)):
        for b in range(ref.shape[0]):
            ref[b, 0:pad, :] = jnp.zeros((pad, 128), f32)
            ref[b, L + pad : L + 2 * pad, :] = jnp.zeros((pad, 128), f32)
    pk_ref[0:PK, :] = jnp.zeros((PK, 128), f32)
    pk_ref[L + PK : L + 2 * PK, :] = jnp.zeros((PK, 128), f32)
    gm1_ref[...] = jnp.zeros((W, W), f32)
    gm2_ref[...] = jnp.zeros((W, W), f32)
    gb_ref[...] = jnp.zeros((4, 8, 128), f32)
    gw_ref[...] = jnp.zeros((K, 8, 128), f32)

    r = lax.broadcasted_iota(jnp.int32, (128, 128), 0)
    c = lax.broadcasted_iota(jnp.int32, (128, 128), 1)
    ahead = jnp.where(c == r // 64 * 64 + r % 2 * 32 + r % 64 // 2, 1.0, 0.0).astype(bf16)
    low32 = lanes(32)

    def cell_rows(block, a, b):
        cell = block * CELLS + (OFFS[b] + HALF) * SPAN + OFFS[a] + HALF
        return slice(int(row_of[cell]) * 32, int(row_of[cell]) * 32 + 32)

    def lay_out(block, raw_w, mat, rws):
        raw_w[11 * C :, :] = jnp.zeros((C, W), bf16)
        for a in range(11):
            for q in range(6):
                one = all_ref[cell_rows(block, a, 2 * q), :].astype(f32)
                two = jnp.zeros((32, 128), f32)
                if q < 5:
                    two = all_ref[cell_rows(block, a, 2 * q + 1), :].astype(f32)
                cut = slice(128 * q, 128 * q + 128)
                raw_w[64 * a : 64 * a + 32, cut] = jnp.where(low32, one, swap(two)).astype(bf16)
                raw_w[64 * a + 32 : 64 * a + 64, cut] = jnp.where(low32, swap(one), two).astype(bf16)
        for i in range(6):
            cut = slice(128 * i, 128 * i + 128)
            v = jnp.dot(ahead, raw_w[cut, :], preferred_element_type=f32)
            v16 = v.astype(bf16)
            mat[cut, :] = v16
            rws[128 * i : 128 * i + 64, :] = v16[64:128]
            rws[128 * i + 64 : 128 * i + 128, :] = v16[0:64]
            for q in range(6):
                at = slice(128 * q, 128 * q + 128)
                raw_w[cut, at] = swap(v[:, at]).astype(bf16)

    own_first = lax.axis_index("wide") * per
    own = jnp.where(lanes(1), len_ref[own_first], len_ref[own_first + 1] if per == 2 else 0)

    def valid(t, n):
        return t + lax.broadcasted_iota(jnp.int32, (n, 128), 0) < own

    for z in range(slabs):
        res_ref[shard * z : shard * z + shard, :] = x_ref[z].astype(f32)[0:shard]
        gin_ref[shard * z : shard * z + shard, :] = cot_ref[z].astype(f32)[0:shard]

    for t in range(0, L, 176):
        v = jnp.where(valid(t, 176), res_ref[t : t + 176, :], 0.0)
        mg_ref[t : t + 176, :] = v
        pk_ref[PK + t : PK + t + 176, :] = v

    def pairs(i, dst):
        n = third + 16
        a = pk_ref[span_of(PK - 8 + third * i, n), :]
        b = pk_ref[PK - 7 + third * i : PK - 7 + third * i + n, :]
        low = lanes(n)
        dst[0, span_of(third * i, n), :] = jnp.where(low, a, swap(b))
        dst[1, span_of(third * i, n), :] = jnp.where(low, swap(a), b)

    def within(t, n, p):
        at = t + lax.broadcasted_iota(jnp.int32, (n, 128), 0)
        inv = 1.0 / jnp.full((1, 128), p, jnp.int32).astype(f32)
        return at - ((at.astype(f32) + 0.5) * inv).astype(jnp.int32) * p

    def build_cols(i, k, src, dst):
        p, nk = periods[k], tiles[k][0]
        n = 176
        for half in range(third // n):
            t = third * i + n * half
            wi = within(t, n, p) + jnp.where(lanes(n), 0, 1)
            for q in range(2 * nk):
                base = BASES[q]
                keep = wi >= -base if base < 0 else wi < p - base
                for s in range(2):
                    v = src[s, 8 + base + t : 8 + base + t + n, :]
                    dst[span_of(s * L + t, n, 16), 128 * q : 128 * q + 128] = jnp.where(
                        keep, v, 0.0
                    ).astype(bf16)

    def build_rows(i, k, src, dst):
        p, nr = periods[k], tiles[k][1]
        n = 176
        low = lanes(n)
        for half in range(third // n):
            t = third * i + n * half
            for q in range(2 * nr):
                one = pl.ds(PP + jnp.clip(t - OFFS[2 * q] * p, -n, L), n)
                a, b = src[0, one, :], src[1, one, :]
                if q < 5:
                    two = pl.ds(PP + jnp.clip(t - OFFS[2 * q + 1] * p, -n, L), n)
                    c, d = src[0, two, :], src[1, two, :]
                else:
                    c = d = jnp.zeros((n, 128), f32)
                cut = slice(128 * q, 128 * q + 128)
                dst[span_of(t, n, 16), cut] = jnp.where(low, a, d).astype(bf16)
                dst[span_of(L + t, n, 16), cut] = jnp.where(low, b, c).astype(bf16)

    def sum_rows(t, n, k, src):
        p, nr = periods[k], tiles[k][1]
        sums = [jnp.zeros((n, 128), f32)] * 2
        for b in range(min(4 * nr, 11)):
            off = PS + jnp.clip(OFFS[b] * p + t, -n, L)
            sums[b % 2] = sums[b % 2] + src[b, pl.ds(off, n), :]
        return sums[0] + swap(sums[1])

    def sum_cols(t, n, k, src):
        p, nk = periods[k], tiles[k][0]
        wi = within(t, n, p)
        sums = [jnp.zeros((n, 128), f32)] * 2
        for b in range(min(4 * nk, 11)):
            d = OFFS[b]
            v = src[b, PS - d + t : PS - d + t + n, :]
            if d < 0:
                v = jnp.where(wi < p + d, v, 0.0)
            elif d > 0:
                v = jnp.where(wi >= d, v, 0.0)
            sums[b % 2] = sums[b % 2] + v
        return sums[0] + swap(sums[1])

    def twice(i, first):
        v = small_ref[i : i + 1, :]
        return jnp.where(lanes(1) == first, v, swap(v))

    bias_one, bias_two = twice(0, True), twice(0, False)
    gain, shift = twice(1, True), twice(1, False)
    NS = 88

    def hidden(i, k):
        for j in range(third // NS):
            t = third * i + NS * j
            slope_ref[k, span_of(t, NS), :] = sum_rows(t, NS, k, s1_ref) + bias_one

    def activate(i, k):
        n = 176
        for t in range(third * i, third * i + third, n):
            v = slope_ref[k, span_of(t, n), :]
            cdf = 0.5 * (1.0 + lax.erf(v * inv_root_two))
            slope_ref[k, span_of(t, n), :] = cdf + v * jnp.exp(-0.5 * v * v) * inv_root_tau
            act = (v * cdf).astype(bf16)
            act_ref[k, span_of(t, n, 16), :] = act
            pk_ref[span_of(PK + t, n), :] = act.astype(f32)

    def branch(i, k):
        for j in range(third // NS):
            t = third * i + NS * j
            br_ref[k, span_of(t, NS), :] = sum_rows(t, NS, k, s2_ref) + bias_two

    def merge(i, k):
        wk = wv_ref[k : k + 1, :]
        at = span_of(third * i, third)
        mg_ref[at, :] += wk * br_ref[k, at, :]

    def rebuild(i, k):
        v = act_ref[k, span_of(third * i, third, 16), :].astype(f32)
        pk_ref[span_of(PK + third * i, third), :] = v

    def spread_branch(i, k):
        wk = wv_ref[k : k + 1, :]
        sum_w = sum_b = jnp.zeros((8, 128), f32)
        for j in range(third // NS):
            t = third * i + NS * j
            gm = mg_ref[span_of(t, NS), :]
            sum_w = sum_w + fold(gm * br_ref[k, span_of(t, NS), :])
            g = (wk * gm).astype(bf16).astype(f32)
            sum_b = sum_b + fold(g)
            p2_ref[0, span_of(PP + t, NS), :] = g
            p2_ref[1, span_of(PP + t, NS), :] = swap(g)
        gw_ref[k] += sum_w
        gb_ref[1] += sum_b

    def spread_hidden(i, k):
        sum_b = jnp.zeros((8, 128), f32)
        for j in range(third // NS):
            t = third * i + NS * j
            g = sum_cols(t, NS, k, s1_ref) * slope_ref[k, span_of(t, NS), :]
            g = g.astype(bf16).astype(f32)
            sum_b = sum_b + fold(g)
            p1_ref[0, span_of(PP + t, NS), :] = g
            p1_ref[1, span_of(PP + t, NS), :] = swap(g)
        gb_ref[0] += sum_b

    def collect(i, k):
        for j in range(third // NS):
            t = third * i + NS * j
            gin_ref[span_of(t, NS), :] += sum_cols(t, NS, k, s2_ref)

    def to_slots(dst, n, d0, d1):
        low = lanes(L)
        for h in range(2):
            a = d0[:, 128 * h : 128 * h + 128]
            b = d1[:, 128 * h : 128 * h + 128]
            dst[4 * n + 2 * h, PS : PS + L, :] = jnp.where(low, a, b)
            if 4 * n + 2 * h + 1 < 11:
                dst[4 * n + 2 * h + 1, PS : PS + L, :] = jnp.where(low, b, a)

    def mm_forward(i, k, src, w, ws, dst):
        if i >= tiles[k][1]:
            return
        depth, cut = slice(0, 256 * tiles[k][0]), slice(256 * i, 256 * i + 256)
        d0 = jnp.dot(src[0:L, depth], w[depth, cut], preferred_element_type=f32)
        d1 = jnp.dot(src[L : 2 * L, depth], ws[depth, cut], preferred_element_type=f32)
        to_slots(dst, i, d0, d1)

    def mm_adjoint(i, k, src, w, wr, dst):
        if i >= tiles[k][0]:
            return
        depth, cut = slice(0, 256 * tiles[k][1]), slice(256 * i, 256 * i + 256)
        dims = (((1,), (1,)), ((), ()))
        d0 = lax.dot_general(src[0:L, depth], w[cut, depth], dims, preferred_element_type=f32)
        d1 = lax.dot_general(src[L : 2 * L, depth], wr[cut, depth], dims, preferred_element_type=f32)
        to_slots(dst, i, d0, d1)

    def mm_weights(i, k, left, right, gm):
        if i >= tiles[k][0]:
            return
        cut, wide_cut = slice(256 * i, 256 * i + 256), slice(0, 256 * tiles[k][1])
        gm[cut, wide_cut] += lax.dot_general(
            left[:, cut], right[:, wide_cut], (((0,), (0,)), ((), ())), preferred_element_type=f32
        )

    blocks = []

    def block(*work):
        blocks.append(work)

        @pl.when(raw[len(blocks) % K] + len(blocks) > 0)
        def _():
            for item in work:
                for i in range(3):
                    item[0](i, *item[1:])

    def once(i, f, *rest):
        if i == 0:
            f(*rest)

    block((once, lay_out, 0, w1s_ref, w1_ref, w1r_ref), (pairs, xf_ref))

    lane = lax.broadcasted_iota(jnp.int32, (1, 128), 1)
    turn = jnp.zeros((1, 128), jnp.int32)
    for j in range(K):
        turn = jnp.where(lane % 8 == j, freqs[j], turn)

    def waves(i):
        t = i * third + lax.broadcasted_iota(jnp.int32, (third, 128), 0)
        turns = t * turn
        whole = ((turns.astype(f32) + 0.5) * (1.0 / L)).astype(jnp.int32)
        angle = (turns - whole * L).astype(f32) * (2.0 * math.pi / L)
        angle = jnp.where(lane < 8, angle, angle - 0.5 * math.pi)
        wave = jnp.where((lane < 16) & (lane % 8 < K), jnp.cos(angle), 0.0)
        hi, mid, lo = (v.astype(f32) for v in split(wave))
        trig_ref[span_of(i * third, third, 16), :] = (
            hi + pltpu.roll(mid, 16, 1) + pltpu.roll(lo, 32, 1)
        ).astype(bf16)

    block(
        (build_cols, 0, xf_ref, xs_ref),
        (mm_forward, 0, xs_ref, w1_ref, w1s_ref, s1_ref),
        (waves,),
    )
    block((once, lay_out, 1, w2s_ref, w2_ref, w2r_ref))

    spec = lax.dot_general(
        trig_ref[...],
        mg_ref[...].astype(bf16),
        (((0,), (0,)), ((), ())),
        preferred_element_type=f32,
    )
    spec = (spec[0:16] + spec[16:32] + spec[32:48]) * (2.0 / L)
    real, imag = spec[0:8], spec[8:16]
    magnitude = jnp.sqrt(real * real + imag * imag + 1.0)
    mean_mag = half_sum(magnitude) * (1.0 / C)
    live = lax.broadcasted_iota(jnp.int32, (8, 128), 0) < K
    top = jnp.max(jnp.where(live, mean_mag, -1e30), axis=0, keepdims=True)
    ex = jnp.where(live, jnp.exp(mean_mag - top), 0.0)
    weights = ex / jnp.sum(ex, axis=0, keepdims=True)
    wv_ref[...] = weights

    block((hidden, 0), (activate, 0))
    for k in range(K):
        if k + 1 < K:
            work = [
                (build_cols, k + 1, xf_ref, xs_ref),
                (mm_forward, k + 1, xs_ref, w1_ref, w1s_ref, s1_ref),
            ]
            if k > 0:
                work = [(branch, k - 1)] + work + [(merge, k - 1)]
            block(*work)
        work = [
            (pairs, af_ref),
            (build_cols, k, af_ref, xs_ref),
            (mm_forward, k, xs_ref, w2_ref, w2s_ref, s2_ref),
        ]
        if k + 1 < K:
            work = [(hidden, k + 1)] + work + [(activate, k + 1)]
        else:
            work = [(branch, k - 1)] + work + [(merge, k - 1)]
        block(*work)

    same = (
        lax.broadcasted_iota(jnp.int32, (384, 128), 0) % 128 // C
        == lax.broadcasted_iota(jnp.int32, (384, 128), 1) // C
    )
    ones = jnp.where(same, 1.0 / C, 0.0).astype(bf16)

    def half_mean(v):
        return jnp.dot(jnp.concatenate(split(v), axis=1), ones, preferred_element_type=f32)

    def normalise(i):
        at = span_of(i * third, third)
        m = mg_ref[at, :]
        ok = valid(i * third, third)
        centered = m - half_mean(m)
        inverse = lax.rsqrt(half_mean(centered * centered) + norm_eps)
        normed = centered * inverse
        res_ref[at, :] = jnp.where(ok, normed * gain + shift, 0.0)
        g_out = jnp.where(ok, gin_ref[at, :], 0.0)
        gb_ref[2] += fold(g_out * normed)
        gb_ref[3] += fold(g_out)
        g_norm = g_out * gain
        gm = inverse * (g_norm - half_mean(g_norm) - normed * half_mean(g_norm * normed))
        mg_ref[at, :] = gm
        gin_ref[at, :] = gm

    block((branch, K - 1), (merge, K - 1), (normalise,), (spread_branch, 0))

    def to_slabs(dst):
        for z in range(slabs):
            v = res_ref[shard * z : shard * z + shard, :]
            v = jnp.concatenate([v, jnp.zeros((dst.shape[1] - shard, 128), f32)], axis=0)
            dst[z] = v.astype(bf16)

    to_slabs(out_ref)

    for k in range(K):
        work = [
            (build_rows, k, p2_ref, r_ref),
            (mm_adjoint, k, r_ref, w2_ref, w2r_ref, s1_ref),
            (rebuild, k),
        ]
        if k > 0:
            work.append((collect, k - 1))
        block(*work)
        work = [
            (pairs, af_ref),
            (build_cols, k, af_ref, xs_ref),
            (mm_weights, k, xs_ref, r_ref, gm2_ref),
            (spread_hidden, k),
        ]
        if k + 1 < K:
            work.append((spread_branch, k + 1))
        block(*work)
        block(
            (build_rows, k, p1_ref, r_ref),
            (mm_adjoint, k, r_ref, w1_ref, w1r_ref, s2_ref),
        )
        block(
            (build_cols, k, xf_ref, xs_ref),
            (mm_weights, k, xs_ref, r_ref, gm1_ref),
        )

    row8 = lax.broadcasted_iota(jnp.int32, (8, 128), 0)
    g_weights = jnp.zeros((8, 128), f32)
    for j in range(K):
        total = jnp.sum(gw_ref[j], axis=0, keepdims=True)
        g_weights = jnp.where(row8 == j, total, g_weights)
    g_weights = half_sum(g_weights)
    weights = wv_ref[...]
    g_score = weights * (g_weights - jnp.sum(weights * g_weights, axis=0, keepdims=True))
    coeff = g_score / (magnitude * C) * (2.0 / L)
    c_hi, c_lo, _ = split(jnp.concatenate([coeff * real, coeff * imag], axis=0))
    c_all = jnp.concatenate([c_hi, c_hi, c_hi, jnp.zeros((80, 128), bf16)], axis=0)
    c_low = jnp.concatenate([c_lo, jnp.zeros((112, 128), bf16)], axis=0)

    def finish(i):
        at = span_of(i * third, third)
        t = trig_ref[span_of(i * third, third, 16), :]
        g = (
            gin_ref[at, :]
            + jnp.dot(t, c_all, preferred_element_type=f32)
            + jnp.dot(t, c_low, preferred_element_type=f32)
        )
        res_ref[at, :] = jnp.where(valid(i * third, third), g, 0.0)

    block((collect, K - 1), (finish,))
    to_slabs(gser_ref)

    sums = []
    for q in range(4):
        total = jnp.sum(gb_ref[q], axis=0, keepdims=True)
        sums.append(total + swap(total))
    gsm_ref[0:1, :] = jnp.where(lanes(1), sums[0], sums[1])
    gsm_ref[1:2, :] = jnp.where(lanes(1), sums[2], sums[3])

    used = set(int(v) for v in row_of)
    for v in range(grad_ref.shape[0] // 32):
        if v not in used:
            grad_ref[32 * v : 32 * v + 32, :] = jnp.zeros((32, 128), f32)
    back = jnp.where(r == c // 64 * 64 + c % 2 * 32 + c % 64 // 2, 1.0, 0.0).astype(bf16)
    back = jnp.concatenate([back, back, back], axis=1)
    for block, mat in enumerate((gm1_ref, gm2_ref)):
        for i in range(6):
            v = jnp.concatenate(split(mat[128 * i : 128 * i + 128, :]), axis=0)
            v = jnp.dot(back, v, preferred_element_type=f32)
            for a in (2 * i, 2 * i + 1):
                if a == 11:
                    continue
                first = 64 * (a % 2)
                for q in range(6):
                    even = v[first : first + 32, 128 * q : 128 * q + 128]
                    odd = v[first + 32 : first + 64, 128 * q : 128 * q + 128]
                    grad_ref[cell_rows(block, a, 2 * q), :] = jnp.where(low32, even, swap(odd))
                    if q < 5:
                        grad_ref[cell_rows(block, a, 2 * q + 1), :] = jnp.where(
                            low32, swap(even), odd
                        )


vm = pl.BlockSpec(memory_space=pltpu.VMEM)
sm = pl.BlockSpec(memory_space=pltpu.SMEM)
sds = jax.ShapeDtypeStruct


def run_block(x, cot, lens, freqs, cells, small, per, row_of, L):
    return pl.pallas_call(
        functools.partial(block_kernel, L, per, row_of),
        out_shape=(
            sds(x.shape, bf16),
            sds(x.shape, bf16),
            sds(cells.shape, f32),
            sds((2, 128), f32),
        ),
        in_specs=[sm, sm, vm, vm, vm, vm],
        out_specs=(vm,) * 4,
        scratch_shapes=[
            pltpu.VMEM((W, W), f32),
            pltpu.VMEM((W, W), f32),
            pltpu.VMEM((W, W), bf16),
            pltpu.VMEM((W, W), bf16),
            pltpu.VMEM((W, W), bf16),
            pltpu.VMEM((W, W), bf16),
            pltpu.VMEM((W, W), bf16),
            pltpu.VMEM((W, W), bf16),
            pltpu.VMEM((L, 128), bf16),
            pltpu.VMEM((L, 128), f32),
            pltpu.VMEM((L, 128), f32),
            pltpu.VMEM((L, 128), f32),
            pltpu.VMEM((2, L + 16, 128), f32),
            pltpu.VMEM((2, L + 16, 128), f32),
            pltpu.VMEM((L + 32, 128), f32),
            pltpu.VMEM((2 * L, W), bf16),
            pltpu.VMEM((12, L + 176, 128), f32),
            pltpu.VMEM((12, L + 176, 128), f32),
            pltpu.VMEM((2, L + 352, 128), f32),
            pltpu.VMEM((2, L + 352, 128), f32),
            pltpu.VMEM((2 * L, W), bf16),
            pltpu.VMEM((K, L, 128), bf16),
            pltpu.VMEM((K, L, 128), f32),
            pltpu.VMEM((K, L, 128), f32),
            pltpu.VMEM((8, 128), f32),
            pltpu.VMEM((K, 8, 128), f32),
            pltpu.VMEM((4, 8, 128), f32),
        ],
        compiler_params=pltpu.CompilerParams(vmem_limit_bytes=63 << 20),
        name="block",
    )(freqs, lens, x, cot, cells, small)


def adam_update(param, grad, first, second):
    first_new = beta_one * first + (1.0 - beta_one) * grad
    second_new = beta_two * second + (1.0 - beta_two) * grad * grad
    first_hat = first_new / (1.0 - beta_one**STEP)
    second_hat = second_new / (1.0 - beta_two**STEP)
    param_new = param - learn_rate * (
        first_hat / (jnp.sqrt(second_hat) + adam_eps) + weight_decay * param
    )
    return (param_new, first_new, second_new)


def local(series, lengths, freqs, cotangent, kernels, kernel_m, kernel_v, small, small_m, small_v):
    wide = lax.axis_size("wide")
    batch = lax.axis_size("batch")
    count = wide * batch
    half, sides = count // 2, math.isqrt(batch // 2)
    me = lax.axis_index(("wide", "batch"))
    span, room, deep, spread, pick, weight, row_of = plan(wide, batch)
    share = kernels.shape[0]
    shard = series.shape[1]
    per = series.shape[0] // wide
    slab = -(-shard // 16) * 16

    tables = np.concatenate([v.reshape(count, -1) for v in (spread, pick, weight)], axis=1)
    table = lax.dynamic_index_in_dim(jnp.asarray(tables), me, 0, keepdims=False)
    aligned = share % 128 == 0
    lead = me * share % TAP

    def to_rows(v):
        if aligned:
            return v.reshape(share // 128, 128)
        wide_v = jnp.zeros((span * TAP,), f32)
        return lax.dynamic_update_slice_in_dim(wide_v, v, lead, 0).reshape(span * 32, 128)

    def from_rows(v):
        if aligned:
            return v.reshape(share)
        return lax.dynamic_slice_in_dim(v.reshape(-1), lead, share, 0)

    lead_step = share // 128 if aligned else 0
    params = pltpu.CompilerParams
    static = (wide, batch, lead_step, span, room, deep, per)
    dma = pltpu.SemaphoreType.DMA
    cell_shape = (wide, sides, sides, 2, room * 32, 128)
    slab_shape = (wide, slab, 128)
    exchange = (half, deep, 32, 128)
    taps_rows = -(-(span * 32 + 32) // 8) * 8
    taps = to_rows(kernels)
    held = taps.shape[0]

    x, cot, cells = pl.pallas_call(
        functools.partial(gather_kernel, *static),
        out_shape=(sds(slab_shape, bf16), sds(slab_shape, bf16), sds(cell_shape, bf16)),
        in_specs=[sm, vm, vm, vm],
        out_specs=(vm,) * 3,
        scratch_shapes=[
            pltpu.VMEM((taps_rows, 128), f32),
            pltpu.VMEM(exchange, f32),
            pltpu.VMEM(exchange, f32),
            pltpu.VMEM(slab_shape, bf16),
            pltpu.VMEM(slab_shape, bf16),
            dma((2, half - 1)),
            dma((2, wide - 1)),
            dma((2, wide - 1)),
            dma((2, wide - 1)),
            dma((2, 2 * (sides - 1))),
            dma((2, 2 * (sides - 1))),
            dma((2, 4 * (sides - 1) + 1)),
        ],
        compiler_params=params(
            collective_id=0, has_side_effects=True, vmem_limit_bytes=62 << 20
        ),
        name="gather",
    )(table, taps, series.transpose(0, 2, 1), cotangent.transpose(0, 2, 1))

    small_rows = small.reshape(2, 128)
    out, gser, grads, gsm = run_block(
        x, cot, lengths, freqs, cells.reshape(-1, 128), small_rows, per, row_of, shard * wide
    )

    link = bf16
    cut = room * 16
    out, gser, grad_share, total = pl.pallas_call(
        functools.partial(reduce_kernel, *static),
        out_shape=(
            sds(slab_shape, bf16),
            sds(slab_shape, bf16),
            sds((held, 128), f32),
            sds((8, 128), f32),
        ),
        in_specs=[sm] + [vm] * 4,
        out_specs=(vm,) * 4,
        scratch_shapes=[
            pltpu.VMEM((wide, sides, sides, room * 32, 128), link),
            pltpu.VMEM((wide, sides, sides, room * 32, 128), link),
            pltpu.VMEM((wide, sides, sides, room * 32, 128), f32),
            pltpu.VMEM((sides - 1, wide, sides, cut, 128), link),
            pltpu.VMEM((sides - 1, wide, sides, cut, 128), link),
            pltpu.VMEM((sides - 1, wide, sides, cut, 128), link),
            pltpu.VMEM((sides - 1, wide, sides, cut, 128), link),
            pltpu.VMEM((wide, sides, cut, 128), f32),
            pltpu.VMEM((wide, sides, cut, 128), f32),
            pltpu.VMEM((sides - 1, wide, cut, 128), link),
            pltpu.VMEM((sides - 1, wide, cut, 128), link),
            pltpu.VMEM((sides - 1, wide, cut, 128), link),
            pltpu.VMEM((sides - 1, wide, cut, 128), link),
            pltpu.VMEM((wide, room * 32, 128), f32),
            pltpu.VMEM((wide, room * 32, 128), link),
            pltpu.VMEM((wide - 1, room * 32, 128), link),
            pltpu.VMEM((room * 32, 128), f32),
            pltpu.VMEM(exchange, f32),
            pltpu.VMEM(exchange, f32),
            pltpu.VMEM((8, 128), f32),
            pltpu.VMEM((count, 8, 128), f32),
            pltpu.VMEM((taps_rows, 128), f32),
            dma((2, 1)),
            dma((2, 2 * (sides - 1))),
            dma((2, 2 * (sides - 1))),
            dma((2, wide - 1)),
            dma((2, wide - 1)),
            dma((2, wide - 1)),
            dma((2, half - 1)),
            dma((2, count - 1)),
        ],
        compiler_params=params(
            collective_id=1, has_side_effects=True, vmem_limit_bytes=62 << 20
        ),
        name="reduce",
    )(table, grads.reshape(cell_shape), gsm, out, gser)

    turned = (series.shape[0], series.shape[2], shard)
    out, gser, norm, new_w, new_m, new_v, new_sw, new_sm, new_sv = pl.pallas_call(
        functools.partial(finish_kernel, per),
        out_shape=(
            sds(turned, bf16),
            sds(turned, bf16),
            sds((1, 1), f32),
            sds((held, 128), f32),
            sds((held, 128), f32),
            sds((held, 128), f32),
            sds((2, 128), f32),
            sds((2, 128), f32),
            sds((2, 128), f32),
        ),
        in_specs=[vm] * 10,
        out_specs=(vm,) * 9,
        compiler_params=params(vmem_limit_bytes=62 << 20),
        name="finish",
    )(
        total,
        grad_share,
        out,
        gser,
        taps,
        to_rows(kernel_m),
        to_rows(kernel_v),
        small_rows,
        small_m.reshape(2, 128),
        small_v.reshape(2, 128),
    )
    return (
        out.transpose(0, 2, 1),
        gser.transpose(0, 2, 1),
        norm.reshape(()),
        from_rows(new_w),
        from_rows(new_m),
        from_rows(new_v),
        new_sw.reshape(-1),
        new_sm.reshape(-1),
        new_sv.reshape(-1),
    )


def solution(mesh):
    placed = (
        P("batch", "wide", None),
        P("batch"),
        P(),
        P("batch", "wide", None),
        P(("wide", "batch")),
        P(("wide", "batch")),
        P(("wide", "batch")),
        P(),
        P(),
        P(),
    )
    return jax.shard_map(
        local,
        mesh=mesh,
        in_specs=placed,
        out_specs=(
            P("batch", "wide", None),
            P("batch", "wide", None),
            P(),
            P(("wide", "batch")),
            P(("wide", "batch")),
            P(("wide", "batch")),
            P(),
            P(),
            P(),
        ),
        check_vma=False,
    )
```

```python
import functools
import math

import jax
import jax.numpy as jnp
import numpy as np
from jax import lax
from jax.experimental import pallas as pl
from jax.experimental.pallas import tpu as pltpu
from jax.sharding import PartitionSpec as P

C = 64
K = 5
NKER = 6
STEP = 10
SPAN = 11
HALF = 5
TAPS = 286
CELLS = SPAN * SPAN
TAP = C * C
DEEP_STEPS = 1

beta_one = 0.9
beta_two = 0.999
learn_rate = 0.1
weight_decay = 0.01
adam_eps = 1e-08
clip_norm = 1.0
norm_eps = 1e-05
inv_root_two = 1.0 / math.sqrt(2.0)
inv_root_tau = 1.0 / math.sqrt(2.0 * math.pi)

bf16 = jnp.bfloat16
f32 = jnp.float32
precise = lax.Precision.HIGHEST

OFFS = (-1, 0, 1, 2, -3, -2, 3, 4, -5, -4, 5, 6)
BASES = (-1, 1, -3, 3, -5, 5)
W = 12 * C


def tap_cells():
    cells = []
    for block in range(2):
        for kernel in range(NKER):
            for row_off in range(-kernel, kernel + 1):
                for col_off in range(-kernel, kernel + 1):
                    cells.append(block * CELLS + (row_off + HALF) * SPAN + col_off + HALF)
    return np.array(cells)


def is_deep(same_plane, step, batch):
    return same_plane or step % batch < DEEP_STEPS


@functools.lru_cache(None)
def plan(wide, batch):
    cells = tap_cells()
    count = wide * batch
    half = count // 2
    share = cells.size * TAP // count
    holds = [
        range(share * d // TAP, (share * (d + 1) - 1) // TAP + 1) for d in range(count)
    ]
    span = max(len(taps) for taps in holds)
    needs = [sorted(set(cells[taps.start : taps.stop].tolist())) for taps in holds]
    room = -(-CELLS // half)
    deep = 1 if max(len(need) for need in needs) <= 4 else 2
    users = [[d for d in range(count) if cell in needs[d]] for cell in range(2 * CELLS)]
    order = sorted(range(2 * CELLS), key=lambda cell: -len(users[cell]))
    for seed in range(1000):
        rng = np.random.RandomState(seed)
        owner = np.full(2 * CELLS, -1)
        filled = np.zeros(count, int)
        between = np.zeros((count, count), int)
        for cell in order:
            first = cell // CELLS * half
            free = [
                o
                for o in range(first, first + half)
                if filled[o] < room and all(
                    between[d, o] < (deep if is_deep(d // batch == o // batch, o - d, batch) else 1)
                    for d in users[cell]
                )
            ]
            if not free:
                break
            cost = [(sum(between[d, o] for d in users[cell]), filled[o]) for o in free]
            least = min(cost)
            free = [o for o, c in zip(free, cost) if c == least]
            o = free[rng.randint(len(free))]
            owner[cell] = o
            filled[o] += 1
            for d in users[cell]:
                between[d, o] += 1
        else:
            break
    place = np.zeros(2 * CELLS, int)
    filled[:] = 0
    for cell in range(2 * CELLS):
        place[cell] = filled[owner[cell]]
        filled[owner[cell]] += 1
    spread = np.zeros((count, half * deep, span), np.float32)
    pick = np.zeros((count, room, half * deep), np.float32)
    between[:] = 0
    for d, taps in enumerate(holds):
        for cell in needs[d]:
            o = owner[cell]
            slot = between[d, o]
            between[d, o] += 1
            pick[o, place[cell], d % half * deep + slot] = 1.0
            for tap in taps:
                if cells[tap] == cell:
                    spread[d, o % half * deep + slot, tap - taps.start] = 1.0
    weight = np.zeros((count, room), np.float32)
    for cell in range(2 * CELLS):
        row, col = divmod(cell % CELLS, SPAN)
        weight[owner[cell], place[cell]] = NKER - max(abs(row - HALF), abs(col - HALF))
    row_of = owner * room + place
    return span, room, deep, spread, pick, weight, row_of


MESH = pl.DeviceIdType.MESH


class Place:
    def __init__(self, wide, batch):
        self.nz, self.nb = wide, batch
        self.ns = math.isqrt(batch // 2)
        self.z = lax.axis_index("wide")
        self.b = lax.axis_index("batch")
        self.core = lax.rem(self.b, 2)
        self.x = lax.rem(self.b // 2, self.ns)
        self.y = self.b // (2 * self.ns)
        self.half = wide * batch // 2
        self.me = self.z * batch + self.b
        self.mine = lax.rem(self.me, self.half)

    def batch_of(self, y, x, core):
        return (y * self.ns + x) * 2 + core

    def at_z(self, d):
        return (lax.rem(self.z + d, self.nz), self.b)

    def at_y(self, d):
        return (self.z, self.batch_of(lax.rem(self.y + d, self.ns), self.x, self.core))

    def at_x(self, d):
        return (self.z, self.batch_of(self.y, lax.rem(self.x + d, self.ns), self.core))

    def sibling(self):
        return (self.z, self.batch_of(self.y, self.x, 1 - self.core))

    def in_half(self, dz, db):
        planes = self.nz // 2
        first = self.z // planes * planes
        z = lax.rem(self.z - first + dz, planes)
        b = lax.rem(self.b + db, self.nb)
        return z * self.nb + b, (first + z, b)

    def half_steps(self):
        return [
            (dz, db) for dz in range(self.nz // 2) for db in range(self.nb) if (dz, db) != (0, 0)
        ]

    def at_all(self, d):
        other = lax.rem(self.me + d, self.nz * self.nb)
        return (other // self.nb, lax.rem(other, self.nb))


def greet(peers):
    barrier = pltpu.get_barrier_semaphore()
    for peer in peers:
        pl.semaphore_signal(barrier, inc=1, device_id=peer, device_id_type=MESH)
    pl.semaphore_wait(barrier, len(peers))


def send(src, dst, sems, k, peer):
    copy = pltpu.make_async_remote_copy(
        src_ref=src,
        dst_ref=dst,
        send_sem=sems.at[0, k],
        recv_sem=sems.at[1, k],
        device_id=peer,
        device_id_type=MESH,
    )
    copy.start()
    return copy


def swap_cells(at, deep, way, src, dst, sems):
    copies = []
    for k, (dz, db) in enumerate(at.half_steps()):
        index, peer = at.in_half(dz, db)
        keep = pl.ds(0, deep if is_deep(dz == 0, way * db, at.nb) else 1)
        copies.append(send(src.at[index, keep], dst.at[at.mine, keep], sems, k, peer))
    dst[at.mine] = src[at.mine]
    return copies


def lane_low(rows):
    return lax.broadcasted_iota(jnp.int32, (rows, 128), 1) < C


def gather_kernel(
    wide,
    batch,
    lead_step,
    span,
    room,
    deep,
    per,
    table_ref,
    taps_ref,
    series_ref,
    cot_ref,
    x_ref,
    c_ref,
    all_ref,
    tap_ref,
    slot_ref,
    got_ref,
    xs_ref,
    cs_ref,
    tap_sem,
    x_sem,
    c_sem,
    z_sem,
    a_sem,
    b_sem,
    core_sem,
):
    at = Place(wide, batch)
    nz, ns, half = at.nz, at.ns, at.half
    shard = series_ref.shape[2]
    pad = x_ref.shape[1] - shard
    held = taps_ref.shape[0]
    got_ref[...] = jnp.zeros(got_ref.shape, f32)
    tap_ref[...] = jnp.zeros(tap_ref.shape, f32)
    tap_ref[pl.ds(lax.rem(at.me * lead_step, 32), held), :] = taps_ref[...]

    @pl.loop(0, half)
    def _(o):
        for s in range(deep):
            total = jnp.zeros((32, 128), f32)
            for t in range(span):
                total = total + (
                    table_ref[(o * deep + s) * span + t] * tap_ref[32 * t : 32 * t + 32, :]
                )
            slot_ref[o, s] = total

    greet(
        [at.in_half(*step)[1] for step in at.half_steps()] + [at.at_z(d) for d in range(1, nz)]
    )

    taps = swap_cells(at, deep, 1, slot_ref, got_ref, tap_sem)

    def pack(src, keep):
        for z in range(nz):
            first = src[per * z].astype(f32)
            second = src[per * z + 1].astype(f32) if per == 2 else jnp.zeros_like(first)
            both = jnp.concatenate([first, second], axis=0).T
            both = jnp.concatenate([both, jnp.zeros((pad, 128), f32)], axis=0)
            keep[z] = both.astype(bf16)

    waits = []

    def exchange(keep, out, sems):
        for d in range(1, nz):
            waits.append(send(keep.at[lax.rem(at.z + d, nz)], out.at[at.z], sems, d - 1, at.at_z(d)))
        out[at.z] = keep[at.z]

    pack(series_ref, xs_ref)
    exchange(xs_ref, x_ref, x_sem)
    pack(cot_ref, cs_ref)

    for copy in taps:
        copy.wait_recv()

    picks = half * deep * span
    for k in range(room):
        total = jnp.zeros((32, 128), f32)

        def add(q, total):
            for s in range(deep):
                total = total + table_ref[picks + k * half * deep + q * deep + s] * got_ref[q, s]
            return total

        total = lax.fori_loop(0, half, add, total)
        all_ref[at.z, at.y, at.x, at.core, 32 * k : 32 * k + 32, :] = (
            total * (1.0 / NKER)
        ).astype(bf16)

    cut = room * 32 // 2
    low, high = pl.ds(0, cut), pl.ds(cut, cut)
    block = all_ref.at[at.z, at.y, at.x, at.core]
    planes = [send(block, block, z_sem, d - 1, at.at_z(d)) for d in range(1, nz)]
    exchange(cs_ref, c_ref, c_sem)
    first, second, last = [], [], []
    for j in range(nz):
        z = lax.rem(at.z + nz - j, nz)
        if j > 0:
            planes[j - 1].wait_recv()
        steps = []
        for d in range(1, ns):
            k = j * (ns - 1) + d - 1
            part = all_ref.at[z, at.y, at.x, at.core, low]
            steps.append(send(part, part, a_sem, k, at.at_y(d)))
            part = all_ref.at[z, at.y, at.x, at.core, high]
            steps.append(send(part, part, b_sem, k, at.at_x(d)))
        first.append(steps)
    for j in range(nz):
        z = lax.rem(at.z + nz - j, nz)
        for copy in first[j]:
            copy.wait_recv()
        steps = []
        for d in range(1, ns):
            k = (nz + j) * (ns - 1) + d - 1
            part = all_ref.at[z, :, at.x, at.core, low]
            steps.append(send(part, part, a_sem, k, at.at_x(d)))
            part = all_ref.at[z, at.y, :, at.core, high]
            steps.append(send(part, part, b_sem, k, at.at_y(d)))
        second.append(steps)
    for j in range(nz):
        z = lax.rem(at.z + nz - j, nz)
        for copy in second[j]:
            copy.wait_recv()
        part = all_ref.at[z, :, :, at.core]
        last.append(send(part, part, core_sem, j, at.sibling()))
    for copy in waits + last:
        copy.wait()
    for copy in taps + planes + sum(first + second, []):
        copy.wait_send()


def reduce_kernel(
    wide,
    batch,
    lead_step,
    span,
    room,
    deep,
    per,
    table_ref,
    grad_ref,
    gsm_ref,
    o_ref,
    g_ref,
    oz_ref,
    gz_ref,
    share_ref,
    total_ref,
    part_ref,
    send_ref,
    core_ref,
    acc_ref,
    sa_ref,
    sb_ref,
    ra_ref,
    rb_ref,
    a_ref,
    b_ref,
    sa2_ref,
    sb2_ref,
    ra2_ref,
    rb2_ref,
    own_ref,
    sz_ref,
    rz_ref,
    sum_ref,
    back_ref,
    got_ref,
    tile_ref,
    tiles_ref,
    tap_ref,
    core_sem,
    a_sem,
    b_sem,
    z_sem,
    o_sem,
    g_sem,
    tap_sem,
    all_sem,
    fetch_sem,
):
    at = Place(wide, batch)
    nz, ns, half = at.nz, at.ns, at.half
    count = nz * at.nb
    cut = room * 32 // 2
    link = send_ref.dtype
    got_ref[...] = jnp.zeros(got_ref.shape, f32)

    fetch = []
    for k, core in enumerate((1 - at.core, at.core)):
        fetch.append(
            pltpu.make_async_copy(grad_ref.at[:, :, :, core], part_ref.at[k], fetch_sem.at[k])
        )
        fetch[k].start()
    greet([at.at_all(d) for d in range(1, count)])
    waits = []

    def exchange(src, dst, sems, steps):
        for d in steps:
            waits.append(send(src.at[lax.rem(at.z + d, nz)], dst.at[at.z], sems, d - 1, at.at_z(d)))

    exchange(o_ref, oz_ref, o_sem, range(1, nz))
    exchange(g_ref, gz_ref, g_sem, range(1, nz))
    oz_ref[at.z] = o_ref[at.z]
    gz_ref[at.z] = g_ref[at.z]

    pieces = [lax.rem(at.z + j, nz) for j in (*range(1, nz), 0)]
    cores, first, second, stage = [], [], [], []
    fetch[0].wait()
    for j, z in enumerate(pieces):
        send_ref[z] = part_ref[0, z].astype(link)
        cores.append(send(send_ref.at[z], core_ref.at[z], core_sem, j, at.sibling()))
    fetch[1].wait()
    for j, z in enumerate(pieces):
        cores[j].wait_recv()
        acc_ref[z] = part_ref[1, z] + core_ref[z].astype(f32)
        steps = []
        for d in range(1, ns):
            x = lax.rem(at.x + d, ns)
            y = lax.rem(at.y + d, ns)
            for o in range(ns):
                sa_ref[d - 1, z, o] = acc_ref[z, o, x, 0:cut, :].astype(link)
                sb_ref[d - 1, z, o] = acc_ref[z, y, o, cut : 2 * cut, :].astype(link)
            k = j * (ns - 1) + d - 1
            steps.append(send(sa_ref.at[d - 1, z], ra_ref.at[d - 1, z], a_sem, k, at.at_x(d)))
            steps.append(send(sb_ref.at[d - 1, z], rb_ref.at[d - 1, z], b_sem, k, at.at_y(d)))
        first.append(steps)
    for j, z in enumerate(pieces):
        for copy in first[j]:
            copy.wait_recv()
        for o in range(ns):
            va = acc_ref[z, o, at.x, 0:cut, :]
            vb = acc_ref[z, at.y, o, cut : 2 * cut, :]
            for d in range(1, ns):
                va = va + ra_ref[d - 1, z, o].astype(f32)
                vb = vb + rb_ref[d - 1, z, o].astype(f32)
            a_ref[z, o] = va
            b_ref[z, o] = vb
        steps = []
        for d in range(1, ns):
            sa2_ref[d - 1, z] = a_ref[z, lax.rem(at.y + d, ns)].astype(link)
            sb2_ref[d - 1, z] = b_ref[z, lax.rem(at.x + d, ns)].astype(link)
            k = (nz + j) * (ns - 1) + d - 1
            steps.append(send(sa2_ref.at[d - 1, z], ra2_ref.at[d - 1, z], a_sem, k, at.at_y(d)))
            steps.append(send(sb2_ref.at[d - 1, z], rb2_ref.at[d - 1, z], b_sem, k, at.at_x(d)))
        second.append(steps)
    for j, z in enumerate(pieces):
        for copy in second[j]:
            copy.wait_recv()
        va = a_ref[z, at.y]
        vb = b_ref[z, at.x]
        for d in range(1, ns):
            va = va + ra2_ref[d - 1, z].astype(f32)
            vb = vb + rb2_ref[d - 1, z].astype(f32)
        own_ref[z, 0:cut, :] = va
        own_ref[z, cut : 2 * cut, :] = vb
        if j < nz - 1:
            sz_ref[z, 0:cut, :] = va.astype(link)
            sz_ref[z, cut : 2 * cut, :] = vb.astype(link)
            stage.append(send(sz_ref.at[z], rz_ref.at[j], z_sem, j, at.at_z(j + 1)))
    for copy in stage:
        copy.wait()
    for copy in cores + sum(first + second, []):
        copy.wait_send()
    total = own_ref[at.z]
    for d in range(1, nz):
        total = total + rz_ref[d - 1].astype(f32)
    sum_ref[...] = total * (1.0 / NKER)

    picks = half * deep * span
    weights = picks + room * half * deep
    square = jnp.zeros((1, 128), f32)
    for k in range(room):
        value = sum_ref[32 * k : 32 * k + 32, :]
        square = square + table_ref[weights + k] * jnp.sum(value * value, axis=0, keepdims=True)
    tile_ref[0:2, :] = gsm_ref[...]
    tile_ref[2:3, :] = square
    tile_ref[3:8, :] = jnp.zeros((5, 128), f32)
    tells = [
        send(tile_ref, tiles_ref.at[at.me], all_sem, d - 1, at.at_all(d)) for d in range(1, count)
    ]
    tiles_ref[at.me] = tile_ref[...]

    @pl.loop(0, half)
    def _(q):
        for s in range(deep):
            value = jnp.zeros((32, 128), f32)
            for k in range(room):
                value = value + (
                    table_ref[picks + k * half * deep + q * deep + s]
                    * sum_ref[32 * k : 32 * k + 32, :]
                )
            back_ref[q, s] = value

    backs = swap_cells(at, deep, -1, back_ref, got_ref, tap_sem)
    for copy in tells:
        copy.wait()
    tile = jnp.zeros((8, 128), f32)
    for d in range(count):
        tile = tile + tiles_ref[d]
    total_ref[...] = tile
    for copy in backs:
        copy.wait()

    @pl.loop(0, span)
    def _(t):
        value = jnp.zeros((32, 128), f32)
        for q in range(half):
            for s in range(deep):
                value = value + table_ref[(q * deep + s) * span + t] * got_ref[q, s]
        tap_ref[pl.ds(pl.multiple_of(32 * t, 32), 32), :] = value

    held = share_ref.shape[0]
    share_ref[...] = tap_ref[pl.ds(lax.rem(at.me * lead_step, 32), held), :]
    for copy in waits:
        copy.wait()


def finish_kernel(
    per,
    total_ref,
    share_ref,
    o_ref,
    g_ref,
    w_ref,
    m_ref,
    v_ref,
    sw_ref,
    sm_ref,
    sv_ref,
    out_ref,
    gser_ref,
    norm_ref,
    nw_ref,
    nm_ref,
    nv_ref,
    nsw_ref,
    nsm_ref,
    nsv_ref,
):
    small = total_ref[0:2, :]
    lanes = jnp.sum(total_ref[2:3, :], axis=1, keepdims=True)
    squares = jnp.sum(jnp.sum(small * small, axis=0, keepdims=True), axis=1, keepdims=True)
    norm = jnp.sqrt(lanes + squares)
    norm_ref[...] = norm
    factor = jnp.minimum(1.0, clip_norm / (norm + 1e-06))
    nsw_ref[...], nsm_ref[...], nsv_ref[...] = adam_update(
        sw_ref[...], small * factor, sm_ref[...], sv_ref[...]
    )
    nw_ref[...], nm_ref[...], nv_ref[...] = adam_update(
        w_ref[...], share_ref[...] * factor, m_ref[...], v_ref[...]
    )
    shard = out_ref.shape[2]
    for src, dst in ((o_ref, out_ref), (g_ref, gser_ref)):
        for z in range(src.shape[0]):
            both = src[z].astype(f32).T
            dst[per * z] = both[0:C, 0:shard].astype(bf16)
            if per == 2:
                dst[per * z + 1] = both[C:, 0:shard].astype(bf16)


def block_kernel(
    L,
    per,
    row_of,
    freq_ref,
    len_ref,
    x_ref,
    cot_ref,
    all_ref,
    small_ref,
    out_ref,
    gser_ref,
    grad_ref,
    gsm_ref,
    gm1_ref,
    gm2_ref,
    w1_ref,
    w2_ref,
    w1s_ref,
    w2s_ref,
    w1r_ref,
    w2r_ref,
    trig_ref,
    res_ref,
    mg_ref,
    gin_ref,
    xf_ref,
    af_ref,
    pk_ref,
    xs_ref,
    s1_ref,
    s2_ref,
    p2_ref,
    p1_ref,
    r_ref,
    act_ref,
    slope_ref,
    br_ref,
    wv_ref,
    gw_ref,
    gb_ref,
):
    slabs = x_ref.shape[0]
    shard = L // slabs
    lanes = lane_low
    third = L // 3
    PS, PP, PK = 88, 176, 16

    def swap(v):
        return pltpu.roll(v, C, 1)

    def span_of(t, n, align=8):
        assert t % align == 0
        return slice(t, t + n)

    def half_sum(v):
        low = lanes(v.shape[0])
        a = jnp.sum(jnp.where(low, v, 0.0), axis=1, keepdims=True)
        b = jnp.sum(jnp.where(low, 0.0, v), axis=1, keepdims=True)
        return jnp.where(low, a, b)

    def fold(v):
        return jnp.sum(v.reshape(v.shape[0] // 8, 8, 128), axis=0)

    def split(v):
        hi = v.astype(bf16)
        rest = v - hi.astype(f32)
        mid = rest.astype(bf16)
        return hi, mid, (rest - mid.astype(f32)).astype(bf16)

    raw = [freq_ref[j] for j in range(K)]
    ranks = [sum((raw[j] > raw[k]).astype(jnp.int32) for k in range(K)) for j in range(K)]
    freqs = [sum(jnp.where(ranks[j] == k, raw[j], 0) for j in range(K)) for k in range(K)]
    order = (1, 2, 3, 0, 4)
    periods = [L // freqs[j] for j in order]
    freqs = [freqs[j] for j in order]
    tiles = [(3, 3), (3, 3), (3, 3), (3, 1), (1, 3)]

    for ref, pad in ((s1_ref, PS), (s2_ref, PS), (p1_ref, PP), (p2_ref, PP)):
        for b in range(ref.shape[0]):
            ref[b, 0:pad, :] = jnp.zeros((pad, 128), f32)
            ref[b, L + pad : L + 2 * pad, :] = jnp.zeros((pad, 128), f32)
    pk_ref[0:PK, :] = jnp.zeros((PK, 128), f32)
    pk_ref[L + PK : L + 2 * PK, :] = jnp.zeros((PK, 128), f32)
    gm1_ref[...] = jnp.zeros((W, W), f32)
    gm2_ref[...] = jnp.zeros((W, W), f32)
    gb_ref[...] = jnp.zeros((4, 8, 128), f32)
    gw_ref[...] = jnp.zeros((K, 8, 128), f32)

    r = lax.broadcasted_iota(jnp.int32, (128, 128), 0)
    c = lax.broadcasted_iota(jnp.int32, (128, 128), 1)
    ahead = jnp.where(c == r // 64 * 64 + r % 2 * 32 + r % 64 // 2, 1.0, 0.0).astype(bf16)
    low32 = lanes(32)

    def cell_rows(block, a, b):
        cell = block * CELLS + (OFFS[b] + HALF) * SPAN + OFFS[a] + HALF
        return slice(int(row_of[cell]) * 32, int(row_of[cell]) * 32 + 32)

    def lay_out(block, raw_w, mat, rws):
        raw_w[11 * C :, :] = jnp.zeros((C, W), bf16)
        for a in range(11):
            for q in range(6):
                one = all_ref[cell_rows(block, a, 2 * q), :].astype(f32)
                two = jnp.zeros((32, 128), f32)
                if q < 5:
                    two = all_ref[cell_rows(block, a, 2 * q + 1), :].astype(f32)
                cut = slice(128 * q, 128 * q + 128)
                raw_w[64 * a : 64 * a + 32, cut] = jnp.where(low32, one, swap(two)).astype(bf16)
                raw_w[64 * a + 32 : 64 * a + 64, cut] = jnp.where(low32, swap(one), two).astype(bf16)
        for i in range(6):
            cut = slice(128 * i, 128 * i + 128)
            v = jnp.dot(ahead, raw_w[cut, :], preferred_element_type=f32)
            v16 = v.astype(bf16)
            mat[cut, :] = v16
            rws[128 * i : 128 * i + 64, :] = v16[64:128]
            rws[128 * i + 64 : 128 * i + 128, :] = v16[0:64]
            for q in range(6):
                at = slice(128 * q, 128 * q + 128)
                raw_w[cut, at] = swap(v[:, at]).astype(bf16)

    own_first = lax.axis_index("wide") * per
    own = jnp.where(lanes(1), len_ref[own_first], len_ref[own_first + 1] if per == 2 else 0)

    def valid(t, n):
        return t + lax.broadcasted_iota(jnp.int32, (n, 128), 0) < own

    for z in range(slabs):
        res_ref[shard * z : shard * z + shard, :] = x_ref[z].astype(f32)[0:shard]
        gin_ref[shard * z : shard * z + shard, :] = cot_ref[z].astype(f32)[0:shard]

    for t in range(0, L, 176):
        v = jnp.where(valid(t, 176), res_ref[t : t + 176, :], 0.0)
        mg_ref[t : t + 176, :] = v
        pk_ref[PK + t : PK + t + 176, :] = v

    def pairs(i, dst):
        n = third + 16
        a = pk_ref[span_of(PK - 8 + third * i, n), :]
        b = pk_ref[PK - 7 + third * i : PK - 7 + third * i + n, :]
        low = lanes(n)
        dst[0, span_of(third * i, n), :] = jnp.where(low, a, swap(b))
        dst[1, span_of(third * i, n), :] = jnp.where(low, swap(a), b)

    def within(t, n, p):
        at = t + lax.broadcasted_iota(jnp.int32, (n, 128), 0)
        inv = 1.0 / jnp.full((1, 128), p, jnp.int32).astype(f32)
        return at - ((at.astype(f32) + 0.5) * inv).astype(jnp.int32) * p

    def build_cols(i, k, src, dst):
        p, nk = periods[k], tiles[k][0]
        n = 176
        for half in range(third // n):
            t = third * i + n * half
            wi = within(t, n, p) + jnp.where(lanes(n), 0, 1)
            for q in range(2 * nk):
                base = BASES[q]
                keep = wi >= -base if base < 0 else wi < p - base
                for s in range(2):
                    v = src[s, 8 + base + t : 8 + base + t + n, :]
                    dst[span_of(s * L + t, n, 16), 128 * q : 128 * q + 128] = jnp.where(
                        keep, v, 0.0
                    ).astype(bf16)

    def build_rows(i, k, src, dst):
        p, nr = periods[k], tiles[k][1]
        n = 176
        low = lanes(n)
        for half in range(third // n):
            t = third * i + n * half
            for q in range(2 * nr):
                one = pl.ds(PP + jnp.clip(t - OFFS[2 * q] * p, -n, L), n)
                a, b = src[0, one, :], src[1, one, :]
                if q < 5:
                    two = pl.ds(PP + jnp.clip(t - OFFS[2 * q + 1] * p, -n, L), n)
                    c, d = src[0, two, :], src[1, two, :]
                else:
                    c = d = jnp.zeros((n, 128), f32)
                cut = slice(128 * q, 128 * q + 128)
                dst[span_of(t, n, 16), cut] = jnp.where(low, a, d).astype(bf16)
                dst[span_of(L + t, n, 16), cut] = jnp.where(low, b, c).astype(bf16)

    def sum_rows(t, n, k, src):
        p, nr = periods[k], tiles[k][1]
        sums = [jnp.zeros((n, 128), f32)] * 2
        for b in range(min(4 * nr, 11)):
            off = PS + jnp.clip(OFFS[b] * p + t, -n, L)
            sums[b % 2] = sums[b % 2] + src[b, pl.ds(off, n), :]
        return sums[0] + swap(sums[1])

    def sum_cols(t, n, k, src):
        p, nk = periods[k], tiles[k][0]
        wi = within(t, n, p)
        sums = [jnp.zeros((n, 128), f32)] * 2
        for b in range(min(4 * nk, 11)):
            d = OFFS[b]
            v = src[b, PS - d + t : PS - d + t + n, :]
            if d < 0:
                v = jnp.where(wi < p + d, v, 0.0)
            elif d > 0:
                v = jnp.where(wi >= d, v, 0.0)
            sums[b % 2] = sums[b % 2] + v
        return sums[0] + swap(sums[1])

    def twice(i, first):
        v = small_ref[i : i + 1, :]
        return jnp.where(lanes(1) == first, v, swap(v))

    bias_one, bias_two = twice(0, True), twice(0, False)
    gain, shift = twice(1, True), twice(1, False)
    NS = 88

    def hidden(i, k):
        for j in range(third // NS):
            t = third * i + NS * j
            slope_ref[k, span_of(t, NS), :] = sum_rows(t, NS, k, s1_ref) + bias_one

    def activate(i, k):
        n = 176
        for t in range(third * i, third * i + third, n):
            v = slope_ref[k, span_of(t, n), :]
            cdf = 0.5 * (1.0 + lax.erf(v * inv_root_two))
            slope_ref[k, span_of(t, n), :] = cdf + v * jnp.exp(-0.5 * v * v) * inv_root_tau
            act = (v * cdf).astype(bf16)
            act_ref[k, span_of(t, n, 16), :] = act
            pk_ref[span_of(PK + t, n), :] = act.astype(f32)

    def branch(i, k):
        for j in range(third // NS):
            t = third * i + NS * j
            br_ref[k, span_of(t, NS), :] = sum_rows(t, NS, k, s2_ref) + bias_two

    def merge(i, k):
        wk = wv_ref[k : k + 1, :]
        at = span_of(third * i, third)
        mg_ref[at, :] += wk * br_ref[k, at, :]

    def rebuild(i, k):
        v = act_ref[k, span_of(third * i, third, 16), :].astype(f32)
        pk_ref[span_of(PK + third * i, third), :] = v

    def spread_branch(i, k):
        wk = wv_ref[k : k + 1, :]
        sum_w = sum_b = jnp.zeros((8, 128), f32)
        for j in range(third // NS):
            t = third * i + NS * j
            gm = mg_ref[span_of(t, NS), :]
            sum_w = sum_w + fold(gm * br_ref[k, span_of(t, NS), :])
            g = (wk * gm).astype(bf16).astype(f32)
            sum_b = sum_b + fold(g)
            p2_ref[0, span_of(PP + t, NS), :] = g
            p2_ref[1, span_of(PP + t, NS), :] = swap(g)
        gw_ref[k] += sum_w
        gb_ref[1] += sum_b

    def spread_hidden(i, k):
        sum_b = jnp.zeros((8, 128), f32)
        for j in range(third // NS):
            t = third * i + NS * j
            g = sum_cols(t, NS, k, s1_ref) * slope_ref[k, span_of(t, NS), :]
            g = g.astype(bf16).astype(f32)
            sum_b = sum_b + fold(g)
            p1_ref[0, span_of(PP + t, NS), :] = g
            p1_ref[1, span_of(PP + t, NS), :] = swap(g)
        gb_ref[0] += sum_b

    def collect(i, k):
        for j in range(third // NS):
            t = third * i + NS * j
            gin_ref[span_of(t, NS), :] += sum_cols(t, NS, k, s2_ref)

    def to_slots(dst, n, d0, d1):
        low = lanes(L)
        for h in range(2):
            a = d0[:, 128 * h : 128 * h + 128]
            b = d1[:, 128 * h : 128 * h + 128]
            dst[4 * n + 2 * h, PS : PS + L, :] = jnp.where(low, a, b)
            if 4 * n + 2 * h + 1 < 11:
                dst[4 * n + 2 * h + 1, PS : PS + L, :] = jnp.where(low, b, a)

    def mm_forward(i, k, src, w, ws, dst):
        if i >= tiles[k][1]:
            return
        depth, cut = slice(0, 256 * tiles[k][0]), slice(256 * i, 256 * i + 256)
        d0 = jnp.dot(src[0:L, depth], w[depth, cut], preferred_element_type=f32)
        d1 = jnp.dot(src[L : 2 * L, depth], ws[depth, cut], preferred_element_type=f32)
        to_slots(dst, i, d0, d1)

    def mm_adjoint(i, k, src, w, wr, dst):
        if i >= tiles[k][0]:
            return
        depth, cut = slice(0, 256 * tiles[k][1]), slice(256 * i, 256 * i + 256)
        dims = (((1,), (1,)), ((), ()))
        d0 = lax.dot_general(src[0:L, depth], w[cut, depth], dims, preferred_element_type=f32)
        d1 = lax.dot_general(src[L : 2 * L, depth], wr[cut, depth], dims, preferred_element_type=f32)
        to_slots(dst, i, d0, d1)

    def mm_weights(i, k, left, right, gm):
        if i >= tiles[k][0]:
            return
        cut, wide_cut = slice(256 * i, 256 * i + 256), slice(0, 256 * tiles[k][1])
        gm[cut, wide_cut] += lax.dot_general(
            left[:, cut], right[:, wide_cut], (((0,), (0,)), ((), ())), preferred_element_type=f32
        )

    blocks = []

    def block(*work):
        blocks.append(work)

        @pl.when(raw[len(blocks) % K] + len(blocks) > 0)
        def _():
            for item in work:
                for i in range(3):
                    item[0](i, *item[1:])

    def once(i, f, *rest):
        if i == 0:
            f(*rest)

    block((once, lay_out, 0, w1s_ref, w1_ref, w1r_ref), (pairs, xf_ref))

    lane = lax.broadcasted_iota(jnp.int32, (1, 128), 1)
    turn = jnp.zeros((1, 128), jnp.int32)
    for j in range(K):
        turn = jnp.where(lane % 8 == j, freqs[j], turn)

    def waves(i):
        t = i * third + lax.broadcasted_iota(jnp.int32, (third, 128), 0)
        turns = t * turn
        whole = ((turns.astype(f32) + 0.5) * (1.0 / L)).astype(jnp.int32)
        angle = (turns - whole * L).astype(f32) * (2.0 * math.pi / L)
        angle = jnp.where(lane < 8, angle, angle - 0.5 * math.pi)
        wave = jnp.where((lane < 16) & (lane % 8 < K), jnp.cos(angle), 0.0)
        hi, mid, lo = (v.astype(f32) for v in split(wave))
        trig_ref[span_of(i * third, third, 16), :] = (
            hi + pltpu.roll(mid, 16, 1) + pltpu.roll(lo, 32, 1)
        ).astype(bf16)

    block(
        (build_cols, 0, xf_ref, xs_ref),
        (mm_forward, 0, xs_ref, w1_ref, w1s_ref, s1_ref),
        (waves,),
    )
    block((once, lay_out, 1, w2s_ref, w2_ref, w2r_ref))

    spec = lax.dot_general(
        trig_ref[...],
        mg_ref[...].astype(bf16),
        (((0,), (0,)), ((), ())),
        preferred_element_type=f32,
    )
    spec = (spec[0:16] + spec[16:32] + spec[32:48]) * (2.0 / L)
    real, imag = spec[0:8], spec[8:16]
    magnitude = jnp.sqrt(real * real + imag * imag + 1.0)
    mean_mag = half_sum(magnitude) * (1.0 / C)
    live = lax.broadcasted_iota(jnp.int32, (8, 128), 0) < K
    top = jnp.max(jnp.where(live, mean_mag, -1e30), axis=0, keepdims=True)
    ex = jnp.where(live, jnp.exp(mean_mag - top), 0.0)
    weights = ex / jnp.sum(ex, axis=0, keepdims=True)
    wv_ref[...] = weights

    block((hidden, 0), (activate, 0))
    for k in range(K):
        if k + 1 < K:
            work = [
                (build_cols, k + 1, xf_ref, xs_ref),
                (mm_forward, k + 1, xs_ref, w1_ref, w1s_ref, s1_ref),
            ]
            if k > 0:
                work = [(branch, k - 1)] + work + [(merge, k - 1)]
            block(*work)
        work = [
            (pairs, af_ref),
            (build_cols, k, af_ref, xs_ref),
            (mm_forward, k, xs_ref, w2_ref, w2s_ref, s2_ref),
        ]
        if k + 1 < K:
            work = [(hidden, k + 1)] + work + [(activate, k + 1)]
        else:
            work = [(branch, k - 1)] + work + [(merge, k - 1)]
        block(*work)

    same = (
        lax.broadcasted_iota(jnp.int32, (384, 128), 0) % 128 // C
        == lax.broadcasted_iota(jnp.int32, (384, 128), 1) // C
    )
    ones = jnp.where(same, 1.0 / C, 0.0).astype(bf16)

    def half_mean(v):
        return jnp.dot(jnp.concatenate(split(v), axis=1), ones, preferred_element_type=f32)

    def normalise(i):
        at = span_of(i * third, third)
        m = mg_ref[at, :]
        ok = valid(i * third, third)
        centered = m - half_mean(m)
        inverse = lax.rsqrt(half_mean(centered * centered) + norm_eps)
        normed = centered * inverse
        res_ref[at, :] = jnp.where(ok, normed * gain + shift, 0.0)
        g_out = jnp.where(ok, gin_ref[at, :], 0.0)
        gb_ref[2] += fold(g_out * normed)
        gb_ref[3] += fold(g_out)
        g_norm = g_out * gain
        gm = inverse * (g_norm - half_mean(g_norm) - normed * half_mean(g_norm * normed))
        mg_ref[at, :] = gm
        gin_ref[at, :] = gm

    block((branch, K - 1), (merge, K - 1), (normalise,), (spread_branch, 0))

    def to_slabs(dst):
        for z in range(slabs):
            v = res_ref[shard * z : shard * z + shard, :]
            v = jnp.concatenate([v, jnp.zeros((dst.shape[1] - shard, 128), f32)], axis=0)
            dst[z] = v.astype(bf16)

    to_slabs(out_ref)

    for k in range(K):
        work = [
            (build_rows, k, p2_ref, r_ref),
            (mm_adjoint, k, r_ref, w2_ref, w2r_ref, s1_ref),
            (rebuild, k),
        ]
        if k > 0:
            work.append((collect, k - 1))
        block(*work)
        work = [
            (pairs, af_ref),
            (build_cols, k, af_ref, xs_ref),
            (mm_weights, k, xs_ref, r_ref, gm2_ref),
            (spread_hidden, k),
        ]
        if k + 1 < K:
            work.append((spread_branch, k + 1))
        block(*work)
        block(
            (build_rows, k, p1_ref, r_ref),
            (mm_adjoint, k, r_ref, w1_ref, w1r_ref, s2_ref),
        )
        block(
            (build_cols, k, xf_ref, xs_ref),
            (mm_weights, k, xs_ref, r_ref, gm1_ref),
        )

    row8 = lax.broadcasted_iota(jnp.int32, (8, 128), 0)
    g_weights = jnp.zeros((8, 128), f32)
    for j in range(K):
        total = jnp.sum(gw_ref[j], axis=0, keepdims=True)
        g_weights = jnp.where(row8 == j, total, g_weights)
    g_weights = half_sum(g_weights)
    weights = wv_ref[...]
    g_score = weights * (g_weights - jnp.sum(weights * g_weights, axis=0, keepdims=True))
    coeff = g_score / (magnitude * C) * (2.0 / L)
    c_hi, c_lo, _ = split(jnp.concatenate([coeff * real, coeff * imag], axis=0))
    c_all = jnp.concatenate([c_hi, c_hi, c_hi, jnp.zeros((80, 128), bf16)], axis=0)
    c_low = jnp.concatenate([c_lo, jnp.zeros((112, 128), bf16)], axis=0)

    def finish(i):
        at = span_of(i * third, third)
        t = trig_ref[span_of(i * third, third, 16), :]
        g = (
            gin_ref[at, :]
            + jnp.dot(t, c_all, preferred_element_type=f32)
            + jnp.dot(t, c_low, preferred_element_type=f32)
        )
        res_ref[at, :] = jnp.where(valid(i * third, third), g, 0.0)

    block((collect, K - 1), (finish,))
    to_slabs(gser_ref)

    sums = []
    for q in range(4):
        total = jnp.sum(gb_ref[q], axis=0, keepdims=True)
        sums.append(total + swap(total))
    gsm_ref[0:1, :] = jnp.where(lanes(1), sums[0], sums[1])
    gsm_ref[1:2, :] = jnp.where(lanes(1), sums[2], sums[3])

    used = set(int(v) for v in row_of)
    for v in range(grad_ref.shape[0] // 32):
        if v not in used:
            grad_ref[32 * v : 32 * v + 32, :] = jnp.zeros((32, 128), f32)
    back = jnp.where(r == c // 64 * 64 + c % 2 * 32 + c % 64 // 2, 1.0, 0.0).astype(bf16)
    back = jnp.concatenate([back, back, back], axis=1)
    for block, mat in enumerate((gm1_ref, gm2_ref)):
        for i in range(6):
            v = jnp.concatenate(split(mat[128 * i : 128 * i + 128, :]), axis=0)
            v = jnp.dot(back, v, preferred_element_type=f32)
            for a in (2 * i, 2 * i + 1):
                if a == 11:
                    continue
                first = 64 * (a % 2)
                for q in range(6):
                    even = v[first : first + 32, 128 * q : 128 * q + 128]
                    odd = v[first + 32 : first + 64, 128 * q : 128 * q + 128]
                    grad_ref[cell_rows(block, a, 2 * q), :] = jnp.where(low32, even, swap(odd))
                    if q < 5:
                        grad_ref[cell_rows(block, a, 2 * q + 1), :] = jnp.where(
                            low32, swap(even), odd
                        )


vm = pl.BlockSpec(memory_space=pltpu.VMEM)
sm = pl.BlockSpec(memory_space=pltpu.SMEM)
sds = jax.ShapeDtypeStruct


def run_block(x, cot, lens, freqs, cells, small, per, row_of, L):
    return pl.pallas_call(
        functools.partial(block_kernel, L, per, row_of),
        out_shape=(
            sds(x.shape, bf16),
            sds(x.shape, bf16),
            sds(cells.shape, f32),
            sds((2, 128), f32),
        ),
        in_specs=[sm, sm, vm, vm, vm, vm],
        out_specs=(vm,) * 4,
        scratch_shapes=[
            pltpu.VMEM((W, W), f32),
            pltpu.VMEM((W, W), f32),
            pltpu.VMEM((W, W), bf16),
            pltpu.VMEM((W, W), bf16),
            pltpu.VMEM((W, W), bf16),
            pltpu.VMEM((W, W), bf16),
            pltpu.VMEM((W, W), bf16),
            pltpu.VMEM((W, W), bf16),
            pltpu.VMEM((L, 128), bf16),
            pltpu.VMEM((L, 128), f32),
            pltpu.VMEM((L, 128), f32),
            pltpu.VMEM((L, 128), f32),
            pltpu.VMEM((2, L + 16, 128), f32),
            pltpu.VMEM((2, L + 16, 128), f32),
            pltpu.VMEM((L + 32, 128), f32),
            pltpu.VMEM((2 * L, W), bf16),
            pltpu.VMEM((12, L + 176, 128), f32),
            pltpu.VMEM((12, L + 176, 128), f32),
            pltpu.VMEM((2, L + 352, 128), f32),
            pltpu.VMEM((2, L + 352, 128), f32),
            pltpu.VMEM((2 * L, W), bf16),
            pltpu.VMEM((K, L, 128), bf16),
            pltpu.VMEM((K, L, 128), f32),
            pltpu.VMEM((K, L, 128), f32),
            pltpu.VMEM((8, 128), f32),
            pltpu.VMEM((K, 8, 128), f32),
            pltpu.VMEM((4, 8, 128), f32),
        ],
        compiler_params=pltpu.CompilerParams(vmem_limit_bytes=63 << 20),
        name="block",
    )(freqs, lens, x, cot, cells, small)


def adam_update(param, grad, first, second):
    first_new = beta_one * first + (1.0 - beta_one) * grad
    second_new = beta_two * second + (1.0 - beta_two) * grad * grad
    first_hat = first_new / (1.0 - beta_one**STEP)
    second_hat = second_new / (1.0 - beta_two**STEP)
    param_new = param - learn_rate * (
        first_hat / (jnp.sqrt(second_hat) + adam_eps) + weight_decay * param
    )
    return (param_new, first_new, second_new)


def local(series, lengths, freqs, cotangent, kernels, kernel_m, kernel_v, small, small_m, small_v):
    wide = lax.axis_size("wide")
    batch = lax.axis_size("batch")
    count = wide * batch
    half, sides = count // 2, math.isqrt(batch // 2)
    me = lax.axis_index(("wide", "batch"))
    span, room, deep, spread, pick, weight, row_of = plan(wide, batch)
    share = kernels.shape[0]
    shard = series.shape[1]
    per = series.shape[0] // wide
    slab = -(-shard // 16) * 16

    tables = np.concatenate([v.reshape(count, -1) for v in (spread, pick, weight)], axis=1)
    table = lax.dynamic_index_in_dim(jnp.asarray(tables), me, 0, keepdims=False)
    aligned = share % 128 == 0
    lead = me * share % TAP

    def to_rows(v):
        if aligned:
            return v.reshape(share // 128, 128)
        wide_v = jnp.zeros((span * TAP,), f32)
        return lax.dynamic_update_slice_in_dim(wide_v, v, lead, 0).reshape(span * 32, 128)

    def from_rows(v):
        if aligned:
            return v.reshape(share)
        return lax.dynamic_slice_in_dim(v.reshape(-1), lead, share, 0)

    lead_step = share // 128 if aligned else 0
    params = pltpu.CompilerParams
    static = (wide, batch, lead_step, span, room, deep, per)
    dma = pltpu.SemaphoreType.DMA
    cell_shape = (wide, sides, sides, 2, room * 32, 128)
    slab_shape = (wide, slab, 128)
    exchange = (half, deep, 32, 128)
    taps_rows = -(-(span * 32 + 32) // 8) * 8
    taps = to_rows(kernels)
    held = taps.shape[0]

    x, cot, cells = pl.pallas_call(
        functools.partial(gather_kernel, *static),
        out_shape=(sds(slab_shape, bf16), sds(slab_shape, bf16), sds(cell_shape, bf16)),
        in_specs=[sm, vm, vm, vm],
        out_specs=(vm,) * 3,
        scratch_shapes=[
            pltpu.VMEM((taps_rows, 128), f32),
            pltpu.VMEM(exchange, f32),
            pltpu.VMEM(exchange, f32),
            pltpu.VMEM(slab_shape, bf16),
            pltpu.VMEM(slab_shape, bf16),
            dma((2, half - 1)),
            dma((2, wide - 1)),
            dma((2, wide - 1)),
            dma((2, wide - 1)),
            dma((2, 2 * wide * (sides - 1))),
            dma((2, 2 * wide * (sides - 1))),
            dma((2, wide)),
        ],
        compiler_params=params(
            collective_id=0, has_side_effects=True, vmem_limit_bytes=62 << 20
        ),
        name="gather",
    )(table, taps, series.transpose(0, 2, 1), cotangent.transpose(0, 2, 1))

    small_rows = small.reshape(2, 128)
    out, gser, grads, gsm = run_block(
        x, cot, lengths, freqs, cells.reshape(-1, 128), small_rows, per, row_of, shard * wide
    )

    link = bf16
    cut = room * 16
    out, gser, grad_share, total = pl.pallas_call(
        functools.partial(reduce_kernel, *static),
        out_shape=(
            sds(slab_shape, bf16),
            sds(slab_shape, bf16),
            sds((held, 128), f32),
            sds((8, 128), f32),
        ),
        in_specs=[sm, pl.BlockSpec(memory_space=pl.ANY), vm, vm, vm],
        out_specs=(vm,) * 4,
        scratch_shapes=[
            pltpu.VMEM((2, wide, sides, sides, room * 32, 128), f32),
            pltpu.VMEM((wide, sides, sides, room * 32, 128), link),
            pltpu.VMEM((wide, sides, sides, room * 32, 128), link),
            pltpu.VMEM((wide, sides, sides, room * 32, 128), f32),
            pltpu.VMEM((sides - 1, wide, sides, cut, 128), link),
            pltpu.VMEM((sides - 1, wide, sides, cut, 128), link),
            pltpu.VMEM((sides - 1, wide, sides, cut, 128), link),
            pltpu.VMEM((sides - 1, wide, sides, cut, 128), link),
            pltpu.VMEM((wide, sides, cut, 128), f32),
            pltpu.VMEM((wide, sides, cut, 128), f32),
            pltpu.VMEM((sides - 1, wide, cut, 128), link),
            pltpu.VMEM((sides - 1, wide, cut, 128), link),
            pltpu.VMEM((sides - 1, wide, cut, 128), link),
            pltpu.VMEM((sides - 1, wide, cut, 128), link),
            pltpu.VMEM((wide, room * 32, 128), f32),
            pltpu.VMEM((wide, room * 32, 128), link),
            pltpu.VMEM((wide - 1, room * 32, 128), link),
            pltpu.VMEM((room * 32, 128), f32),
            pltpu.VMEM(exchange, f32),
            pltpu.VMEM(exchange, f32),
            pltpu.VMEM((8, 128), f32),
            pltpu.VMEM((count, 8, 128), f32),
            pltpu.VMEM((taps_rows, 128), f32),
            dma((2, wide)),
            dma((2, 2 * wide * (sides - 1))),
            dma((2, 2 * wide * (sides - 1))),
            dma((2, wide - 1)),
            dma((2, wide - 1)),
            dma((2, wide - 1)),
            dma((2, half - 1)),
            dma((2, count - 1)),
            dma((2,)),
        ],
        compiler_params=params(
            collective_id=1, has_side_effects=True, vmem_limit_bytes=62 << 20
        ),
        name="reduce",
    )(table, grads.reshape(cell_shape), gsm, out, gser)

    turned = (series.shape[0], series.shape[2], shard)
    out, gser, norm, new_w, new_m, new_v, new_sw, new_sm, new_sv = pl.pallas_call(
        functools.partial(finish_kernel, per),
        out_shape=(
            sds(turned, bf16),
            sds(turned, bf16),
            sds((1, 1), f32),
            sds((held, 128), f32),
            sds((held, 128), f32),
            sds((held, 128), f32),
            sds((2, 128), f32),
            sds((2, 128), f32),
            sds((2, 128), f32),
        ),
        in_specs=[vm] * 10,
        out_specs=(vm,) * 9,
        compiler_params=params(vmem_limit_bytes=62 << 20),
        name="finish",
    )(
        total,
        grad_share,
        out,
        gser,
        taps,
        to_rows(kernel_m),
        to_rows(kernel_v),
        small_rows,
        small_m.reshape(2, 128),
        small_v.reshape(2, 128),
    )
    return (
        out.transpose(0, 2, 1),
        gser.transpose(0, 2, 1),
        norm.reshape(()),
        from_rows(new_w),
        from_rows(new_m),
        from_rows(new_v),
        new_sw.reshape(-1),
        new_sm.reshape(-1),
        new_sv.reshape(-1),
    )


def solution(mesh):
    placed = (
        P("batch", "wide", None),
        P("batch"),
        P(),
        P("batch", "wide", None),
        P(("wide", "batch")),
        P(("wide", "batch")),
        P(("wide", "batch")),
        P(),
        P(),
        P(),
    )
    return jax.shard_map(
        local,
        mesh=mesh,
        in_specs=placed,
        out_specs=(
            P("batch", "wide", None),
            P("batch", "wide", None),
            P(),
            P(("wide", "batch")),
            P(("wide", "batch")),
            P(("wide", "batch")),
            P(),
            P(),
            P(),
        ),
        check_vma=False,
    )
```

```python
import functools
import math

import jax
import jax.numpy as jnp
import numpy as np
from jax import lax
from jax.experimental import pallas as pl
from jax.experimental.pallas import tpu as pltpu
from jax.sharding import PartitionSpec as P

C = 64
K = 5
NKER = 6
STEP = 10
SPAN = 11
HALF = 5
TAPS = 286
CELLS = SPAN * SPAN
TAP = C * C
DEEP_STEPS = 1

beta_one = 0.9
beta_two = 0.999
learn_rate = 0.1
weight_decay = 0.01
adam_eps = 1e-08
clip_norm = 1.0
norm_eps = 1e-05
inv_root_two = 1.0 / math.sqrt(2.0)
inv_root_tau = 1.0 / math.sqrt(2.0 * math.pi)

bf16 = jnp.bfloat16
f32 = jnp.float32
precise = lax.Precision.HIGHEST

OFFS = (-1, 0, 1, 2, -3, -2, 3, 4, -5, -4, 5, 6)
BASES = (-1, 1, -3, 3, -5, 5)
W = 12 * C


def tap_cells():
    cells = []
    for block in range(2):
        for kernel in range(NKER):
            for row_off in range(-kernel, kernel + 1):
                for col_off in range(-kernel, kernel + 1):
                    cells.append(block * CELLS + (row_off + HALF) * SPAN + col_off + HALF)
    return np.array(cells)


def is_deep(same_plane, step, batch):
    return same_plane or step % batch < DEEP_STEPS


@functools.lru_cache(None)
def plan(wide, batch):
    cells = tap_cells()
    count = wide * batch
    half = count // 2
    share = cells.size * TAP // count
    holds = [
        range(share * d // TAP, (share * (d + 1) - 1) // TAP + 1) for d in range(count)
    ]
    span = max(len(taps) for taps in holds)
    needs = [sorted(set(cells[taps.start : taps.stop].tolist())) for taps in holds]
    room = -(-CELLS // half)
    deep = 1 if max(len(need) for need in needs) <= 4 else 2
    users = [[d for d in range(count) if cell in needs[d]] for cell in range(2 * CELLS)]
    order = sorted(range(2 * CELLS), key=lambda cell: -len(users[cell]))
    for seed in range(1000):
        rng = np.random.RandomState(seed)
        owner = np.full(2 * CELLS, -1)
        filled = np.zeros(count, int)
        between = np.zeros((count, count), int)
        for cell in order:
            first = cell // CELLS * half
            free = [
                o
                for o in range(first, first + half)
                if filled[o] < room and all(
                    between[d, o] < (deep if is_deep(d // batch == o // batch, o - d, batch) else 1)
                    for d in users[cell]
                )
            ]
            if not free:
                break
            cost = [(sum(between[d, o] for d in users[cell]), filled[o]) for o in free]
            least = min(cost)
            free = [o for o, c in zip(free, cost) if c == least]
            o = free[rng.randint(len(free))]
            owner[cell] = o
            filled[o] += 1
            for d in users[cell]:
                between[d, o] += 1
        else:
            break
    place = np.zeros(2 * CELLS, int)
    filled[:] = 0
    for cell in range(2 * CELLS):
        place[cell] = filled[owner[cell]]
        filled[owner[cell]] += 1
    spread = np.zeros((count, half * deep, span), np.float32)
    pick = np.zeros((count, room, half * deep), np.float32)
    between[:] = 0
    for d, taps in enumerate(holds):
        for cell in needs[d]:
            o = owner[cell]
            slot = between[d, o]
            between[d, o] += 1
            pick[o, place[cell], d % half * deep + slot] = 1.0
            for tap in taps:
                if cells[tap] == cell:
                    spread[d, o % half * deep + slot, tap - taps.start] = 1.0
    weight = np.zeros((count, room), np.float32)
    for cell in range(2 * CELLS):
        row, col = divmod(cell % CELLS, SPAN)
        weight[owner[cell], place[cell]] = NKER - max(abs(row - HALF), abs(col - HALF))
    row_of = owner * room + place
    return span, room, deep, spread, pick, weight, row_of


MESH = pl.DeviceIdType.MESH


class Place:
    def __init__(self, wide, batch):
        self.nz, self.nb = wide, batch
        self.ns = math.isqrt(batch // 2)
        self.z = lax.axis_index("wide")
        self.b = lax.axis_index("batch")
        self.core = lax.rem(self.b, 2)
        self.x = lax.rem(self.b // 2, self.ns)
        self.y = self.b // (2 * self.ns)
        self.half = wide * batch // 2
        self.me = self.z * batch + self.b
        self.mine = lax.rem(self.me, self.half)

    def batch_of(self, y, x, core):
        return (y * self.ns + x) * 2 + core

    def at_z(self, d):
        return (lax.rem(self.z + d, self.nz), self.b)

    def at_y(self, d):
        return (self.z, self.batch_of(lax.rem(self.y + d, self.ns), self.x, self.core))

    def at_x(self, d):
        return (self.z, self.batch_of(self.y, lax.rem(self.x + d, self.ns), self.core))

    def sibling(self):
        return (self.z, self.batch_of(self.y, self.x, 1 - self.core))

    def in_half(self, dz, db):
        planes = self.nz // 2
        first = self.z // planes * planes
        z = lax.rem(self.z - first + dz, planes)
        b = lax.rem(self.b + db, self.nb)
        return z * self.nb + b, (first + z, b)

    def half_steps(self):
        return [
            (dz, db) for dz in range(self.nz // 2) for db in range(self.nb) if (dz, db) != (0, 0)
        ]

    def at_all(self, d):
        other = lax.rem(self.me + d, self.nz * self.nb)
        return (other // self.nb, lax.rem(other, self.nb))


def greet(peers):
    barrier = pltpu.get_barrier_semaphore()
    for peer in peers:
        pl.semaphore_signal(barrier, inc=1, device_id=peer, device_id_type=MESH)
    pl.semaphore_wait(barrier, len(peers))


def send(src, dst, sems, k, peer):
    copy = pltpu.make_async_remote_copy(
        src_ref=src,
        dst_ref=dst,
        send_sem=sems.at[0, k],
        recv_sem=sems.at[1, k],
        device_id=peer,
        device_id_type=MESH,
    )
    copy.start()
    return copy


def swap_cells(at, deep, way, src, dst, sems):
    copies = []
    for k, (dz, db) in enumerate(at.half_steps()):
        index, peer = at.in_half(dz, db)
        keep = pl.ds(0, deep if is_deep(dz == 0, way * db, at.nb) else 1)
        copies.append(send(src.at[index, keep], dst.at[at.mine, keep], sems, k, peer))
    dst[at.mine] = src[at.mine]
    return copies


def lane_low(rows):
    return lax.broadcasted_iota(jnp.int32, (rows, 128), 1) < C


def gather_kernel(
    wide,
    batch,
    lead_step,
    span,
    room,
    deep,
    per,
    table_ref,
    taps_ref,
    series_ref,
    cot_ref,
    x_ref,
    c_ref,
    all_ref,
    tap_ref,
    slot_ref,
    got_ref,
    xs_ref,
    cs_ref,
    tap_sem,
    x_sem,
    c_sem,
    z_sem,
    a_sem,
    b_sem,
    core_sem,
):
    at = Place(wide, batch)
    nz, ns, half = at.nz, at.ns, at.half
    shard = series_ref.shape[2]
    pad = x_ref.shape[1] - shard
    held = taps_ref.shape[0]
    got_ref[...] = jnp.zeros(got_ref.shape, f32)
    tap_ref[...] = jnp.zeros(tap_ref.shape, f32)
    tap_ref[pl.ds(lax.rem(at.me * lead_step, 32), held), :] = taps_ref[...]

    @pl.loop(0, half)
    def _(o):
        for s in range(deep):
            total = jnp.zeros((32, 128), f32)
            for t in range(span):
                total = total + (
                    table_ref[(o * deep + s) * span + t] * tap_ref[32 * t : 32 * t + 32, :]
                )
            slot_ref[o, s] = total

    greet(
        [at.in_half(*step)[1] for step in at.half_steps()] + [at.at_z(d) for d in range(1, nz)]
    )

    taps = swap_cells(at, deep, 1, slot_ref, got_ref, tap_sem)

    def pack(src, keep):
        for z in range(nz):
            first = src[per * z].astype(f32)
            second = src[per * z + 1].astype(f32) if per == 2 else jnp.zeros_like(first)
            both = jnp.concatenate([first, second], axis=0).T
            both = jnp.concatenate([both, jnp.zeros((pad, 128), f32)], axis=0)
            keep[z] = both.astype(bf16)

    waits = []

    def exchange(keep, out, sems):
        for d in range(1, nz):
            waits.append(send(keep.at[lax.rem(at.z + d, nz)], out.at[at.z], sems, d - 1, at.at_z(d)))
        out[at.z] = keep[at.z]

    pack(series_ref, xs_ref)
    exchange(xs_ref, x_ref, x_sem)
    pack(cot_ref, cs_ref)

    for copy in taps:
        copy.wait_recv()

    picks = half * deep * span
    for k in range(room):
        total = jnp.zeros((32, 128), f32)

        def add(q, total):
            for s in range(deep):
                total = total + table_ref[picks + k * half * deep + q * deep + s] * got_ref[q, s]
            return total

        total = lax.fori_loop(0, half, add, total)
        all_ref[at.z, at.y, at.x, at.core, 32 * k : 32 * k + 32, :] = (
            total * (1.0 / NKER)
        ).astype(bf16)

    cut = room * 32 // 2
    low, high = pl.ds(0, cut), pl.ds(cut, cut)
    block = all_ref.at[at.z, at.y, at.x, at.core]
    planes = [send(block, block, z_sem, d - 1, at.at_z(d)) for d in range(1, nz)]
    exchange(cs_ref, c_ref, c_sem)
    first, second, last = [], [], []
    for j in range(nz):
        z = lax.rem(at.z + nz - j, nz)
        if j > 0:
            planes[j - 1].wait_recv()
        steps = []
        for d in range(1, ns):
            k = j * (ns - 1) + d - 1
            part = all_ref.at[z, at.y, at.x, at.core, low]
            steps.append(send(part, part, a_sem, k, at.at_y(d)))
            part = all_ref.at[z, at.y, at.x, at.core, high]
            steps.append(send(part, part, b_sem, k, at.at_x(d)))
        first.append(steps)
    for j in range(nz):
        z = lax.rem(at.z + nz - j, nz)
        for copy in first[j]:
            copy.wait_recv()
        steps = []
        for d in range(1, ns):
            k = (nz + j) * (ns - 1) + d - 1
            part = all_ref.at[z, :, at.x, at.core, low]
            steps.append(send(part, part, a_sem, k, at.at_x(d)))
            part = all_ref.at[z, at.y, :, at.core, high]
            steps.append(send(part, part, b_sem, k, at.at_y(d)))
        second.append(steps)
    for j in range(nz):
        z = lax.rem(at.z + nz - j, nz)
        for copy in second[j]:
            copy.wait_recv()
        part = all_ref.at[z, :, :, at.core]
        last.append(send(part, part, core_sem, j, at.sibling()))
    for copy in waits + last:
        copy.wait()
    for copy in taps + planes + sum(first + second, []):
        copy.wait_send()


def reduce_kernel(
    wide,
    batch,
    lead_step,
    span,
    room,
    deep,
    per,
    table_ref,
    grad_ref,
    gsm_ref,
    o_ref,
    g_ref,
    oz_ref,
    gz_ref,
    share_ref,
    total_ref,
    part_ref,
    send_ref,
    core_ref,
    acc_ref,
    sa_ref,
    sb_ref,
    ra_ref,
    rb_ref,
    a_ref,
    b_ref,
    sa2_ref,
    sb2_ref,
    ra2_ref,
    rb2_ref,
    own_ref,
    sz_ref,
    rz_ref,
    sum_ref,
    back_ref,
    got_ref,
    tile_ref,
    tiles_ref,
    tap_ref,
    core_sem,
    a_sem,
    b_sem,
    z_sem,
    o_sem,
    g_sem,
    tap_sem,
    all_sem,
    fetch_sem,
):
    at = Place(wide, batch)
    nz, ns, half = at.nz, at.ns, at.half
    count = nz * at.nb
    cut = room * 32 // 2
    link = send_ref.dtype
    got_ref[...] = jnp.zeros(got_ref.shape, f32)

    fetch = []
    for k, core in enumerate((1 - at.core, at.core)):
        fetch.append(
            pltpu.make_async_copy(grad_ref.at[:, :, :, core], part_ref.at[k], fetch_sem.at[k])
        )
        fetch[k].start()
    greet([at.at_all(d) for d in range(1, count)])
    waits = []

    def exchange(src, dst, sems, steps):
        for d in steps:
            waits.append(send(src.at[lax.rem(at.z + d, nz)], dst.at[at.z], sems, d - 1, at.at_z(d)))

    exchange(o_ref, oz_ref, o_sem, range(1, nz))
    exchange(g_ref, gz_ref, g_sem, range(1, nz))
    oz_ref[at.z] = o_ref[at.z]
    gz_ref[at.z] = g_ref[at.z]

    pieces = [lax.rem(at.z + j, nz) for j in (*range(1, nz), 0)]
    cores, first, second, stage = [], [], [], []
    fetch[0].wait()
    for j, z in enumerate(pieces):
        send_ref[z] = part_ref[0, z].astype(link)
        cores.append(send(send_ref.at[z], core_ref.at[z], core_sem, j, at.sibling()))
    fetch[1].wait()
    for j, z in enumerate(pieces):
        cores[j].wait_recv()
        acc_ref[z] = part_ref[1, z] + core_ref[z].astype(f32)
        steps = []
        for d in range(1, ns):
            x = lax.rem(at.x + d, ns)
            y = lax.rem(at.y + d, ns)
            for o in range(ns):
                sa_ref[d - 1, z, o] = acc_ref[z, o, x, 0:cut, :].astype(link)
                sb_ref[d - 1, z, o] = acc_ref[z, y, o, cut : 2 * cut, :].astype(link)
            k = j * (ns - 1) + d - 1
            steps.append(send(sa_ref.at[d - 1, z], ra_ref.at[d - 1, z], a_sem, k, at.at_x(d)))
            steps.append(send(sb_ref.at[d - 1, z], rb_ref.at[d - 1, z], b_sem, k, at.at_y(d)))
        first.append(steps)
    for j, z in enumerate(pieces):
        for copy in first[j]:
            copy.wait_recv()
        for o in range(ns):
            va = acc_ref[z, o, at.x, 0:cut, :]
            vb = acc_ref[z, at.y, o, cut : 2 * cut, :]
            for d in range(1, ns):
                va = va + ra_ref[d - 1, z, o].astype(f32)
                vb = vb + rb_ref[d - 1, z, o].astype(f32)
            a_ref[z, o] = va
            b_ref[z, o] = vb
        steps = []
        for d in range(1, ns):
            sa2_ref[d - 1, z] = a_ref[z, lax.rem(at.y + d, ns)].astype(link)
            sb2_ref[d - 1, z] = b_ref[z, lax.rem(at.x + d, ns)].astype(link)
            k = (nz + j) * (ns - 1) + d - 1
            steps.append(send(sa2_ref.at[d - 1, z], ra2_ref.at[d - 1, z], a_sem, k, at.at_y(d)))
            steps.append(send(sb2_ref.at[d - 1, z], rb2_ref.at[d - 1, z], b_sem, k, at.at_x(d)))
        second.append(steps)
    for j, z in enumerate(pieces):
        for copy in second[j]:
            copy.wait_recv()
        va = a_ref[z, at.y]
        vb = b_ref[z, at.x]
        for d in range(1, ns):
            va = va + ra2_ref[d - 1, z].astype(f32)
            vb = vb + rb2_ref[d - 1, z].astype(f32)
        own_ref[z, 0:cut, :] = va
        own_ref[z, cut : 2 * cut, :] = vb
        if j < nz - 1:
            sz_ref[z, 0:cut, :] = va.astype(link)
            sz_ref[z, cut : 2 * cut, :] = vb.astype(link)
            stage.append(send(sz_ref.at[z], rz_ref.at[j], z_sem, j, at.at_z(j + 1)))
    for copy in stage:
        copy.wait()
    for copy in cores + sum(first + second, []):
        copy.wait_send()
    total = own_ref[at.z]
    for d in range(1, nz):
        total = total + rz_ref[d - 1].astype(f32)
    sum_ref[...] = total * (1.0 / NKER)

    picks = half * deep * span
    weights = picks + room * half * deep
    square = jnp.zeros((1, 128), f32)
    for k in range(room):
        value = sum_ref[32 * k : 32 * k + 32, :]
        square = square + table_ref[weights + k] * jnp.sum(value * value, axis=0, keepdims=True)
    tile_ref[0:2, :] = gsm_ref[...]
    tile_ref[2:3, :] = square
    tile_ref[3:8, :] = jnp.zeros((5, 128), f32)
    tells = [
        send(tile_ref, tiles_ref.at[at.me], all_sem, d - 1, at.at_all(d)) for d in range(1, count)
    ]
    tiles_ref[at.me] = tile_ref[...]

    @pl.loop(0, half)
    def _(q):
        for s in range(deep):
            value = jnp.zeros((32, 128), f32)
            for k in range(room):
                value = value + (
                    table_ref[picks + k * half * deep + q * deep + s]
                    * sum_ref[32 * k : 32 * k + 32, :]
                )
            back_ref[q, s] = value

    backs = swap_cells(at, deep, -1, back_ref, got_ref, tap_sem)
    for copy in tells:
        copy.wait()
    tile = jnp.zeros((8, 128), f32)
    for d in range(count):
        tile = tile + tiles_ref[d]
    total_ref[...] = tile
    for copy in backs:
        copy.wait()

    @pl.loop(0, span)
    def _(t):
        value = jnp.zeros((32, 128), f32)
        for q in range(half):
            for s in range(deep):
                value = value + table_ref[(q * deep + s) * span + t] * got_ref[q, s]
        tap_ref[pl.ds(pl.multiple_of(32 * t, 32), 32), :] = value

    held = share_ref.shape[0]
    share_ref[...] = tap_ref[pl.ds(lax.rem(at.me * lead_step, 32), held), :]
    for copy in waits:
        copy.wait()


def finish_kernel(
    per,
    total_ref,
    share_ref,
    o_ref,
    g_ref,
    w_ref,
    m_ref,
    v_ref,
    sw_ref,
    sm_ref,
    sv_ref,
    out_ref,
    gser_ref,
    norm_ref,
    nw_ref,
    nm_ref,
    nv_ref,
    nsw_ref,
    nsm_ref,
    nsv_ref,
):
    small = total_ref[0:2, :]
    lanes = jnp.sum(total_ref[2:3, :], axis=1, keepdims=True)
    squares = jnp.sum(jnp.sum(small * small, axis=0, keepdims=True), axis=1, keepdims=True)
    norm = jnp.sqrt(lanes + squares)
    norm_ref[...] = norm
    factor = jnp.minimum(1.0, clip_norm / (norm + 1e-06))
    nsw_ref[...], nsm_ref[...], nsv_ref[...] = adam_update(
        sw_ref[...], small * factor, sm_ref[...], sv_ref[...]
    )
    nw_ref[...], nm_ref[...], nv_ref[...] = adam_update(
        w_ref[...], share_ref[...] * factor, m_ref[...], v_ref[...]
    )
    shard = out_ref.shape[2]
    for src, dst in ((o_ref, out_ref), (g_ref, gser_ref)):
        for z in range(src.shape[0]):
            both = src[z].astype(f32).T
            dst[per * z] = both[0:C, 0:shard].astype(bf16)
            if per == 2:
                dst[per * z + 1] = both[C:, 0:shard].astype(bf16)


def block_kernel(
    L,
    per,
    row_of,
    freq_ref,
    len_ref,
    x_ref,
    cot_ref,
    all_ref,
    small_ref,
    out_ref,
    gser_ref,
    grad_ref,
    gsm_ref,
    gm1_ref,
    gm2_ref,
    w1_ref,
    w2_ref,
    w1s_ref,
    w2s_ref,
    w1r_ref,
    w2r_ref,
    trig_ref,
    res_ref,
    mg_ref,
    gin_ref,
    xf_ref,
    af_ref,
    pk_ref,
    xs_ref,
    s1_ref,
    s2_ref,
    p2_ref,
    p1_ref,
    r_ref,
    act_ref,
    slope_ref,
    br_ref,
    wv_ref,
    gw_ref,
    gb_ref,
):
    slabs = x_ref.shape[0]
    shard = L // slabs
    lanes = lane_low
    third = L // 3
    PS, PP, PK = 88, 176, 16

    def swap(v):
        return pltpu.roll(v, C, 1)

    def span_of(t, n, align=8):
        assert t % align == 0
        return slice(t, t + n)

    def half_sum(v):
        low = lanes(v.shape[0])
        a = jnp.sum(jnp.where(low, v, 0.0), axis=1, keepdims=True)
        b = jnp.sum(jnp.where(low, 0.0, v), axis=1, keepdims=True)
        return jnp.where(low, a, b)

    def fold(v):
        return jnp.sum(v.reshape(v.shape[0] // 8, 8, 128), axis=0)

    def split(v):
        hi = v.astype(bf16)
        rest = v - hi.astype(f32)
        mid = rest.astype(bf16)
        return hi, mid, (rest - mid.astype(f32)).astype(bf16)

    raw = [freq_ref[j] for j in range(K)]
    ranks = [sum((raw[j] > raw[k]).astype(jnp.int32) for k in range(K)) for j in range(K)]
    freqs = [sum(jnp.where(ranks[j] == k, raw[j], 0) for j in range(K)) for k in range(K)]
    order = (1, 2, 3, 0, 4)
    periods = [L // freqs[j] for j in order]
    freqs = [freqs[j] for j in order]
    tiles = [(3, 3), (3, 3), (3, 3), (3, 1), (1, 3)]

    for ref, pad in ((s1_ref, PS), (s2_ref, PS), (p1_ref, PP), (p2_ref, PP)):
        for b in range(ref.shape[0]):
            ref[b, 0:pad, :] = jnp.zeros((pad, 128), f32)
            ref[b, L + pad : L + 2 * pad, :] = jnp.zeros((pad, 128), f32)
    pk_ref[0:PK, :] = jnp.zeros((PK, 128), f32)
    pk_ref[L + PK : L + 2 * PK, :] = jnp.zeros((PK, 128), f32)
    gb_ref[...] = jnp.zeros((4, 8, 128), f32)
    gw_ref[...] = jnp.zeros((K, 8, 128), f32)

    r = lax.broadcasted_iota(jnp.int32, (128, 128), 0)
    c = lax.broadcasted_iota(jnp.int32, (128, 128), 1)
    ahead = jnp.where(c == r // 64 * 64 + r % 2 * 32 + r % 64 // 2, 1.0, 0.0).astype(bf16)
    low32 = lanes(32)

    def cell_rows(block, a, b):
        cell = block * CELLS + (OFFS[b] + HALF) * SPAN + OFFS[a] + HALF
        return slice(int(row_of[cell]) * 32, int(row_of[cell]) * 32 + 32)

    def lay_out(block, raw_w, mat, rws):
        raw_w[11 * C :, :] = jnp.zeros((C, W), bf16)
        for a in range(11):
            for q in range(6):
                one = all_ref[cell_rows(block, a, 2 * q), :].astype(f32)
                two = jnp.zeros((32, 128), f32)
                if q < 5:
                    two = all_ref[cell_rows(block, a, 2 * q + 1), :].astype(f32)
                cut = slice(128 * q, 128 * q + 128)
                raw_w[64 * a : 64 * a + 32, cut] = jnp.where(low32, one, swap(two)).astype(bf16)
                raw_w[64 * a + 32 : 64 * a + 64, cut] = jnp.where(low32, swap(one), two).astype(bf16)
        for i in range(6):
            cut = slice(128 * i, 128 * i + 128)
            v = jnp.dot(ahead, raw_w[cut, :], preferred_element_type=f32)
            v16 = v.astype(bf16)
            mat[cut, :] = v16
            rws[128 * i : 128 * i + 64, :] = v16[64:128]
            rws[128 * i + 64 : 128 * i + 128, :] = v16[0:64]
            for q in range(6):
                at = slice(128 * q, 128 * q + 128)
                raw_w[cut, at] = swap(v[:, at]).astype(bf16)

    own_first = lax.axis_index("wide") * per
    own = jnp.where(lanes(1), len_ref[own_first], len_ref[own_first + 1] if per == 2 else 0)

    def valid(t, n):
        return t + lax.broadcasted_iota(jnp.int32, (n, 128), 0) < own

    for z in range(slabs):
        res_ref[shard * z : shard * z + shard, :] = x_ref[z].astype(f32)[0:shard]
        gin_ref[shard * z : shard * z + shard, :] = cot_ref[z].astype(f32)[0:shard]

    for t in range(0, L, 176):
        v = jnp.where(valid(t, 176), res_ref[t : t + 176, :], 0.0)
        mg_ref[t : t + 176, :] = v
        pk_ref[PK + t : PK + t + 176, :] = v

    def pairs(i, dst):
        n = third + 16
        a = pk_ref[span_of(PK - 8 + third * i, n), :]
        b = pk_ref[PK - 7 + third * i : PK - 7 + third * i + n, :]
        low = lanes(n)
        dst[0, span_of(third * i, n), :] = jnp.where(low, a, swap(b))
        dst[1, span_of(third * i, n), :] = jnp.where(low, swap(a), b)

    def within(t, n, p):
        at = t + lax.broadcasted_iota(jnp.int32, (n, 128), 0)
        inv = 1.0 / jnp.full((1, 128), p, jnp.int32).astype(f32)
        return at - ((at.astype(f32) + 0.5) * inv).astype(jnp.int32) * p

    def build_cols(i, k, src, dst):
        p, nk = periods[k], tiles[k][0]
        n = 176
        for half in range(third // n):
            t = third * i + n * half
            wi = within(t, n, p) + jnp.where(lanes(n), 0, 1)
            for q in range(2 * nk):
                base = BASES[q]
                keep = wi >= -base if base < 0 else wi < p - base
                for s in range(2):
                    v = src[s, 8 + base + t : 8 + base + t + n, :]
                    dst[span_of(s * L + t, n, 16), 128 * q : 128 * q + 128] = jnp.where(
                        keep, v, 0.0
                    ).astype(bf16)

    def build_rows(i, k, src, dst):
        p, nr = periods[k], tiles[k][1]
        n = 176
        low = lanes(n)
        for half in range(third // n):
            t = third * i + n * half
            for q in range(2 * nr):
                one = pl.ds(PP + jnp.clip(t - OFFS[2 * q] * p, -n, L), n)
                a, b = src[0, one, :], src[1, one, :]
                if q < 5:
                    two = pl.ds(PP + jnp.clip(t - OFFS[2 * q + 1] * p, -n, L), n)
                    c, d = src[0, two, :], src[1, two, :]
                else:
                    c = d = jnp.zeros((n, 128), f32)
                cut = slice(128 * q, 128 * q + 128)
                dst[span_of(t, n, 16), cut] = jnp.where(low, a, d).astype(bf16)
                dst[span_of(L + t, n, 16), cut] = jnp.where(low, b, c).astype(bf16)

    def sum_rows(t, n, k, src):
        p, nr = periods[k], tiles[k][1]
        sums = [jnp.zeros((n, 128), f32)] * 2
        for b in range(min(4 * nr, 11)):
            off = PS + jnp.clip(OFFS[b] * p + t, -n, L)
            sums[b % 2] = sums[b % 2] + src[b, pl.ds(off, n), :]
        return sums[0] + swap(sums[1])

    def sum_cols(t, n, k, src):
        p, nk = periods[k], tiles[k][0]
        wi = within(t, n, p)
        sums = [jnp.zeros((n, 128), f32)] * 2
        for b in range(min(4 * nk, 11)):
            d = OFFS[b]
            v = src[b, PS - d + t : PS - d + t + n, :]
            if d < 0:
                v = jnp.where(wi < p + d, v, 0.0)
            elif d > 0:
                v = jnp.where(wi >= d, v, 0.0)
            sums[b % 2] = sums[b % 2] + v
        return sums[0] + swap(sums[1])

    def twice(i, first):
        v = small_ref[i : i + 1, :]
        return jnp.where(lanes(1) == first, v, swap(v))

    bias_one, bias_two = twice(0, True), twice(0, False)
    gain, shift = twice(1, True), twice(1, False)
    NS = 88

    def hidden(i, k):
        for j in range(third // NS):
            t = third * i + NS * j
            slope_ref[k, span_of(t, NS), :] = sum_rows(t, NS, k, s1_ref) + bias_one

    def activate(i, k):
        n = 176
        for t in range(third * i, third * i + third, n):
            v = slope_ref[k, span_of(t, n), :]
            cdf = 0.5 * (1.0 + lax.erf(v * inv_root_two))
            slope_ref[k, span_of(t, n), :] = cdf + v * jnp.exp(-0.5 * v * v) * inv_root_tau
            act = (v * cdf).astype(bf16)
            act_ref[k, span_of(t, n, 16), :] = act
            pk_ref[span_of(PK + t, n), :] = act.astype(f32)

    def branch(i, k):
        for j in range(third // NS):
            t = third * i + NS * j
            br_ref[k, span_of(t, NS), :] = sum_rows(t, NS, k, s2_ref) + bias_two

    def merge(i, k):
        wk = wv_ref[k : k + 1, :]
        at = span_of(third * i, third)
        mg_ref[at, :] += wk * br_ref[k, at, :]

    def rebuild(i, k):
        v = act_ref[k, span_of(third * i, third, 16), :].astype(f32)
        pk_ref[span_of(PK + third * i, third), :] = v

    def spread_branch(i, k):
        wk = wv_ref[k : k + 1, :]
        sum_w = sum_b = jnp.zeros((8, 128), f32)
        for j in range(third // NS):
            t = third * i + NS * j
            gm = mg_ref[span_of(t, NS), :]
            sum_w = sum_w + fold(gm * br_ref[k, span_of(t, NS), :])
            g = (wk * gm).astype(bf16).astype(f32)
            sum_b = sum_b + fold(g)
            p2_ref[0, span_of(PP + t, NS), :] = g
            p2_ref[1, span_of(PP + t, NS), :] = swap(g)
        gw_ref[k] += sum_w
        gb_ref[1] += sum_b

    def spread_hidden(i, k):
        sum_b = jnp.zeros((8, 128), f32)
        for j in range(third // NS):
            t = third * i + NS * j
            g = sum_cols(t, NS, k, s1_ref) * slope_ref[k, span_of(t, NS), :]
            g = g.astype(bf16).astype(f32)
            sum_b = sum_b + fold(g)
            p1_ref[0, span_of(PP + t, NS), :] = g
            p1_ref[1, span_of(PP + t, NS), :] = swap(g)
        gb_ref[0] += sum_b

    def collect(i, k):
        for j in range(third // NS):
            t = third * i + NS * j
            gin_ref[span_of(t, NS), :] += sum_cols(t, NS, k, s2_ref)

    def to_slots(dst, n, d0, d1):
        low = lanes(L)
        for h in range(2):
            a = d0[:, 128 * h : 128 * h + 128]
            b = d1[:, 128 * h : 128 * h + 128]
            dst[4 * n + 2 * h, PS : PS + L, :] = jnp.where(low, a, b)
            if 4 * n + 2 * h + 1 < 11:
                dst[4 * n + 2 * h + 1, PS : PS + L, :] = jnp.where(low, b, a)

    def mm_forward(i, k, src, w, ws, dst):
        if i >= tiles[k][1]:
            return
        depth, cut = slice(0, 256 * tiles[k][0]), slice(256 * i, 256 * i + 256)
        d0 = jnp.dot(src[0:L, depth], w[depth, cut], preferred_element_type=f32)
        d1 = jnp.dot(src[L : 2 * L, depth], ws[depth, cut], preferred_element_type=f32)
        to_slots(dst, i, d0, d1)

    def mm_adjoint(i, k, src, w, wr, dst):
        if i >= tiles[k][0]:
            return
        depth, cut = slice(0, 256 * tiles[k][1]), slice(256 * i, 256 * i + 256)
        dims = (((1,), (1,)), ((), ()))
        d0 = lax.dot_general(src[0:L, depth], w[cut, depth], dims, preferred_element_type=f32)
        d1 = lax.dot_general(src[L : 2 * L, depth], wr[cut, depth], dims, preferred_element_type=f32)
        to_slots(dst, i, d0, d1)

    def mm_weights(i, k, left, right, gm):
        if i >= tiles[k][0]:
            return
        cut, wide_cut = slice(256 * i, 256 * i + 256), slice(0, 256 * tiles[k][1])
        v = lax.dot_general(
            left[:, cut], right[:, wide_cut], (((0,), (0,)), ((), ())), preferred_element_type=f32
        )
        gm[cut, wide_cut] = v if k == 0 else gm[cut, wide_cut] + v

    blocks = []

    def block(*work):
        blocks.append(work)

        @pl.when(raw[len(blocks) % K] + len(blocks) > 0)
        def _():
            for item in work:
                for i in range(3):
                    item[0](i, *item[1:])

    def once(i, f, *rest):
        if i == 0:
            f(*rest)

    block((once, lay_out, 0, w1s_ref, w1_ref, w1r_ref), (pairs, xf_ref))

    lane = lax.broadcasted_iota(jnp.int32, (1, 128), 1)
    turn = jnp.zeros((1, 128), jnp.int32)
    for j in range(K):
        turn = jnp.where(lane % 8 == j, freqs[j], turn)

    def waves(i):
        t = i * third + lax.broadcasted_iota(jnp.int32, (third, 128), 0)
        turns = t * turn
        whole = ((turns.astype(f32) + 0.5) * (1.0 / L)).astype(jnp.int32)
        angle = (turns - whole * L).astype(f32) * (2.0 * math.pi / L)
        angle = jnp.where(lane < 8, angle, angle - 0.5 * math.pi)
        wave = jnp.where((lane < 16) & (lane % 8 < K), jnp.cos(angle), 0.0)
        hi, mid, lo = (v.astype(f32) for v in split(wave))
        trig_ref[span_of(i * third, third, 16), :] = (
            hi + pltpu.roll(mid, 16, 1) + pltpu.roll(lo, 32, 1)
        ).astype(bf16)

    block(
        (build_cols, 0, xf_ref, xs_ref),
        (mm_forward, 0, xs_ref, w1_ref, w1s_ref, s1_ref),
        (waves,),
    )
    block((once, lay_out, 1, w2s_ref, w2_ref, w2r_ref))

    spec = lax.dot_general(
        trig_ref[...],
        mg_ref[...].astype(bf16),
        (((0,), (0,)), ((), ())),
        preferred_element_type=f32,
    )
    spec = (spec[0:16] + spec[16:32] + spec[32:48]) * (2.0 / L)
    real, imag = spec[0:8], spec[8:16]
    magnitude = jnp.sqrt(real * real + imag * imag + 1.0)
    mean_mag = half_sum(magnitude) * (1.0 / C)
    live = lax.broadcasted_iota(jnp.int32, (8, 128), 0) < K
    top = jnp.max(jnp.where(live, mean_mag, -1e30), axis=0, keepdims=True)
    ex = jnp.where(live, jnp.exp(mean_mag - top), 0.0)
    weights = ex / jnp.sum(ex, axis=0, keepdims=True)
    wv_ref[...] = weights

    block((hidden, 0), (activate, 0))
    for k in range(K):
        if k + 1 < K:
            work = [
                (build_cols, k + 1, xf_ref, xs_ref),
                (mm_forward, k + 1, xs_ref, w1_ref, w1s_ref, s1_ref),
            ]
            if k > 0:
                work = [(branch, k - 1)] + work + [(merge, k - 1)]
            block(*work)
        work = [
            (pairs, af_ref),
            (build_cols, k, af_ref, xs_ref),
            (mm_forward, k, xs_ref, w2_ref, w2s_ref, s2_ref),
        ]
        if k + 1 < K:
            work = [(hidden, k + 1)] + work + [(activate, k + 1)]
        else:
            work = [(branch, k - 1)] + work + [(merge, k - 1)]
        block(*work)

    same = (
        lax.broadcasted_iota(jnp.int32, (384, 128), 0) % 128 // C
        == lax.broadcasted_iota(jnp.int32, (384, 128), 1) // C
    )
    ones = jnp.where(same, 1.0 / C, 0.0).astype(bf16)

    def half_mean(v):
        return jnp.dot(jnp.concatenate(split(v), axis=1), ones, preferred_element_type=f32)

    def normalise(i):
        at = span_of(i * third, third)
        m = mg_ref[at, :]
        ok = valid(i * third, third)
        centered = m - half_mean(m)
        inverse = lax.rsqrt(half_mean(centered * centered) + norm_eps)
        normed = centered * inverse
        res_ref[at, :] = jnp.where(ok, normed * gain + shift, 0.0)
        g_out = jnp.where(ok, gin_ref[at, :], 0.0)
        gb_ref[2] += fold(g_out * normed)
        gb_ref[3] += fold(g_out)
        g_norm = g_out * gain
        gm = inverse * (g_norm - half_mean(g_norm) - normed * half_mean(g_norm * normed))
        mg_ref[at, :] = gm
        gin_ref[at, :] = gm

    block((branch, K - 1), (merge, K - 1), (normalise,), (spread_branch, 0))

    def to_slabs(dst):
        for z in range(slabs):
            v = res_ref[shard * z : shard * z + shard, :]
            v = jnp.concatenate([v, jnp.zeros((dst.shape[1] - shard, 128), f32)], axis=0)
            dst[z] = v.astype(bf16)

    to_slabs(out_ref)

    for k in range(K):
        work = [
            (build_rows, k, p2_ref, r_ref),
            (mm_adjoint, k, r_ref, w2_ref, w2r_ref, s1_ref),
            (rebuild, k),
        ]
        if k > 0:
            work.append((collect, k - 1))
        work += [
            (pairs, af_ref),
            (build_cols, k, af_ref, xs_ref),
            (mm_weights, k, xs_ref, r_ref, gm2_ref),
            (spread_hidden, k),
        ]
        if k + 1 < K:
            work.append((spread_branch, k + 1))
        block(*work)
        block(
            (build_rows, k, p1_ref, r_ref),
            (mm_adjoint, k, r_ref, w1_ref, w1r_ref, s2_ref),
            (build_cols, k, xf_ref, xs_ref),
            (mm_weights, k, xs_ref, r_ref, gm1_ref),
        )

    row8 = lax.broadcasted_iota(jnp.int32, (8, 128), 0)
    g_weights = jnp.zeros((8, 128), f32)
    for j in range(K):
        total = jnp.sum(gw_ref[j], axis=0, keepdims=True)
        g_weights = jnp.where(row8 == j, total, g_weights)
    g_weights = half_sum(g_weights)
    weights = wv_ref[...]
    g_score = weights * (g_weights - jnp.sum(weights * g_weights, axis=0, keepdims=True))
    coeff = g_score / (magnitude * C) * (2.0 / L)
    c_hi, c_lo, _ = split(jnp.concatenate([coeff * real, coeff * imag], axis=0))
    c_all = jnp.concatenate([c_hi, c_hi, c_hi, jnp.zeros((80, 128), bf16)], axis=0)
    c_low = jnp.concatenate([c_lo, jnp.zeros((112, 128), bf16)], axis=0)

    def finish(i):
        at = span_of(i * third, third)
        t = trig_ref[span_of(i * third, third, 16), :]
        g = (
            gin_ref[at, :]
            + jnp.dot(t, c_all, preferred_element_type=f32)
            + jnp.dot(t, c_low, preferred_element_type=f32)
        )
        res_ref[at, :] = jnp.where(valid(i * third, third), g, 0.0)

    block((collect, K - 1), (finish,))
    to_slabs(gser_ref)

    sums = []
    for q in range(4):
        total = jnp.sum(gb_ref[q], axis=0, keepdims=True)
        sums.append(total + swap(total))
    gsm_ref[0:1, :] = jnp.where(lanes(1), sums[0], sums[1])
    gsm_ref[1:2, :] = jnp.where(lanes(1), sums[2], sums[3])

    used = set(int(v) for v in row_of)
    for v in range(grad_ref.shape[0] // 32):
        if v not in used:
            grad_ref[32 * v : 32 * v + 32, :] = jnp.zeros((32, 128), f32)
    back = jnp.where(r == c // 64 * 64 + c % 2 * 32 + c % 64 // 2, 1.0, 0.0).astype(bf16)
    back = jnp.concatenate([back, back, back], axis=1)
    for block, mat in enumerate((gm1_ref, gm2_ref)):
        for i in range(6):
            v = jnp.concatenate(split(mat[128 * i : 128 * i + 128, :]), axis=0)
            v = jnp.dot(back, v, preferred_element_type=f32)
            for a in (2 * i, 2 * i + 1):
                if a == 11:
                    continue
                first = 64 * (a % 2)
                for q in range(6):
                    even = v[first : first + 32, 128 * q : 128 * q + 128]
                    odd = v[first + 32 : first + 64, 128 * q : 128 * q + 128]
                    grad_ref[cell_rows(block, a, 2 * q), :] = jnp.where(low32, even, swap(odd))
                    if q < 5:
                        grad_ref[cell_rows(block, a, 2 * q + 1), :] = jnp.where(
                            low32, swap(even), odd
                        )


vm = pl.BlockSpec(memory_space=pltpu.VMEM)
sm = pl.BlockSpec(memory_space=pltpu.SMEM)
sds = jax.ShapeDtypeStruct


def run_block(x, cot, lens, freqs, cells, small, per, row_of, L):
    return pl.pallas_call(
        functools.partial(block_kernel, L, per, row_of),
        out_shape=(
            sds(x.shape, bf16),
            sds(x.shape, bf16),
            sds(cells.shape, f32),
            sds((2, 128), f32),
        ),
        in_specs=[sm, sm, vm, vm, vm, vm],
        out_specs=(vm,) * 4,
        scratch_shapes=[
            pltpu.VMEM((W, W), f32),
            pltpu.VMEM((W, W), f32),
            pltpu.VMEM((W, W), bf16),
            pltpu.VMEM((W, W), bf16),
            pltpu.VMEM((W, W), bf16),
            pltpu.VMEM((W, W), bf16),
            pltpu.VMEM((W, W), bf16),
            pltpu.VMEM((W, W), bf16),
            pltpu.VMEM((L, 128), bf16),
            pltpu.VMEM((L, 128), f32),
            pltpu.VMEM((L, 128), f32),
            pltpu.VMEM((L, 128), f32),
            pltpu.VMEM((2, L + 16, 128), f32),
            pltpu.VMEM((2, L + 16, 128), f32),
            pltpu.VMEM((L + 32, 128), f32),
            pltpu.VMEM((2 * L, W), bf16),
            pltpu.VMEM((12, L + 176, 128), f32),
            pltpu.VMEM((12, L + 176, 128), f32),
            pltpu.VMEM((2, L + 352, 128), f32),
            pltpu.VMEM((2, L + 352, 128), f32),
            pltpu.VMEM((2 * L, W), bf16),
            pltpu.VMEM((K, L, 128), bf16),
            pltpu.VMEM((K, L, 128), f32),
            pltpu.VMEM((K, L, 128), f32),
            pltpu.VMEM((8, 128), f32),
            pltpu.VMEM((K, 8, 128), f32),
            pltpu.VMEM((4, 8, 128), f32),
        ],
        compiler_params=pltpu.CompilerParams(vmem_limit_bytes=63 << 20),
        name="block",
    )(freqs, lens, x, cot, cells, small)


def adam_update(param, grad, first, second):
    first_new = beta_one * first + (1.0 - beta_one) * grad
    second_new = beta_two * second + (1.0 - beta_two) * grad * grad
    first_hat = first_new / (1.0 - beta_one**STEP)
    second_hat = second_new / (1.0 - beta_two**STEP)
    param_new = param - learn_rate * (
        first_hat / (jnp.sqrt(second_hat) + adam_eps) + weight_decay * param
    )
    return (param_new, first_new, second_new)


def local(series, lengths, freqs, cotangent, kernels, kernel_m, kernel_v, small, small_m, small_v):
    wide = lax.axis_size("wide")
    batch = lax.axis_size("batch")
    count = wide * batch
    half, sides = count // 2, math.isqrt(batch // 2)
    me = lax.axis_index(("wide", "batch"))
    span, room, deep, spread, pick, weight, row_of = plan(wide, batch)
    share = kernels.shape[0]
    shard = series.shape[1]
    per = series.shape[0] // wide
    slab = -(-shard // 16) * 16

    tables = np.concatenate([v.reshape(count, -1) for v in (spread, pick, weight)], axis=1)
    table = lax.dynamic_index_in_dim(jnp.asarray(tables), me, 0, keepdims=False)
    aligned = share % 128 == 0
    lead = me * share % TAP

    def to_rows(v):
        if aligned:
            return v.reshape(share // 128, 128)
        wide_v = jnp.zeros((span * TAP,), f32)
        return lax.dynamic_update_slice_in_dim(wide_v, v, lead, 0).reshape(span * 32, 128)

    def from_rows(v):
        if aligned:
            return v.reshape(share)
        return lax.dynamic_slice_in_dim(v.reshape(-1), lead, share, 0)

    lead_step = share // 128 if aligned else 0
    params = pltpu.CompilerParams
    static = (wide, batch, lead_step, span, room, deep, per)
    dma = pltpu.SemaphoreType.DMA
    cell_shape = (wide, sides, sides, 2, room * 32, 128)
    slab_shape = (wide, slab, 128)
    exchange = (half, deep, 32, 128)
    taps_rows = -(-(span * 32 + 32) // 8) * 8
    taps = to_rows(kernels)
    held = taps.shape[0]

    x, cot, cells = pl.pallas_call(
        functools.partial(gather_kernel, *static),
        out_shape=(sds(slab_shape, bf16), sds(slab_shape, bf16), sds(cell_shape, bf16)),
        in_specs=[sm, vm, vm, vm],
        out_specs=(vm,) * 3,
        scratch_shapes=[
            pltpu.VMEM((taps_rows, 128), f32),
            pltpu.VMEM(exchange, f32),
            pltpu.VMEM(exchange, f32),
            pltpu.VMEM(slab_shape, bf16),
            pltpu.VMEM(slab_shape, bf16),
            dma((2, half - 1)),
            dma((2, wide - 1)),
            dma((2, wide - 1)),
            dma((2, wide - 1)),
            dma((2, 2 * wide * (sides - 1))),
            dma((2, 2 * wide * (sides - 1))),
            dma((2, wide)),
        ],
        compiler_params=params(
            collective_id=0, has_side_effects=True, vmem_limit_bytes=62 << 20
        ),
        name="gather",
    )(table, taps, series.transpose(0, 2, 1), cotangent.transpose(0, 2, 1))

    small_rows = small.reshape(2, 128)
    out, gser, grads, gsm = run_block(
        x, cot, lengths, freqs, cells.reshape(-1, 128), small_rows, per, row_of, shard * wide
    )

    link = bf16
    cut = room * 16
    out, gser, grad_share, total = pl.pallas_call(
        functools.partial(reduce_kernel, *static),
        out_shape=(
            sds(slab_shape, bf16),
            sds(slab_shape, bf16),
            sds((held, 128), f32),
            sds((8, 128), f32),
        ),
        in_specs=[sm, pl.BlockSpec(memory_space=pl.ANY), vm, vm, vm],
        out_specs=(vm,) * 4,
        scratch_shapes=[
            pltpu.VMEM((2, wide, sides, sides, room * 32, 128), f32),
            pltpu.VMEM((wide, sides, sides, room * 32, 128), link),
            pltpu.VMEM((wide, sides, sides, room * 32, 128), link),
            pltpu.VMEM((wide, sides, sides, room * 32, 128), f32),
            pltpu.VMEM((sides - 1, wide, sides, cut, 128), link),
            pltpu.VMEM((sides - 1, wide, sides, cut, 128), link),
            pltpu.VMEM((sides - 1, wide, sides, cut, 128), link),
            pltpu.VMEM((sides - 1, wide, sides, cut, 128), link),
            pltpu.VMEM((wide, sides, cut, 128), f32),
            pltpu.VMEM((wide, sides, cut, 128), f32),
            pltpu.VMEM((sides - 1, wide, cut, 128), link),
            pltpu.VMEM((sides - 1, wide, cut, 128), link),
            pltpu.VMEM((sides - 1, wide, cut, 128), link),
            pltpu.VMEM((sides - 1, wide, cut, 128), link),
            pltpu.VMEM((wide, room * 32, 128), f32),
            pltpu.VMEM((wide, room * 32, 128), link),
            pltpu.VMEM((wide - 1, room * 32, 128), link),
            pltpu.VMEM((room * 32, 128), f32),
            pltpu.VMEM(exchange, f32),
            pltpu.VMEM(exchange, f32),
            pltpu.VMEM((8, 128), f32),
            pltpu.VMEM((count, 8, 128), f32),
            pltpu.VMEM((taps_rows, 128), f32),
            dma((2, wide)),
            dma((2, 2 * wide * (sides - 1))),
            dma((2, 2 * wide * (sides - 1))),
            dma((2, wide - 1)),
            dma((2, wide - 1)),
            dma((2, wide - 1)),
            dma((2, half - 1)),
            dma((2, count - 1)),
            dma((2,)),
        ],
        compiler_params=params(
            collective_id=1, has_side_effects=True, vmem_limit_bytes=32 << 20
        ),
        name="reduce",
    )(table, grads.reshape(cell_shape), gsm, out, gser)

    turned = (series.shape[0], series.shape[2], shard)
    out, gser, norm, new_w, new_m, new_v, new_sw, new_sm, new_sv = pl.pallas_call(
        functools.partial(finish_kernel, per),
        out_shape=(
            sds(turned, bf16),
            sds(turned, bf16),
            sds((1, 1), f32),
            sds((held, 128), f32),
            sds((held, 128), f32),
            sds((held, 128), f32),
            sds((2, 128), f32),
            sds((2, 128), f32),
            sds((2, 128), f32),
        ),
        in_specs=[vm] * 10,
        out_specs=(vm,) * 9,
        compiler_params=params(vmem_limit_bytes=40 << 20),
        name="finish",
    )(
        total,
        grad_share,
        out,
        gser,
        taps,
        to_rows(kernel_m),
        to_rows(kernel_v),
        small_rows,
        small_m.reshape(2, 128),
        small_v.reshape(2, 128),
    )
    return (
        out.transpose(0, 2, 1),
        gser.transpose(0, 2, 1),
        norm.reshape(()),
        from_rows(new_w),
        from_rows(new_m),
        from_rows(new_v),
        new_sw.reshape(-1),
        new_sm.reshape(-1),
        new_sv.reshape(-1),
    )


def solution(mesh):
    placed = (
        P("batch", "wide", None),
        P("batch"),
        P(),
        P("batch", "wide", None),
        P(("wide", "batch")),
        P(("wide", "batch")),
        P(("wide", "batch")),
        P(),
        P(),
        P(),
    )
    return jax.shard_map(
        local,
        mesh=mesh,
        in_specs=placed,
        out_specs=(
            P("batch", "wide", None),
            P("batch", "wide", None),
            P(),
            P(("wide", "batch")),
            P(("wide", "batch")),
            P(("wide", "batch")),
            P(),
            P(),
            P(),
        ),
        check_vma=False,
    )
```
